32 devices in a mesh: pb: 4 (over z), ka: 8 (over y, x, core).
Axes of the slice: x: 2, y: 2, z: 4, core: 2. Of those that a mesh axis runs over, the one named last changes fastest.
Arguments:
- queries: bfloat16 [4096, 2048], P('pb'), may hold values from -8 to 8
- keys: bfloat16 [4096, 2048], P(('ka', 'pb')), may hold values from -8 to 8
- values: bfloat16 [4096, 2048], P(('ka', 'pb')), may hold values from -6 to 6
- block_mask: int32 [32, 32], P('pb', 'ka'), may hold values from 0 to 1, as said below
Outputs:
- attended: bfloat16 [4096, 2048], P('pb')
The draws below stay inside these ranges and needn't reach their ends.
Inputs may be any that keep to these rules, and one draw needn't show every extreme that they name: `block_mask`: 1 where the two blocks are equal or adjacent, in the first 2 block rows and block columns, and for 3 block columns drawn for each block row; 0 elsewhere.
All inputs are finite; a program needn't handle non-finite values.
Results may differ from the reference program's by a relative error of at most 0.0047.
Values may be sent and summed in bfloat16 or wider, within the bound.
No kernel may reach another device: no remote copies, remote signals or barrier semaphores. Data moves between devices by JAX's collectives and lax.ppermute only.
A program may use at most 128 MiB of HBM per device.

```python
import jax
import jax.numpy as jnp
from jax import lax

HEADS = 16
HEAD_DIM = 128
BLOCK = 128
GLOBAL = 2
RANDOM = 3
D = 2048
TOKENS = 4096
NB = 32


def paired_rows(key):
    base_q = jax.random.normal(jax.random.fold_in(key, 1), (TOKENS, D), jnp.float32)
    base_k = jax.random.normal(jax.random.fold_in(key, 2), (TOKENS, D), jnp.float32)
    return (jnp.clip(base_q, -8.0, 8.0), jnp.clip(base_k, -8.0, 8.0))


def draw_queries(key, part):
    return paired_rows(key)[0].astype(jnp.bfloat16)


def draw_keys(key, part):
    return paired_rows(key)[1].astype(jnp.bfloat16)


def draw_block_mask(key, part):
    row_ids = jnp.arange(NB, dtype=jnp.int32)[:, None]
    col_ids = jnp.arange(NB, dtype=jnp.int32)[None, :]
    near = jnp.abs(row_ids - col_ids) <= 1
    global_part = (row_ids < GLOBAL) | (col_ids < GLOBAL)
    picks = jax.random.randint(jax.random.fold_in(key, 9), (NB, RANDOM), 0, NB)
    random_part = jnp.any(picks[:, :, None] == col_ids[:, None, :], axis=1)
    return (near | global_part | random_part).astype(jnp.int32)


def block_scale(key, extent, cuts, smallest, high):
    def one(dim, blocks):
        draws = jax.random.uniform(jax.random.fold_in(jax.random.fold_in(key, 6), dim), (blocks,), jnp.float32, smallest / len(cuts), high / len(cuts))
        return jnp.repeat(jnp.exp(draws), extent[dim] // blocks).reshape((-1,) + (1,) * (len(extent) - dim - 1))

    loudness = one(*cuts[0])
    for cut in cuts[1:]:
        loudness = loudness * one(*cut)
    return loudness


def bell_draw(rng, extent, width, bound, cuts=(), kind=jnp.bfloat16):
    loudness = block_scale(rng, extent, cuts, -0.22, 0.18) if cuts else 1.0
    entries = jax.random.normal(rng, extent, jnp.float32) * width * loudness
    return jnp.minimum(jnp.maximum(entries, -bound), bound).astype(kind)


def setup_inputs(seed: int = 0) -> dict:
    key_of = jax.random.split(jax.random.key(seed), 5)
    queries = draw_queries(jax.random.fold_in(key_of[4], 71), 0)
    keys = draw_keys(jax.random.fold_in(key_of[4], 71), 0)
    values = bell_draw(key_of[2], (TOKENS, D), 1.0, 6.0, ((0, 32),))
    block_mask = draw_block_mask(jax.random.fold_in(key_of[4], 71), 0)
    return {"queries": queries, "keys": keys, "values": values, "block_mask": block_mask}


NEG = -1e30


def reference(queries, keys, values, block_mask):
    scale = HEAD_DIM ** -0.5
    nblocks = TOKENS // BLOCK

    def one_head(head_index):
        start = (head_index * HEAD_DIM).astype(jnp.int32)
        q_head = lax.dynamic_slice_in_dim(queries, start, HEAD_DIM, 1)
        k_head = lax.dynamic_slice_in_dim(keys, start, HEAD_DIM, 1)
        v_head = lax.dynamic_slice_in_dim(values, start, HEAD_DIM, 1)
        q_blocks = q_head.reshape(nblocks, BLOCK, HEAD_DIM)

        def one_block(pair):
            q_rows, mask_row = pair
            allowed = jnp.repeat(mask_row, BLOCK) > 0
            scores = jnp.dot(q_rows, k_head.T, preferred_element_type=jnp.float32) * scale
            row_top = jnp.max(jnp.where(allowed[None, :], scores, NEG), axis=1, keepdims=True)
            weights = jnp.where(allowed[None, :], jnp.exp(scores - row_top), 0.0)
            totals = jnp.sum(weights, axis=1, keepdims=True)
            numer = jnp.dot(weights.astype(jnp.bfloat16), v_head, preferred_element_type=jnp.float32)
            return (numer / totals).astype(jnp.bfloat16)

        return lax.map(one_block, (q_blocks, block_mask))

    stacked = lax.map(one_head, jnp.arange(HEADS).astype(jnp.int32))
    return stacked.transpose(1, 2, 0, 3).reshape(TOKENS, HEADS * HEAD_DIM)
```

```python
import functools
import math

import jax
import jax.numpy as jnp
from jax import lax
from jax.experimental import pallas as pl
from jax.experimental.pallas import tpu as pltpu
from jax.sharding import PartitionSpec as P

HEADS = 16
HEAD_DIM = 128
BLOCK = 128
NEG = -1e30
EXP2_SCALE = math.log2(math.e) / math.sqrt(HEAD_DIM)
VMEM_BYTES = 40 * 1024 * 1024

VMEM = pl.BlockSpec(memory_space=pltpu.VMEM)
SMEM = pl.BlockSpec(memory_space=pltpu.SMEM)
ANY = pl.BlockSpec(memory_space=pl.ANY)


def params():
    return pltpu.CompilerParams(vmem_limit_bytes=VMEM_BYTES)


def pack_kernel(n_ka, heads, me_ref, k_ref, v_ref, *out_refs):
    key_blocks = k_ref.shape[0] // BLOCK
    for c in range(heads):
        for k in range(n_ka):
            col = pl.multiple_of(((me_ref[0] ^ k) * heads + c) * HEAD_DIM, HEAD_DIM)
            for t in range(key_blocks):
                rows = slice(t * BLOCK, (t + 1) * BLOCK)
                out_refs[c][k, 0, t] = k_ref[rows, pl.ds(col, HEAD_DIM)]
                out_refs[c][k, 1, t] = v_ref[rows, pl.ds(col, HEAD_DIM)].T


def pack(me, keys, values, n_ka, heads):
    key_blocks = keys.shape[0] // BLOCK
    shape = jax.ShapeDtypeStruct((n_ka, 2, key_blocks, BLOCK, HEAD_DIM), keys.dtype)
    return pl.pallas_call(
        functools.partial(pack_kernel, n_ka, heads),
        out_shape=[shape] * heads,
        in_specs=[SMEM, VMEM, VMEM],
        out_specs=[VMEM] * heads,
        compiler_params=params(),
        name="pack",
    )(me, keys, values)


def attend_kernel(deltas, first, last, n_pb, info_ref, mask_ref, q_ref, *refs):
    n_src = len(deltas)
    kv_refs, refs = refs[:n_src], refs[n_src:]
    if not first:
        (m_in, l_in, acc_in), refs = refs[:3], refs[3:]
    if last:
        (out_ref,), refs = refs[:1], refs[1:]
    else:
        (m_out, l_out, acc_out), refs = refs[:3], refs[3:]
    kv, live, sems = refs
    copies = [pltpu.make_async_copy(kv_refs[s], kv.at[s], sems.at[s]) for s in range(n_src)]
    for copy in copies:
        copy.start()
    rows = q_ref.shape[0] // BLOCK
    n_slots, key_blocks = kv.shape[1], kv.shape[3]
    pb = info_ref[0]
    for copy in copies:
        copy.wait()

    def row_step(r, _):
        count = jnp.int32(0)
        for s, delta in enumerate(deltas):
            j = pb + delta
            inside = ((j >= 0) & (j < n_pb)).astype(jnp.int32)
            j = jnp.clip(j, 0, n_pb - 1)
            for slot in range(n_slots):
                for t in range(key_blocks):
                    live[count] = (s * n_slots + slot) * key_blocks + t
                    column = j * key_blocks + t
                    count += inside * mask_ref[(slot * rows + r) * (n_pb * key_blocks) + column]
        live[count] = 0
        q = q_ref[pl.ds(pl.multiple_of(r * BLOCK, BLOCK), BLOCK), :]

        def block(i):
            index = live[i]
            t, index = index % key_blocks, index // key_blocks
            s, slot = index // n_slots, index % n_slots
            return s, slot, t

        def pair_step(i, carry):
            m, l, acc = carry
            s0, slot0, t0 = block(2 * i)
            s1, slot1, t1 = block(2 * i + 1)
            nt = (((1,), (1,)), ((), ()))
            nn = (((1,), (0,)), ((), ()))
            f32 = jnp.float32
            x0 = lax.dot_general(kv[s0, slot0, 0, t0], q, nt, preferred_element_type=f32)
            x1 = lax.dot_general(kv[s1, slot1, 0, t1], q, nt, preferred_element_type=f32)
            x1 = jnp.where(2 * i + 1 < count, x1, NEG)
            top = jnp.max(jnp.maximum(x0, x1), axis=0, keepdims=True)
            m_new = jnp.maximum(m, top)
            alpha = jnp.exp2((m - m_new) * EXP2_SCALE)
            w0 = jnp.exp2((x0 - m_new) * EXP2_SCALE)
            w1 = jnp.exp2((x1 - m_new) * EXP2_SCALE)
            l = l * alpha + jnp.sum(w0 + w1, axis=0, keepdims=True)
            bf16 = jnp.bfloat16
            acc = acc * alpha
            acc += lax.dot_general(kv[s0, slot0, 1, t0], w0.astype(bf16), nn, preferred_element_type=f32)
            acc += lax.dot_general(kv[s1, slot1, 1, t1], w1.astype(bf16), nn, preferred_element_type=f32)
            return m_new, l, acc

        if first:
            carry = (
                jnp.full((1, BLOCK), NEG, jnp.float32),
                jnp.zeros((1, BLOCK), jnp.float32),
                jnp.zeros((HEAD_DIM, BLOCK), jnp.float32),
            )
        else:
            carry = (m_in[r], l_in[r], acc_in[r])
        m, l, acc = lax.fori_loop(0, (count + 1) // 2, pair_step, carry)
        if last:
            done = (acc / l).T.astype(out_ref.dtype)
            out_ref[pl.ds(pl.multiple_of(r * BLOCK, BLOCK), BLOCK), :] = done
        else:
            m_out[r], l_out[r], acc_out[r] = m, l, acc
        return 0

    lax.fori_loop(0, rows, row_step, 0)


def attend(info, mask, q, sources, deltas, state, last, n_pb, name):
    rows = q.shape[0] // BLOCK
    first = state is None
    state = () if first else state
    stat = jax.ShapeDtypeStruct((rows, 1, BLOCK), jnp.float32)
    if last:
        out_shape = [jax.ShapeDtypeStruct(q.shape, q.dtype)]
    else:
        out_shape = [stat, stat, jax.ShapeDtypeStruct((rows, HEAD_DIM, BLOCK), jnp.float32)]
    shape = sources[0].shape
    blocks = len(deltas) * shape[0] * shape[2]
    return pl.pallas_call(
        functools.partial(attend_kernel, deltas, first, last, n_pb),
        out_shape=out_shape,
        in_specs=[SMEM, SMEM, VMEM] + [ANY] * len(sources) + [VMEM] * len(state),
        out_specs=[VMEM] * len(out_shape),
        scratch_shapes=[
            pltpu.VMEM((len(sources),) + shape, q.dtype),
            pltpu.SMEM((blocks + 1,), jnp.int32),
            pltpu.SemaphoreType.DMA((len(sources),)),
        ],
        compiler_params=params(),
        cost_estimate=pl.CostEstimate(
            flops=rows * blocks * 4 * BLOCK * BLOCK * HEAD_DIM,
            bytes_accessed=4 * q.size,
            transcendentals=rows * blocks * BLOCK * BLOCK,
        ),
        name=name,
    )(info, mask, q, *sources, *state)


def place_kernel(n_ka, heads, c, me_ref, *refs):
    pieces, out_ref, sems = refs[:n_ka], refs[-2], refs[-1]
    copies = []
    for k in range(n_ka):
        col = pl.multiple_of(((me_ref[0] ^ k) * heads + c) * HEAD_DIM, HEAD_DIM)
        copies.append(pltpu.make_async_copy(pieces[k], out_ref.at[:, pl.ds(col, HEAD_DIM)], sems.at[k]))
    for copy in copies:
        copy.start()
    for copy in copies:
        copy.wait()


def place(me, pieces, whole, c, heads):
    n_ka = len(pieces)
    rows = pieces[0].shape[0]
    extra = () if whole is None else (whole,)
    return pl.pallas_call(
        functools.partial(place_kernel, n_ka, heads, c),
        out_shape=jax.ShapeDtypeStruct((rows, HEADS * HEAD_DIM), pieces[0].dtype),
        in_specs=[SMEM] + [ANY] * (n_ka + len(extra)),
        out_specs=ANY,
        scratch_shapes=[pltpu.SemaphoreType.DMA((n_ka,))],
        input_output_aliases={1 + n_ka: 0} if extra else {},
        compiler_params=params(),
        name="place",
    )(me, *pieces, *extra)


def local(n_pb, n_ka, queries, keys, values, block_mask):
    heads = HEADS // n_ka
    me = lax.axis_index("ka").astype(jnp.int32)
    pb = lax.axis_index("pb").astype(jnp.int32)
    me1, pb1 = me[None], pb[None]

    def swap(x, k):
        return lax.ppermute(x, "ka", [(i, i ^ k) for i in range(n_ka)])

    def move(x, step):
        hops = [(i, i + step) for i in range(n_pb) if 0 <= i + step < n_pb]
        return lax.ppermute(x, "pb", hops)

    mask = block_mask[None]
    bit = 1
    while bit < n_ka:
        mask = jnp.concatenate([mask, swap(mask, bit)])
        bit *= 2
    mask = mask.reshape((n_ka // 2, 2) + block_mask.shape).swapaxes(0, 1).reshape(-1)

    packed = pack(me1, keys, values, n_ka, heads)

    outs = None
    whole = None
    owns = []
    for c in range(heads):
        msgs = packed[c]
        mixed = [msgs[:2]] + [swap(msgs[k : k + 2], k) for k in range(2, n_ka, 2)]
        theirs = swap(jnp.stack([x[1] for x in mixed]), 1)
        owns.append(jnp.concatenate([jnp.stack([x[0] for x in mixed]), theirs]))

    for c in range(heads):
        q = lax.dynamic_slice_in_dim(queries, (me * heads + c) * HEAD_DIM, HEAD_DIM, 1)
        own = owns[c]
        from_left, from_right = own, own
        state = None
        sources, deltas = [own], [0]
        for step in range(1, n_pb):
            from_left, from_right = move(from_left, 1), move(from_right, -1)
            sources, deltas = sources + [from_left, from_right], deltas + [-step, step]
            state = attend(
                pb1, mask, q, sources, tuple(deltas), state, step == n_pb - 1, n_pb, f"attend_{c}_{step}"
            )
            sources, deltas = [], []
        (out,) = state
        pieces = [out] + [swap(out, k) for k in range(2, n_ka, 2)]
        others = [swap(x, 1) for x in pieces]
        pieces = [x for two in zip(pieces, others) for x in two]
        whole = place(me1, pieces, whole, c, heads)
    return whole


def solution(mesh):
    n_pb, n_ka = mesh.shape["pb"], mesh.shape["ka"]
    return jax.shard_map(
        functools.partial(local, n_pb, n_ka),
        mesh=mesh,
        in_specs=(P("pb", None), P(("ka", "pb"), None), P(("ka", "pb"), None), P("pb", "ka")),
        out_specs=P("pb", None),
        check_vma=False,
    )
```

```python
import functools
import math

import jax
import jax.numpy as jnp
from jax import lax
from jax.experimental import pallas as pl
from jax.experimental.pallas import tpu as pltpu
from jax.sharding import PartitionSpec as P

HEADS = 16
HEAD_DIM = 128
BLOCK = 128
NEG = -1e30
EXP2_SCALE = math.log2(math.e) / math.sqrt(HEAD_DIM)
GROUP = 4
ROW_SHIFT = 16
VMEM_BYTES = 40 * 1024 * 1024

VMEM = pl.BlockSpec(memory_space=pltpu.VMEM)
SMEM = pl.BlockSpec(memory_space=pltpu.SMEM)
ANY = pl.BlockSpec(memory_space=pl.ANY)


def params():
    return pltpu.CompilerParams(vmem_limit_bytes=VMEM_BYTES)


def pack_kernel(n_ka, heads, me_ref, k_ref, v_ref, mask_ref, *out_refs):
    key_blocks = k_ref.shape[0] // BLOCK
    for c in range(heads):
        for k in range(n_ka):
            col = pl.multiple_of(((me_ref[0] ^ k) * heads + c) * HEAD_DIM, HEAD_DIM)
            for t in range(key_blocks):
                rows, at = slice(t * BLOCK, (t + 1) * BLOCK), 2 * t * BLOCK
                out_refs[c][k, at : at + BLOCK] = k_ref[rows, pl.ds(col, HEAD_DIM)]
                out_refs[c][k, at + BLOCK : at + 2 * BLOCK] = v_ref[rows, pl.ds(col, HEAD_DIM)].T
            if c == 0:
                out_refs[c][k, 2 * key_blocks * BLOCK :] = mask_ref[...]


def pack(me, keys, values, mask, n_ka, heads):
    sizes = [2 * keys.shape[0] + (mask.shape[0] if c == 0 else 0) for c in range(heads)]
    return pl.pallas_call(
        functools.partial(pack_kernel, n_ka, heads),
        out_shape=[jax.ShapeDtypeStruct((n_ka, size, HEAD_DIM), keys.dtype) for size in sizes],
        in_specs=[SMEM, VMEM, VMEM, VMEM],
        out_specs=[VMEM] * heads,
        compiler_params=params(),
        name="pack",
    )(me, keys, values, mask)


def plan_kernel(steps, n_pb, n_slots, key_blocks, rows, pb_ref, mask_ref, count_ref, *live_refs):
    pb = pb_ref[0]
    sign = 1 - 2 * (pb & 1)
    for step, (deltas, live) in enumerate(zip(steps, live_refs)):

        def row_step(r, base):
            count = jnp.int32(0)
            for s, delta in enumerate(deltas):
                j = pb + delta * sign
                inside = ((j >= 0) & (j < n_pb)).astype(jnp.int32)
                j = jnp.clip(j, 0, n_pb - 1)
                for slot in range(n_slots):
                    for t in range(key_blocks):
                        live[2 * base + count] = (r << ROW_SHIFT) + (s * n_slots + slot) * key_blocks + t
                        column = j * key_blocks + t
                        count += inside * mask_ref[(slot * rows + r) * (n_pb * key_blocks) + column]
            live[2 * base + count] = -1
            return base + ((count + 1) >> 1)

        total = lax.fori_loop(0, rows, row_step, jnp.int32(0))
        for u in range(GROUP):
            live[2 * (total + u)] = 0
            live[2 * (total + u) + 1] = -1
        count_ref[step] = total


def plan(pb, mask, steps, n_pb, n_slots, key_blocks, rows):
    sizes = [rows * ((len(deltas) * n_slots * key_blocks + 2) // 2) + GROUP for deltas in steps]
    out_shape = [jax.ShapeDtypeStruct((len(steps),), jnp.int32)]
    out_shape += [jax.ShapeDtypeStruct((2 * size,), jnp.int32) for size in sizes]
    return pl.pallas_call(
        functools.partial(plan_kernel, steps, n_pb, n_slots, key_blocks, rows),
        out_shape=out_shape,
        in_specs=[SMEM, SMEM],
        out_specs=[SMEM] * len(out_shape),
        compiler_params=params(),
        name="plan",
    )(pb, mask)


def attend_kernel(n_src, step, first, last, count_ref, live_ref, q_ref, *refs):
    kv_refs, refs = refs[:n_src], refs[n_src:]
    state_in, refs = ((), refs) if first else (refs[:3], refs[3:])
    if last:
        (out_ref, kv, *state, sems) = refs
    else:
        (*state, kv, sems) = refs
    m_ref, l_ref, acc_ref = state
    blocks = kv.shape[0] // n_src
    copies = [
        pltpu.make_async_copy(kv_refs[s], kv.at[pl.ds(s * blocks, blocks)], sems.at[s]) for s in range(n_src)
    ]
    copies += [pltpu.make_async_copy(a, b, sems.at[n_src + i]) for i, (a, b) in enumerate(zip(state_in, state))]
    for copy in copies:
        copy.start()
    if first:
        m_ref[...] = jnp.full(m_ref.shape, NEG, jnp.float32)
        l_ref[...] = jnp.zeros(l_ref.shape, jnp.float32)
        acc_ref[...] = jnp.zeros(acc_ref.shape, jnp.float32)
    for copy in copies:
        copy.wait()
    total = count_ref[step]
    nt = (((1,), (1,)), ((), ()))
    nn = (((1,), (0,)), ((), ()))
    f32, bf16 = jnp.float32, jnp.bfloat16

    def group_step(g, _):
        found = []
        for u in range(GROUP):
            index = g * GROUP + u
            code0, code1 = live_ref[2 * index], live_ref[2 * index + 1]
            r = code0 >> ROW_SHIFT
            b0 = code0 & ((1 << ROW_SHIFT) - 1)
            b1 = jnp.maximum(code1, 0) & ((1 << ROW_SHIFT) - 1)
            q = q_ref[pl.ds(pl.multiple_of(r * BLOCK, BLOCK), BLOCK), :]
            x0 = lax.dot_general(kv[b0, 0], q, nt, preferred_element_type=f32)
            x1 = lax.dot_general(kv[b1, 0], q, nt, preferred_element_type=f32)
            x0 = jnp.where(index < total, x0, NEG)
            x1 = jnp.where(code1 >= 0, x1, NEG)
            top = jnp.max(jnp.maximum(x0, x1), axis=0, keepdims=True)
            w0 = jnp.exp2((x0 - top) * EXP2_SCALE)
            w1 = jnp.exp2((x1 - top) * EXP2_SCALE)
            total_w = jnp.sum(w0 + w1, axis=0, keepdims=True)
            part = lax.dot_general(kv[b0, 1], w0.astype(bf16), nn, preferred_element_type=f32)
            part += lax.dot_general(kv[b1, 1], w1.astype(bf16), nn, preferred_element_type=f32)
            found.append((r, top, total_w, part))
        for r, top, total_w, part in found:
            m = m_ref[r]
            m_new = jnp.maximum(m, top)
            alpha = jnp.exp2((m - m_new) * EXP2_SCALE)
            beta = jnp.exp2((top - m_new) * EXP2_SCALE)
            m_ref[r] = m_new
            l_ref[r] = l_ref[r] * alpha + total_w * beta
            acc_ref[r] = acc_ref[r] * alpha + part * beta
        return 0

    lax.fori_loop(0, (total + GROUP - 1) // GROUP, group_step, 0)
    if last:

        def finish(r, _):
            done = (acc_ref[r] / l_ref[r]).T.astype(out_ref.dtype)
            out_ref[pl.ds(pl.multiple_of(r * BLOCK, BLOCK), BLOCK), :] = done
            return 0

        lax.fori_loop(0, q_ref.shape[0] // BLOCK, finish, 0)


def attend(counts, live, q, sources, state, step, last, name):
    rows = q.shape[0] // BLOCK
    first = state is None
    state = () if first else tuple(state)
    stat = (rows, 1, BLOCK)
    shapes = [stat, stat, (rows, HEAD_DIM, BLOCK)]
    if last:
        out_shape = [jax.ShapeDtypeStruct(q.shape, q.dtype)]
    else:
        out_shape = [jax.ShapeDtypeStruct(shape, jnp.float32) for shape in shapes]
    n_src = len(sources)
    blocks = sources[0].shape[0]
    scratch = [pltpu.VMEM((n_src * blocks,) + sources[0].shape[1:], q.dtype)]
    if last:
        scratch += [pltpu.VMEM(shape, jnp.float32) for shape in shapes]
    scratch.append(pltpu.SemaphoreType.DMA((n_src + 3,)))
    live_blocks = rows * n_src * blocks // 4
    return pl.pallas_call(
        functools.partial(attend_kernel, n_src, step, first, last),
        out_shape=out_shape,
        in_specs=[SMEM, SMEM, VMEM] + [ANY] * (n_src + len(state)),
        out_specs=[VMEM] * len(out_shape),
        scratch_shapes=scratch,
        compiler_params=params(),
        cost_estimate=pl.CostEstimate(
            flops=live_blocks * 4 * BLOCK * BLOCK * HEAD_DIM,
            bytes_accessed=8 * q.size + 2 * n_src * sources[0].size,
            transcendentals=live_blocks * BLOCK * BLOCK,
        ),
        name=name,
    )(counts, live, q, *sources, *state)


def place_kernel(n_ka, heads, c, me_ref, *refs):
    pieces, out_ref, sems = refs[:n_ka], refs[-2], refs[-1]
    copies = []
    for k in range(n_ka):
        col = pl.multiple_of(((me_ref[0] ^ k) * heads + c) * HEAD_DIM, HEAD_DIM)
        copies.append(pltpu.make_async_copy(pieces[k], out_ref.at[:, pl.ds(col, HEAD_DIM)], sems.at[k]))
    for copy in copies:
        copy.start()
    for copy in copies:
        copy.wait()


def place(me, pieces, whole, c, heads):
    n_ka = len(pieces)
    rows = pieces[0].shape[0]
    extra = () if whole is None else (whole,)
    return pl.pallas_call(
        functools.partial(place_kernel, n_ka, heads, c),
        out_shape=jax.ShapeDtypeStruct((rows, HEADS * HEAD_DIM), pieces[0].dtype),
        in_specs=[SMEM] + [ANY] * (n_ka + len(extra)),
        out_specs=ANY,
        scratch_shapes=[pltpu.SemaphoreType.DMA((n_ka,))],
        input_output_aliases={1 + n_ka: 0} if extra else {},
        compiler_params=params(),
        name="place",
    )(me, *pieces, *extra)


def local(n_pb, n_ka, queries, keys, values, block_mask):
    heads = HEADS // n_ka
    key_blocks = keys.shape[0] // BLOCK
    rows = queries.shape[0] // BLOCK
    me = lax.axis_index("ka").astype(jnp.int32)
    pb = lax.axis_index("pb").astype(jnp.int32)
    me1, pb1 = me[None], pb[None]

    def swap(x, k):
        return lax.ppermute(x, "ka", [(i, i ^ k) for i in range(n_ka)])

    def exchange(x, odd, step):
        hops = []
        for low in range(odd, n_pb - 1, 2):
            hops += [(low, low + 1)] if low - (step - 1) >= 0 else []
            hops += [(low + 1, low)] if low + 1 + (step - 1) < n_pb else []
        return lax.ppermute(x, "pb", hops) if hops else None

    pad = (-rows) % 16
    mask = jnp.pad(block_mask.astype(keys.dtype), ((0, pad), (0, BLOCK - block_mask.shape[1])))
    packed = pack(me1, keys, values, mask, n_ka, heads)

    owns = []
    for c in range(heads):
        msgs = packed[c]
        mixed = [msgs[:2]] + [swap(msgs[k : k + 2], k) for k in range(2, n_ka, 2)]
        theirs = swap(jnp.stack([x[1] for x in mixed]), 1)
        all_kv = jnp.concatenate([jnp.stack([x[0] for x in mixed]), theirs])
        if c == 0:
            masks = all_kv[:, 2 * keys.shape[0] :, :][:, :rows, : block_mask.shape[1]]
            masks = masks.astype(jnp.int32).reshape(-1)
        owns.append(all_kv[:, : 2 * keys.shape[0]].reshape(n_ka * key_blocks, 2, BLOCK, HEAD_DIM))

    steps = []
    arrived = [[] for _ in range(heads)]
    state = [None] * heads
    last_even, last_odd = list(owns), list(owns)
    for step in range(1, n_pb):
        deltas = (0,) if step == 1 else ()
        for c in range(heads):
            even, odd = exchange(last_odd[c], 0, step), exchange(last_even[c], 1, step)
            last_even[c], last_odd[c] = even, odd
            arrived[c].append(([owns[c]] if step == 1 else []) + [x for x in (even, odd) if x is not None])
        deltas += (step,) if even is not None else ()
        deltas += (-step,) if odd is not None else ()
        steps.append(deltas)

    counts, *lives = plan(pb1, masks, steps, n_pb, n_ka, key_blocks, rows)

    whole = None
    for step in range(1, n_pb):
        for c in range(heads):
            q = lax.dynamic_slice_in_dim(queries, (me * heads + c) * HEAD_DIM, HEAD_DIM, 1)
            name = f"attend_{c}_{step}"
            last = step == n_pb - 1
            state[c] = attend(counts, lives[step - 1], q, arrived[c][step - 1], state[c], step - 1, last, name)
    for c in range(heads):
        (out,) = state[c]
        pieces = [out] + [swap(out, k) for k in range(2, n_ka, 2)]
        others = [swap(x, 1) for x in pieces]
        pieces = [x for two in zip(pieces, others) for x in two]
        whole = place(me1, pieces, whole, c, heads)
    return whole


def solution(mesh):
    n_pb, n_ka = mesh.shape["pb"], mesh.shape["ka"]
    return jax.shard_map(
        functools.partial(local, n_pb, n_ka),
        mesh=mesh,
        in_specs=(P("pb", None), P(("ka", "pb"), None), P(("ka", "pb"), None), P("pb", "ka")),
        out_specs=P("pb", None),
        check_vma=False,
    )
```

```python
import functools
import math

import jax
import jax.numpy as jnp
from jax import lax
from jax.experimental import pallas as pl
from jax.experimental.pallas import tpu as pltpu
from jax.sharding import PartitionSpec as P

HEADS = 16
HEAD_DIM = 128
BLOCK = 128
NEG = -1e30
EXP2_SCALE = math.log2(math.e) / math.sqrt(HEAD_DIM)
GROUP = 4
ROW_SHIFT = 16
VMEM_BYTES = 40 * 1024 * 1024

VMEM = pl.BlockSpec(memory_space=pltpu.VMEM)
SMEM = pl.BlockSpec(memory_space=pltpu.SMEM)
ANY = pl.BlockSpec(memory_space=pl.ANY)


def params():
    return pltpu.CompilerParams(vmem_limit_bytes=VMEM_BYTES)


def mask_rows(rows):
    return -(-rows // 16) * 16


def pack_kernel(n_ka, heads, me_ref, k_ref, v_ref, mask_ref, *out_refs):
    key_blocks = k_ref.shape[0] // BLOCK
    for c in range(heads):
        for k in range(n_ka):
            col = pl.multiple_of(((me_ref[0] ^ k) * heads + c) * HEAD_DIM, HEAD_DIM)
            for t in range(key_blocks):
                rows, at = slice(t * BLOCK, (t + 1) * BLOCK), 2 * t * BLOCK
                out_refs[c][k, at : at + BLOCK] = k_ref[rows, pl.ds(col, HEAD_DIM)]
                out_refs[c][k, at + BLOCK : at + 2 * BLOCK] = v_ref[rows, pl.ds(col, HEAD_DIM)].T
    rows = mask_rows(mask_ref.shape[0])
    row = lax.broadcasted_iota(jnp.int32, (rows, HEAD_DIM), 0)
    column = lax.broadcasted_iota(jnp.int32, (rows, HEAD_DIM), 1)
    mask = jnp.zeros((rows, HEAD_DIM), jnp.int32)
    for i in range(mask_ref.shape[0]):
        for j in range(mask_ref.shape[1]):
            mask = jnp.where((row == i) & (column == j), mask_ref[i, j], mask)
    mask = mask.astype(jnp.float32).astype(k_ref.dtype)
    for k in range(n_ka):
        out_refs[0][k, 2 * key_blocks * BLOCK :] = mask


def pack(me, keys, values, mask, n_ka, heads):
    sizes = [2 * keys.shape[0] + (mask_rows(mask.shape[0]) if c == 0 else 0) for c in range(heads)]
    return pl.pallas_call(
        functools.partial(pack_kernel, n_ka, heads),
        out_shape=[jax.ShapeDtypeStruct((n_ka, size, HEAD_DIM), keys.dtype) for size in sizes],
        in_specs=[SMEM, VMEM, VMEM, SMEM],
        out_specs=[VMEM] * heads,
        compiler_params=params(),
        name="pack",
    )(me, keys, values, mask)


def plan_kernel(steps, n_pb, n_slots, key_blocks, rows, pb_ref, mask_ref, count_ref, *live_refs):
    pb = pb_ref[0]
    sign = 1 - 2 * (pb & 1)
    for step, (deltas, live) in enumerate(zip(steps, live_refs)):

        def row_step(r, base):
            count = jnp.int32(0)
            for s, delta in enumerate(deltas):
                j = pb + delta * sign
                inside = ((j >= 0) & (j < n_pb)).astype(jnp.int32)
                j = jnp.clip(j, 0, n_pb - 1)
                for slot in range(n_slots):
                    for t in range(key_blocks):
                        live[2 * base + count] = (r << ROW_SHIFT) + (s * n_slots + slot) * key_blocks + t
                        column = j * key_blocks + t
                        count += inside * mask_ref[(slot * rows + r) * (n_pb * key_blocks) + column]
            live[2 * base + count] = -1
            return base + ((count + 1) >> 1)

        total = lax.fori_loop(0, rows, row_step, jnp.int32(0))
        for u in range(GROUP):
            live[2 * (total + u)] = 0
            live[2 * (total + u) + 1] = -1
        count_ref[step] = total


def plan(pb, mask, steps, n_pb, n_slots, key_blocks, rows):
    sizes = [rows * ((len(deltas) * n_slots * key_blocks + 2) // 2) + GROUP for deltas in steps]
    out_shape = [jax.ShapeDtypeStruct((len(steps),), jnp.int32)]
    out_shape += [jax.ShapeDtypeStruct((2 * size,), jnp.int32) for size in sizes]
    return pl.pallas_call(
        functools.partial(plan_kernel, steps, n_pb, n_slots, key_blocks, rows),
        out_shape=out_shape,
        in_specs=[SMEM, SMEM],
        out_specs=[SMEM] * len(out_shape),
        compiler_params=params(),
        name="plan",
    )(pb, mask)


def attend_kernel(n_src, step, first, last, count_ref, live_ref, head_ref, q_all, *refs):
    kv_refs, refs = refs[:n_src], refs[n_src:]
    state_in, refs = ((), refs) if first else (refs[:3], refs[3:])
    if last:
        (out_ref, kv, q_ref, *state, sems) = refs
    else:
        (*state, kv, q_ref, sems) = refs
    m_ref, l_ref, acc_ref = state
    blocks = kv.shape[0] // n_src
    copies = [
        pltpu.make_async_copy(kv_refs[s], kv.at[pl.ds(s * blocks, blocks)], sems.at[s]) for s in range(n_src)
    ]
    copies += [pltpu.make_async_copy(a, b, sems.at[n_src + i]) for i, (a, b) in enumerate(zip(state_in, state))]
    column = pl.multiple_of(head_ref[0] * HEAD_DIM, HEAD_DIM)
    copies.append(pltpu.make_async_copy(q_all.at[:, pl.ds(column, HEAD_DIM)], q_ref, sems.at[n_src + 3]))
    for copy in copies:
        copy.start()
    if first:
        m_ref[...] = jnp.full(m_ref.shape, NEG, jnp.float32)
        l_ref[...] = jnp.zeros(l_ref.shape, jnp.float32)
        acc_ref[...] = jnp.zeros(acc_ref.shape, jnp.float32)
    for copy in copies:
        copy.wait()
    total = count_ref[step]
    nt = (((1,), (1,)), ((), ()))
    nn = (((1,), (0,)), ((), ()))
    f32, bf16 = jnp.float32, jnp.bfloat16

    def group_step(g, _):
        found = []
        for u in range(GROUP):
            index = g * GROUP + u
            code0, code1 = live_ref[2 * index], live_ref[2 * index + 1]
            r = code0 >> ROW_SHIFT
            b0 = code0 & ((1 << ROW_SHIFT) - 1)
            b1 = jnp.maximum(code1, 0) & ((1 << ROW_SHIFT) - 1)
            q = q_ref[pl.ds(pl.multiple_of(r * BLOCK, BLOCK), BLOCK), :]
            x0 = lax.dot_general(kv[b0, 0], q, nt, preferred_element_type=f32)
            x1 = lax.dot_general(kv[b1, 0], q, nt, preferred_element_type=f32)
            x0 = jnp.where(index < total, x0, NEG)
            x1 = jnp.where(code1 >= 0, x1, NEG)
            top = jnp.max(jnp.maximum(x0, x1), axis=0, keepdims=True)
            w0 = jnp.exp2((x0 - top) * EXP2_SCALE)
            w1 = jnp.exp2((x1 - top) * EXP2_SCALE)
            total_w = jnp.sum(w0 + w1, axis=0, keepdims=True)
            part = lax.dot_general(kv[b0, 1], w0.astype(bf16), nn, preferred_element_type=f32)
            part += lax.dot_general(kv[b1, 1], w1.astype(bf16), nn, preferred_element_type=f32)
            found.append((r, top, total_w, part))
        for r, top, total_w, part in found:
            m = m_ref[r]
            m_new = jnp.maximum(m, top)
            alpha = jnp.exp2((m - m_new) * EXP2_SCALE)
            beta = jnp.exp2((top - m_new) * EXP2_SCALE)
            m_ref[r] = m_new
            l_ref[r] = l_ref[r] * alpha + total_w * beta
            acc_ref[r] = acc_ref[r] * alpha + part * beta
        return 0

    lax.fori_loop(0, (total + GROUP - 1) // GROUP, group_step, 0)
    if last:

        def finish(r, _):
            done = (acc_ref[r] / l_ref[r]).T.astype(out_ref.dtype)
            out_ref[pl.ds(pl.multiple_of(r * BLOCK, BLOCK), BLOCK), :] = done
            return 0

        lax.fori_loop(0, q_ref.shape[0] // BLOCK, finish, 0)


def attend(counts, live, head, queries, sources, state, step, last, name):
    q = jax.ShapeDtypeStruct((queries.shape[0], HEAD_DIM), queries.dtype)
    rows = q.shape[0] // BLOCK
    first = state is None
    state = () if first else tuple(state)
    stat = (rows, 1, BLOCK)
    shapes = [stat, stat, (rows, HEAD_DIM, BLOCK)]
    if last:
        out_shape = [jax.ShapeDtypeStruct(q.shape, q.dtype)]
    else:
        out_shape = [jax.ShapeDtypeStruct(shape, jnp.float32) for shape in shapes]
    n_src = len(sources)
    blocks = sources[0].shape[0]
    scratch = [pltpu.VMEM((n_src * blocks,) + sources[0].shape[1:], q.dtype), pltpu.VMEM(q.shape, q.dtype)]
    if last:
        scratch += [pltpu.VMEM(shape, jnp.float32) for shape in shapes]
    scratch.append(pltpu.SemaphoreType.DMA((n_src + 4,)))
    live_blocks = rows * n_src * blocks // 4
    return pl.pallas_call(
        functools.partial(attend_kernel, n_src, step, first, last),
        out_shape=out_shape,
        in_specs=[SMEM, SMEM, SMEM, ANY] + [ANY] * (n_src + len(state)),
        out_specs=[VMEM] * len(out_shape),
        scratch_shapes=scratch,
        compiler_params=params(),
        cost_estimate=pl.CostEstimate(
            flops=live_blocks * 4 * BLOCK * BLOCK * HEAD_DIM,
            bytes_accessed=8 * q.size + 2 * n_src * sources[0].size,
            transcendentals=live_blocks * BLOCK * BLOCK,
        ),
        name=name,
    )(counts, live, head, queries, *sources, *state)


def place_kernel(n_ka, heads, c, me_ref, *refs):
    pieces, out_ref, sems = refs[:n_ka], refs[-2], refs[-1]
    copies = []
    for k in range(n_ka):
        col = pl.multiple_of(((me_ref[0] ^ k) * heads + c) * HEAD_DIM, HEAD_DIM)
        copies.append(pltpu.make_async_copy(pieces[k], out_ref.at[:, pl.ds(col, HEAD_DIM)], sems.at[k]))
    for copy in copies:
        copy.start()
    for copy in copies:
        copy.wait()


def place(me, pieces, whole, c, heads):
    n_ka = len(pieces)
    rows = pieces[0].shape[0]
    extra = () if whole is None else (whole,)
    return pl.pallas_call(
        functools.partial(place_kernel, n_ka, heads, c),
        out_shape=jax.ShapeDtypeStruct((rows, HEADS * HEAD_DIM), pieces[0].dtype),
        in_specs=[SMEM] + [ANY] * (n_ka + len(extra)),
        out_specs=ANY,
        scratch_shapes=[pltpu.SemaphoreType.DMA((n_ka,))],
        input_output_aliases={1 + n_ka: 0} if extra else {},
        compiler_params=params(),
        name="place",
    )(me, *pieces, *extra)


def local(n_pb, n_ka, queries, keys, values, block_mask):
    heads = HEADS // n_ka
    key_blocks = keys.shape[0] // BLOCK
    rows = queries.shape[0] // BLOCK
    me = lax.axis_index("ka").astype(jnp.int32)
    pb = lax.axis_index("pb").astype(jnp.int32)
    me1, pb1 = me[None], pb[None]

    def swap(x, k):
        return lax.ppermute(x, "ka", [(i, i ^ k) for i in range(n_ka)])

    def hops(odd, step):
        found = []
        for low in range(odd, n_pb - 1, 2):
            found += [(low, low + 1)] if low - (step - 1) >= 0 else []
            found += [(low + 1, low)] if low + 1 + (step - 1) < n_pb else []
        return found

    def exchange(x, odd, step):
        found = hops(odd, step)
        return lax.ppermute(x, "pb", found) if found else None

    packed = pack(me1, keys, values, block_mask, n_ka, heads)

    owns = []
    for c in range(heads):
        msgs = packed[c]
        mixed = [msgs[:2]] + [swap(msgs[k : k + 2], k) for k in range(2, n_ka, 2)]
        theirs = swap(jnp.stack([x[1] for x in mixed]), 1)
        all_kv = jnp.concatenate([jnp.stack([x[0] for x in mixed]), theirs])
        if c == 0:
            masks = all_kv[:, 2 * keys.shape[0] :, :][:, :rows, : block_mask.shape[1]]
            masks = masks.astype(jnp.int32).reshape(-1)
        owns.append(all_kv[:, : 2 * keys.shape[0]].reshape(n_ka * key_blocks, 2, BLOCK, HEAD_DIM))

    steps = [(0,)]
    for step in range(1, n_pb):
        even, odd = hops(0, step), hops(1, step)
        steps.append(((step,) if even else ()) + ((-step,) if odd else ()))
    counts, *lives = plan(pb1, masks, steps, n_pb, n_ka, key_blocks, rows)

    def run(c, step, sources):
        last = step == n_pb - 1
        head = me1 * heads + c
        return attend(counts, lives[step], head, queries, sources, state[c], step, last, f"attend_{c}_{step}")

    def after(arrays, done):
        if done is None:
            return arrays
        return lax.optimization_barrier((arrays, done[0]))[0]

    state = [None] * heads
    over_even, over_odd = [None] * heads, [None] * heads
    done = None
    for step in range(1, n_pb):
        for c in range(heads):
            if step == 1:
                owns[c] = after(owns[c], done)
                even, odd = owns[c], owns[c]
            else:
                even, odd = after((over_odd[c], over_even[c]), done)
            over_even[c], over_odd[c] = exchange(even, 0, step), exchange(odd, 1, step)
            sources = [owns[c]] if step == 1 else [x for x in (odd, even) if x is not None]
            done = state[c] = run(c, step - 1, sources)
    for c in range(heads):
        state[c] = run(c, n_pb - 1, [x for x in (over_even[c], over_odd[c]) if x is not None])

    whole = None
    for c in range(heads):
        (out,) = state[c]
        pieces = [out] + [swap(out, k) for k in range(2, n_ka, 2)]
        others = [swap(x, 1) for x in pieces]
        pieces = [x for two in zip(pieces, others) for x in two]
        whole = place(me1, pieces, whole, c, heads)
    return whole


def solution(mesh):
    n_pb, n_ka = mesh.shape["pb"], mesh.shape["ka"]
    return jax.shard_map(
        functools.partial(local, n_pb, n_ka),
        mesh=mesh,
        in_specs=(P("pb", None), P(("ka", "pb"), None), P(("ka", "pb"), None), P("pb", "ka")),
        out_specs=P("pb", None),
        check_vma=False,
    )
```

```python
import functools
import math

import jax
import jax.numpy as jnp
from jax import lax
from jax.experimental import pallas as pl
from jax.experimental.pallas import tpu as pltpu
from jax.sharding import PartitionSpec as P

HEADS = 16
HEAD_DIM = 128
BLOCK = 128
NEG = -1e30
EXP2_SCALE = math.log2(math.e) / math.sqrt(HEAD_DIM)
GROUP = 8
ROW_SHIFT = 16
VMEM_BYTES = 40 * 1024 * 1024

VMEM = pl.BlockSpec(memory_space=pltpu.VMEM)
SMEM = pl.BlockSpec(memory_space=pltpu.SMEM)
ANY = pl.BlockSpec(memory_space=pl.ANY)


def params():
    return pltpu.CompilerParams(vmem_limit_bytes=VMEM_BYTES)


def mask_rows(rows):
    return -(-rows // 16) * 16


def pack_kernel(n_ka, heads, me_ref, k_ref, v_ref, mask_ref, *out_refs):
    key_blocks = k_ref.shape[0] // BLOCK
    for c in range(heads):
        for k in range(n_ka):
            col = pl.multiple_of(((me_ref[0] ^ k) * heads + c) * HEAD_DIM, HEAD_DIM)
            for t in range(key_blocks):
                rows, at = slice(t * BLOCK, (t + 1) * BLOCK), 2 * t * BLOCK
                out_refs[c][k, at : at + BLOCK] = k_ref[rows, pl.ds(col, HEAD_DIM)]
                out_refs[c][k, at + BLOCK : at + 2 * BLOCK] = v_ref[rows, pl.ds(col, HEAD_DIM)].T
    rows = mask_rows(mask_ref.shape[0])
    row = lax.broadcasted_iota(jnp.int32, (rows, HEAD_DIM), 0)
    column = lax.broadcasted_iota(jnp.int32, (rows, HEAD_DIM), 1)
    mask = jnp.zeros((rows, HEAD_DIM), jnp.int32)
    for i in range(mask_ref.shape[0]):
        for j in range(mask_ref.shape[1]):
            mask = jnp.where((row == i) & (column == j), mask_ref[i, j], mask)
    mask = mask.astype(jnp.float32).astype(k_ref.dtype)
    for k in range(n_ka):
        out_refs[0][k, 2 * key_blocks * BLOCK :] = mask


def pack(me, keys, values, mask, n_ka, heads):
    sizes = [2 * keys.shape[0] + (mask_rows(mask.shape[0]) if c == 0 else 0) for c in range(heads)]
    return pl.pallas_call(
        functools.partial(pack_kernel, n_ka, heads),
        out_shape=[jax.ShapeDtypeStruct((n_ka, size, HEAD_DIM), keys.dtype) for size in sizes],
        in_specs=[SMEM, VMEM, VMEM, SMEM],
        out_specs=[VMEM] * heads,
        compiler_params=params(),
        name="pack",
    )(me, keys, values, mask)


def plan_kernel(steps, n_pb, n_slots, key_blocks, rows, pb_ref, mask_ref, count_ref, *live_refs):
    pb = pb_ref[0]
    sign = 1 - 2 * (pb & 1)
    for step, (deltas, live) in enumerate(zip(steps, live_refs)):

        def row_step(r, base):
            count = jnp.int32(0)
            for s, delta in enumerate(deltas):
                j = pb + delta * sign
                inside = ((j >= 0) & (j < n_pb)).astype(jnp.int32)
                j = jnp.clip(j, 0, n_pb - 1)
                for slot in range(n_slots):
                    for t in range(key_blocks):
                        live[2 * base + count] = (r << ROW_SHIFT) + (s * n_slots + slot) * key_blocks + t
                        column = j * key_blocks + t
                        count += inside * mask_ref[(slot * rows + r) * (n_pb * key_blocks) + column]
            live[2 * base + count] = -1
            return base + ((count + 1) >> 1)

        total = lax.fori_loop(0, rows, row_step, jnp.int32(0))
        for u in range(GROUP):
            live[2 * (total + u)] = 0
            live[2 * (total + u) + 1] = -1
        count_ref[step] = total


def plan(pb, mask, steps, n_pb, n_slots, key_blocks, rows):
    sizes = [rows * ((len(deltas) * n_slots * key_blocks + 2) // 2) + GROUP for deltas in steps]
    out_shape = [jax.ShapeDtypeStruct((len(steps),), jnp.int32)]
    out_shape += [jax.ShapeDtypeStruct((2 * size,), jnp.int32) for size in sizes]
    return pl.pallas_call(
        functools.partial(plan_kernel, steps, n_pb, n_slots, key_blocks, rows),
        out_shape=out_shape,
        in_specs=[SMEM, SMEM],
        out_specs=[SMEM] * len(out_shape),
        compiler_params=params(),
        name="plan",
    )(pb, mask)


def attend_kernel(n_src, step, first, last, count_ref, live_ref, head_ref, q_all, *refs):
    kv_refs, refs = refs[:n_src], refs[n_src:]
    state_in, refs = ((), refs) if first else (refs[:3], refs[3:])
    if last:
        (out_ref, kv, q_ref, qt_ref, *state, sems) = refs
    else:
        (*state, kv, q_ref, qt_ref, sems) = refs
    m_ref, l_ref, acc_ref = state
    blocks = kv.shape[0] // n_src
    copies = [
        pltpu.make_async_copy(kv_refs[s], kv.at[pl.ds(s * blocks, blocks)], sems.at[s]) for s in range(n_src)
    ]
    copies += [pltpu.make_async_copy(a, b, sems.at[n_src + i]) for i, (a, b) in enumerate(zip(state_in, state))]
    column = pl.multiple_of(head_ref[0] * HEAD_DIM, HEAD_DIM)
    copies.append(pltpu.make_async_copy(q_all.at[:, pl.ds(column, HEAD_DIM)], q_ref, sems.at[n_src + 3]))
    for copy in copies:
        copy.start()
    if first:
        m_ref[...] = jnp.full(m_ref.shape, NEG, jnp.float32)
        l_ref[...] = jnp.zeros(l_ref.shape, jnp.float32)
        acc_ref[...] = jnp.zeros(acc_ref.shape, jnp.float32)
    for copy in copies:
        copy.wait()
    total = count_ref[step]

    def turn(r, _):
        qt_ref[r] = q_ref[pl.ds(pl.multiple_of(r * BLOCK, BLOCK), BLOCK), :].T
        return 0

    lax.fori_loop(0, q_ref.shape[0] // BLOCK, turn, 0, unroll=True)
    nt = (((1,), (1,)), ((), ()))
    nn = (((1,), (0,)), ((), ()))
    f32, bf16 = jnp.float32, jnp.bfloat16

    def group_step(g, _):
        found = []
        for u in range(GROUP):
            index = g * GROUP + u
            code0, code1 = live_ref[2 * index], live_ref[2 * index + 1]
            r = code0 >> ROW_SHIFT
            b0 = code0 & ((1 << ROW_SHIFT) - 1)
            b1 = jnp.maximum(code1, 0) & ((1 << ROW_SHIFT) - 1)
            q = qt_ref[r]
            x = lax.dot_general(jnp.concatenate([kv[b0, 0], kv[b1, 0]]), q, nn, preferred_element_type=f32)
            x0, x1 = x[:BLOCK], x[BLOCK:]
            x0 = jnp.where(index < total, x0, NEG)
            x1 = jnp.where(code1 >= 0, x1, NEG)
            top = jnp.max(jnp.maximum(x0, x1), axis=0, keepdims=True)
            w0 = jnp.exp2((x0 - top) * EXP2_SCALE)
            w1 = jnp.exp2((x1 - top) * EXP2_SCALE)
            total_w = jnp.sum(w0 + w1, axis=0, keepdims=True)
            w = jnp.concatenate([w0.astype(bf16), w1.astype(bf16)])
            part = lax.dot_general(jnp.concatenate([kv[b0, 1], kv[b1, 1]], axis=1), w, nn, preferred_element_type=f32)
            found.append((r, top, total_w, part))
        for r, top, total_w, part in found:
            m = m_ref[r]
            m_new = jnp.maximum(m, top)
            alpha = jnp.exp2((m - m_new) * EXP2_SCALE)
            beta = jnp.exp2((top - m_new) * EXP2_SCALE)
            m_ref[r] = m_new
            l_ref[r] = l_ref[r] * alpha + total_w * beta
            acc_ref[r] = acc_ref[r] * alpha + part * beta
        return 0

    lax.fori_loop(0, (total + GROUP - 1) // GROUP, group_step, 0)
    if last:

        def finish(r, _):
            done = (acc_ref[r] / l_ref[r]).T.astype(out_ref.dtype)
            out_ref[pl.ds(pl.multiple_of(r * BLOCK, BLOCK), BLOCK), :] = done
            return 0

        lax.fori_loop(0, q_ref.shape[0] // BLOCK, finish, 0)


def attend(counts, live, head, queries, sources, state, step, last, name):
    q = jax.ShapeDtypeStruct((queries.shape[0], HEAD_DIM), queries.dtype)
    rows = q.shape[0] // BLOCK
    first = state is None
    state = () if first else tuple(state)
    stat = (rows, 1, BLOCK)
    shapes = [stat, stat, (rows, HEAD_DIM, BLOCK)]
    if last:
        out_shape = [jax.ShapeDtypeStruct(q.shape, q.dtype)]
    else:
        out_shape = [jax.ShapeDtypeStruct(shape, jnp.float32) for shape in shapes]
    n_src = len(sources)
    blocks = sources[0].shape[0]
    scratch = [pltpu.VMEM((n_src * blocks,) + sources[0].shape[1:], q.dtype), pltpu.VMEM(q.shape, q.dtype), pltpu.VMEM((rows, HEAD_DIM, BLOCK), q.dtype)]
    if last:
        scratch += [pltpu.VMEM(shape, jnp.float32) for shape in shapes]
    scratch.append(pltpu.SemaphoreType.DMA((n_src + 4,)))
    live_blocks = rows * n_src * blocks // 4
    return pl.pallas_call(
        functools.partial(attend_kernel, n_src, step, first, last),
        out_shape=out_shape,
        in_specs=[SMEM, SMEM, SMEM, ANY] + [ANY] * (n_src + len(state)),
        out_specs=[VMEM] * len(out_shape),
        scratch_shapes=scratch,
        compiler_params=params(),
        cost_estimate=pl.CostEstimate(
            flops=live_blocks * 4 * BLOCK * BLOCK * HEAD_DIM,
            bytes_accessed=8 * q.size + 2 * n_src * sources[0].size,
            transcendentals=live_blocks * BLOCK * BLOCK,
        ),
        name=name,
    )(counts, live, head, queries, *sources, *state)


def place_kernel(n_ka, heads, c, me_ref, *refs):
    pieces, out_ref, sems = refs[:n_ka], refs[-2], refs[-1]
    copies = []
    for k in range(n_ka):
        col = pl.multiple_of(((me_ref[0] ^ k) * heads + c) * HEAD_DIM, HEAD_DIM)
        copies.append(pltpu.make_async_copy(pieces[k], out_ref.at[:, pl.ds(col, HEAD_DIM)], sems.at[k]))
    for copy in copies:
        copy.start()
    for copy in copies:
        copy.wait()


def place(me, pieces, whole, c, heads):
    n_ka = len(pieces)
    rows = pieces[0].shape[0]
    extra = () if whole is None else (whole,)
    return pl.pallas_call(
        functools.partial(place_kernel, n_ka, heads, c),
        out_shape=jax.ShapeDtypeStruct((rows, HEADS * HEAD_DIM), pieces[0].dtype),
        in_specs=[SMEM] + [ANY] * (n_ka + len(extra)),
        out_specs=ANY,
        scratch_shapes=[pltpu.SemaphoreType.DMA((n_ka,))],
        input_output_aliases={1 + n_ka: 0} if extra else {},
        compiler_params=params(),
        name="place",
    )(me, *pieces, *extra)


def local(n_pb, n_ka, queries, keys, values, block_mask):
    heads = HEADS // n_ka
    key_blocks = keys.shape[0] // BLOCK
    rows = queries.shape[0] // BLOCK
    me = lax.axis_index("ka").astype(jnp.int32)
    pb = lax.axis_index("pb").astype(jnp.int32)
    me1, pb1 = me[None], pb[None]

    def swap(x, k):
        return lax.ppermute(x, "ka", [(i, i ^ k) for i in range(n_ka)])

    def hops(odd, step):
        found = []
        for low in range(odd, n_pb - 1, 2):
            found += [(low, low + 1)] if low - (step - 1) >= 0 else []
            found += [(low + 1, low)] if low + 1 + (step - 1) < n_pb else []
        return found

    def exchange(x, odd, step):
        found = hops(odd, step)
        return lax.ppermute(x, "pb", found) if found else None

    packed = pack(me1, keys, values, block_mask, n_ka, heads)

    owns = []
    for c in range(heads):
        msgs = packed[c]
        mixed = [msgs[:2]] + [swap(msgs[k : k + 2], k) for k in range(2, n_ka, 2)]
        theirs = swap(jnp.stack([x[1] for x in mixed]), 1)
        all_kv = jnp.concatenate([jnp.stack([x[0] for x in mixed]), theirs])
        if c == 0:
            masks = all_kv[:, 2 * keys.shape[0] :, :][:, :rows, : block_mask.shape[1]]
            masks = masks.astype(jnp.int32).reshape(-1)
        owns.append(all_kv[:, : 2 * keys.shape[0]].reshape(n_ka * key_blocks, 2, BLOCK, HEAD_DIM))

    steps = [(0,)]
    for step in range(1, n_pb):
        even, odd = hops(0, step), hops(1, step)
        steps.append(((step,) if even else ()) + ((-step,) if odd else ()))
    counts, *lives = plan(pb1, masks, steps, n_pb, n_ka, key_blocks, rows)

    def run(c, step, sources):
        last = step == n_pb - 1
        head = me1 * heads + c
        return attend(counts, lives[step], head, queries, sources, state[c], step, last, f"attend_{c}_{step}")

    def after(arrays, done):
        if done is None:
            return arrays
        return lax.optimization_barrier((arrays, done[0]))[0]

    state = [None] * heads
    over_even, over_odd = [None] * heads, [None] * heads
    done = None
    for step in range(1, n_pb):
        for c in range(heads):
            if step == 1:
                owns[c] = after(owns[c], done)
                even, odd = owns[c], owns[c]
            else:
                even, odd = after((over_odd[c], over_even[c]), done)
            over_even[c], over_odd[c] = exchange(even, 0, step), exchange(odd, 1, step)
            sources = [owns[c]] if step == 1 else [x for x in (odd, even) if x is not None]
            done = state[c] = run(c, step - 1, sources)
    for c in range(heads):
        state[c] = run(c, n_pb - 1, [x for x in (over_even[c], over_odd[c]) if x is not None])

    whole = None
    for c in range(heads):
        (out,) = state[c]
        pieces = [out] + [swap(out, k) for k in range(2, n_ka, 2)]
        others = [swap(x, 1) for x in pieces]
        pieces = [x for two in zip(pieces, others) for x in two]
        whole = place(me1, pieces, whole, c, heads)
    return whole


def solution(mesh):
    n_pb, n_ka = mesh.shape["pb"], mesh.shape["ka"]
    return jax.shard_map(
        functools.partial(local, n_pb, n_ka),
        mesh=mesh,
        in_specs=(P("pb", None), P(("ka", "pb"), None), P(("ka", "pb"), None), P("pb", "ka")),
        out_specs=P("pb", None),
        check_vma=False,
    )
```

```python
import functools
import math

import jax
import jax.numpy as jnp
from jax import lax
from jax.experimental import pallas as pl
from jax.experimental.pallas import tpu as pltpu
from jax.sharding import PartitionSpec as P

HEADS = 16
HEAD_DIM = 128
BLOCK = 128
NEG = -1e30
EXP2_SCALE = math.log2(math.e) / math.sqrt(HEAD_DIM)
GROUP = 8
ROW_SHIFT = 16
VMEM_BYTES = 40 * 1024 * 1024

VMEM = pl.BlockSpec(memory_space=pltpu.VMEM)
SMEM = pl.BlockSpec(memory_space=pltpu.SMEM)
ANY = pl.BlockSpec(memory_space=pl.ANY)


def params():
    return pltpu.CompilerParams(vmem_limit_bytes=VMEM_BYTES)


def mask_rows(rows):
    return -(-rows // 16) * 16


def pack_kernel(n_ka, heads, me_ref, k_ref, v_ref, mask_ref, *out_refs):
    key_blocks = k_ref.shape[0] // BLOCK
    for c in range(heads):
        for k in range(n_ka):
            col = pl.multiple_of(((me_ref[0] ^ k) * heads + c) * HEAD_DIM, HEAD_DIM)
            for t in range(key_blocks):
                rows, at = slice(t * BLOCK, (t + 1) * BLOCK), 2 * t * BLOCK
                out_refs[c][k, at : at + BLOCK] = k_ref[rows, pl.ds(col, HEAD_DIM)]
                out_refs[c][k, at + BLOCK : at + 2 * BLOCK] = v_ref[rows, pl.ds(col, HEAD_DIM)].T
    rows = mask_rows(mask_ref.shape[0])
    row = lax.broadcasted_iota(jnp.int32, (rows, HEAD_DIM), 0)
    column = lax.broadcasted_iota(jnp.int32, (rows, HEAD_DIM), 1)
    mask = jnp.zeros((rows, HEAD_DIM), jnp.int32)
    for i in range(mask_ref.shape[0]):
        for j in range(mask_ref.shape[1]):
            mask = jnp.where((row == i) & (column == j), mask_ref[i, j], mask)
    mask = mask.astype(jnp.float32).astype(k_ref.dtype)
    for k in range(n_ka):
        out_refs[0][k, 2 * key_blocks * BLOCK :] = mask


def pack(me, keys, values, mask, n_ka, heads):
    sizes = [2 * keys.shape[0] + (mask_rows(mask.shape[0]) if c == 0 else 0) for c in range(heads)]
    return pl.pallas_call(
        functools.partial(pack_kernel, n_ka, heads),
        out_shape=[jax.ShapeDtypeStruct((n_ka, size, HEAD_DIM), keys.dtype) for size in sizes],
        in_specs=[SMEM, VMEM, VMEM, SMEM],
        out_specs=[VMEM] * heads,
        compiler_params=params(),
        name="pack",
    )(me, keys, values, mask)


def plan_kernel(steps, n_pb, n_slots, key_blocks, rows, relay, pb_ref, *refs):
    mask_refs, count_ref, live_refs = refs[: -len(steps) - 1], refs[-len(steps) - 1], refs[-len(steps) :]
    pb = pb_ref[0]
    sign = 1 - 2 * (pb & 1)
    inner = ((pb > 0) & (pb < n_pb - 1)).astype(jnp.int32)
    for step, (sources, live) in enumerate(zip(steps, live_refs)):
        total = jnp.int32(0)
        for guest, mask_ref in enumerate(mask_refs):

            def row_step(r, base, guest=guest, mask_ref=mask_ref):
                count = jnp.int32(0)
                for s, (delta, open_to_guests) in enumerate(sources):
                    if guest and not open_to_guests:
                        continue
                    j = pb + delta * sign
                    inside = ((j >= 0) & (j < n_pb)).astype(jnp.int32)
                    if relay and abs(delta) > 1:
                        inside = inside * inner
                    j = jnp.clip(j, 0, n_pb - 1)
                    for slot in range(n_slots):
                        for t in range(key_blocks):
                            block = (s * n_slots + slot) * key_blocks + t
                            live[2 * base + count] = ((r + guest * rows) << ROW_SHIFT) + block
                            column = j * key_blocks + t
                            count += inside * mask_ref[(slot * rows + r) * (n_pb * key_blocks) + column]
                live[2 * base + count] = -1
                return base + ((count + 1) >> 1)

            total = lax.fori_loop(0, rows, row_step, total)
        for u in range(GROUP):
            live[2 * (total + u)] = 0
            live[2 * (total + u) + 1] = -1
        count_ref[step] = total


def plan(pb, masks, steps, n_pb, n_slots, key_blocks, rows, relay):
    sizes = [len(masks) * rows * ((len(step) * n_slots * key_blocks + 2) // 2) + GROUP for step in steps]
    out_shape = [jax.ShapeDtypeStruct((len(steps),), jnp.int32)]
    out_shape += [jax.ShapeDtypeStruct((2 * size,), jnp.int32) for size in sizes]
    counts, *lives = pl.pallas_call(
        functools.partial(plan_kernel, steps, n_pb, n_slots, key_blocks, rows, relay),
        out_shape=out_shape,
        in_specs=[SMEM] * (1 + len(masks)),
        out_specs=[SMEM] * len(out_shape),
        compiler_params=params(),
        name="plan",
    )(pb, *masks)
    return [(counts, i, live) for i, live in enumerate(lives)]


def attend_kernel(n_src, entry, first, mode, guests, count_ref, live_ref, head_ref, q_all, *refs):
    n_kv = n_src
    guest_ref, refs = (refs[0], refs[1:]) if guests else (None, refs)
    kv_refs, refs = refs[:n_kv], refs[n_kv:]
    state_in, refs = ((), refs) if first else (refs[:3], refs[3:])
    if mode == "last":
        (out_ref, kv, q_ref, qt_ref, *state, sems) = refs
    elif mode == "send":
        (*state, part_ref, stat_ref, kv, q_ref, qt_ref, sems) = refs
    else:
        (*state, kv, q_ref, qt_ref, sems) = refs
    m_ref, l_ref, acc_ref = state
    blocks = kv.shape[0] // n_src
    tokens = q_all.shape[0]
    rows = tokens // BLOCK
    copies = [
        pltpu.make_async_copy(kv_refs[s], kv.at[pl.ds(s * blocks, blocks)], sems.at[s]) for s in range(n_src)
    ]
    copies += [pltpu.make_async_copy(a, b, sems.at[n_src + i]) for i, (a, b) in enumerate(zip(state_in, state))]
    column = pl.multiple_of(head_ref[0] * HEAD_DIM, HEAD_DIM)
    q_own = q_all.at[:, pl.ds(column, HEAD_DIM)]
    copies.append(pltpu.make_async_copy(q_own, q_ref.at[pl.ds(0, tokens)], sems.at[n_src + 3]))
    if guests:
        copies.append(pltpu.make_async_copy(guest_ref, q_ref.at[pl.ds(tokens, tokens)], sems.at[n_src + 4]))
    for copy in copies:
        copy.start()
    if first:
        m_ref[...] = jnp.full(m_ref.shape, NEG, jnp.float32)
        l_ref[...] = jnp.zeros(l_ref.shape, jnp.float32)
        acc_ref[...] = jnp.zeros(acc_ref.shape, jnp.float32)
    for copy in copies:
        copy.wait()
    total = count_ref[entry]

    for r in range(rows * (2 if guests else 1)):
        qt_ref[r] = q_ref[r * BLOCK : (r + 1) * BLOCK, :].T
    nn = (((1,), (0,)), ((), ()))
    f32, bf16 = jnp.float32, jnp.bfloat16

    def group_step(g, _):
        found = []
        for u in range(GROUP):
            index = g * GROUP + u
            code0, code1 = live_ref[2 * index], live_ref[2 * index + 1]
            r = code0 >> ROW_SHIFT
            b0 = code0 & ((1 << ROW_SHIFT) - 1)
            b1 = jnp.maximum(code1, 0) & ((1 << ROW_SHIFT) - 1)
            x = lax.dot_general(jnp.concatenate([kv[b0, 0], kv[b1, 0]]), qt_ref[r], nn, preferred_element_type=f32)
            x0 = jnp.where(index < total, x[:BLOCK], NEG)
            x1 = jnp.where(code1 >= 0, x[BLOCK:], NEG)
            top = jnp.max(jnp.maximum(x0, x1), axis=0, keepdims=True)
            w0 = jnp.exp2((x0 - top) * EXP2_SCALE)
            w1 = jnp.exp2((x1 - top) * EXP2_SCALE)
            total_w = jnp.sum(w0 + w1, axis=0, keepdims=True)
            w = jnp.concatenate([w0.astype(bf16), w1.astype(bf16)])
            v = jnp.concatenate([kv[b0, 1], kv[b1, 1]], axis=1)
            found.append((r, top, total_w, lax.dot_general(v, w, nn, preferred_element_type=f32)))
        for r, top, total_w, part in found:
            m = m_ref[r]
            m_new = jnp.maximum(m, top)
            alpha = jnp.exp2((m - m_new) * EXP2_SCALE)
            beta = jnp.exp2((top - m_new) * EXP2_SCALE)
            m_ref[r] = m_new
            l_ref[r] = l_ref[r] * alpha + total_w * beta
            acc_ref[r] = acc_ref[r] * alpha + part * beta
        return 0

    lax.fori_loop(0, (total + GROUP - 1) // GROUP, group_step, 0)
    if mode == "last":
        for r in range(rows):
            out_ref[r * BLOCK : (r + 1) * BLOCK, :] = (acc_ref[r] / l_ref[r]).T.astype(out_ref.dtype)
    if mode == "send":
        for r in range(rows):
            l = l_ref[rows + r]
            part_ref[r] = (acc_ref[rows + r] / jnp.where(l > 0, l, 1.0)).astype(part_ref.dtype)
            stat_ref[0, r], stat_ref[1, r] = m_ref[rows + r], l


def attend(listed, head, queries, guest, sources, state, mode, sets, name):
    counts, entry, live = listed
    tokens, dtype = queries.shape[0], queries.dtype
    rows = tokens // BLOCK
    first = state is None
    state = () if first else tuple(state)
    stat = (sets * rows, 1, BLOCK)
    shapes = [stat, stat, (sets * rows, HEAD_DIM, BLOCK)]
    if mode == "last":
        out_shape = [jax.ShapeDtypeStruct((tokens, HEAD_DIM), dtype)]
    else:
        out_shape = [jax.ShapeDtypeStruct(shape, jnp.float32) for shape in shapes]
    if mode == "send":
        out_shape.append(jax.ShapeDtypeStruct((rows, HEAD_DIM, BLOCK), dtype))
        out_shape.append(jax.ShapeDtypeStruct((2, rows, 1, BLOCK), jnp.float32))
    n_src = len(sources)
    blocks = sources[0].shape[0]
    guests = () if guest is None else (guest,)
    met = (1 + len(guests)) * rows
    scratch = [pltpu.VMEM((n_src * blocks,) + sources[0].shape[1:], dtype)]
    scratch += [pltpu.VMEM((met * BLOCK, HEAD_DIM), dtype), pltpu.VMEM((met, HEAD_DIM, BLOCK), dtype)]
    if mode == "last":
        scratch += [pltpu.VMEM(shape, jnp.float32) for shape in shapes]
    scratch.append(pltpu.SemaphoreType.DMA((n_src + 5,)))
    live_blocks = rows * n_src * blocks // 4
    return pl.pallas_call(
        functools.partial(attend_kernel, n_src, entry, first, mode, bool(guests)),
        out_shape=out_shape,
        in_specs=[SMEM, SMEM, SMEM, ANY] + [ANY] * (len(guests) + n_src + len(state)),
        out_specs=[VMEM] * len(out_shape),
        scratch_shapes=scratch,
        compiler_params=params(),
        cost_estimate=pl.CostEstimate(
            flops=live_blocks * 4 * BLOCK * BLOCK * HEAD_DIM,
            bytes_accessed=8 * tokens * HEAD_DIM + 2 * n_src * sources[0].size,
            transcendentals=live_blocks * BLOCK * BLOCK,
        ),
        name=name,
    )(counts, live, head, queries, *guests, *sources, *state)


def merge_kernel(outer_ref, m_ref, l_ref, acc_ref, part_ref, stat_ref, out_ref):
    outer = outer_ref[0] > 0
    for r in range(part_ref.shape[0]):
        m, l = m_ref[r], l_ref[r]
        extra = jnp.where(outer, stat_ref[1, r], 0.0)
        top = jnp.where(outer, stat_ref[0, r], NEG)
        m_new = jnp.maximum(m, top)
        alpha = jnp.exp2((m - m_new) * EXP2_SCALE)
        beta = jnp.exp2((top - m_new) * EXP2_SCALE) * extra
        done = (acc_ref[r] * alpha + part_ref[r].astype(jnp.float32) * beta) / (l * alpha + beta)
        out_ref[r * BLOCK : (r + 1) * BLOCK, :] = done.T.astype(out_ref.dtype)


def merge(outer, state, part, stat, name):
    rows = part.shape[0]
    half = lambda x: pl.BlockSpec((rows,) + x.shape[1:], lambda i: (0, 0, 0))
    return pl.pallas_call(
        merge_kernel,
        out_shape=jax.ShapeDtypeStruct((rows * BLOCK, HEAD_DIM), part.dtype),
        grid=(1,),
        in_specs=[SMEM] + [half(x) for x in state] + [VMEM, VMEM],
        out_specs=VMEM,
        compiler_params=params(),
        name=name,
    )(outer, *state, part, stat)


def place_kernel(n_ka, heads, c, me_ref, *refs):
    pieces, out_ref, sems = refs[:n_ka], refs[-2], refs[-1]
    copies = []
    for k in range(n_ka):
        col = pl.multiple_of(((me_ref[0] ^ k) * heads + c) * HEAD_DIM, HEAD_DIM)
        copies.append(pltpu.make_async_copy(pieces[k], out_ref.at[:, pl.ds(col, HEAD_DIM)], sems.at[k]))
    for copy in copies:
        copy.start()
    for copy in copies:
        copy.wait()


def place(me, pieces, whole, c, heads):
    n_ka = len(pieces)
    rows = pieces[0].shape[0]
    extra = () if whole is None else (whole,)
    return pl.pallas_call(
        functools.partial(place_kernel, n_ka, heads, c),
        out_shape=jax.ShapeDtypeStruct((rows, HEADS * HEAD_DIM), pieces[0].dtype),
        in_specs=[SMEM] + [ANY] * (n_ka + len(extra)),
        out_specs=ANY,
        scratch_shapes=[pltpu.SemaphoreType.DMA((n_ka,))],
        input_output_aliases={1 + n_ka: 0} if extra else {},
        compiler_params=params(),
        name="place",
    )(me, *pieces, *extra)


def local(n_pb, n_ka, queries, keys, values, block_mask):
    heads = HEADS // n_ka
    shard = keys.shape[0]
    key_blocks = shard // BLOCK
    rows = queries.shape[0] // BLOCK
    me = lax.axis_index("ka").astype(jnp.int32)
    pb = lax.axis_index("pb").astype(jnp.int32)
    me1, pb1 = me[None], pb[None]
    relay = n_pb >= 4 and n_pb % 2 == 0
    early = heads - 1 if heads > 1 and n_pb > 1 else None

    def swap(x, k):
        return lax.ppermute(x, "ka", [(i, i ^ k) for i in range(n_ka)])

    def hops(odd, step):
        found = []
        for low in range(odd, n_pb - 1, 2):
            found += [(low, low + 1)] if low - (step - 1) >= 0 else []
            found += [(low + 1, low)] if low + 1 + (step - 1) < n_pb else []
        if relay and step > 1:
            found = [(i, j) for i, j in found if 0 < j < n_pb - 1]
        return found

    def exchange(x, odd, step):
        found = hops(odd, step)
        return lax.ppermute(x, "pb", found) if found else None

    def inward(x):
        return lax.ppermute(x, "pb", [(0, 1), (n_pb - 1, n_pb - 2)])

    def outward(x):
        return lax.ppermute(x, "pb", [(1, 0), (n_pb - 2, n_pb - 1)])

    def sort(parts):
        mixed = []
        for k in range(0, n_ka, 2):
            two = [x[k : k + 2] for x in parts]
            joined = jnp.concatenate(two) if len(two) > 1 else two[0]
            joined = swap(joined, k) if k else joined
            mixed.append(joined.reshape((len(parts), 2) + joined.shape[1:]))
        theirs = swap(jnp.stack([x[:, 1] for x in mixed], axis=1), 1)
        return [jnp.concatenate([jnp.stack([x[i, 0] for x in mixed]), theirs[i]]) for i in range(len(parts))]

    def blocks(x):
        return x[:, : 2 * shard].reshape(n_ka * key_blocks, 2, BLOCK, HEAD_DIM)

    def after(arrays, done):
        return arrays if done is None else lax.optimization_barrier((arrays, done))[0]

    def flags(x):
        return x[:, :rows, : block_mask.shape[1]].astype(jnp.int32).reshape(-1)

    packed = pack(me1, keys, values, block_mask, n_ka, heads)
    ahead = [exchange(packed[early], odd, 1) for odd in (0, 1)] if early is not None else []
    ahead_from = [i for i, x in enumerate(ahead) if x is not None]

    owns = []
    for c in range(heads):
        (own,) = sort([packed[c]])
        owns.append(blocks(own))
        if c == 0:
            marks = own[:, 2 * shard :]
    masks = [flags(marks)]

    steps = [((0, False),)]
    for step in range(1, n_pb):
        found = (((step, False),) if hops(0, step) else ()) + (((-step, True),) if hops(1, step) else ())
        if found:
            steps.append(found)
    last = len(steps) - 1
    sets = 2 if relay else 1
    lists = plan(pb1, masks, steps[:1], n_pb, n_ka, key_blocks, rows, relay)
    if relay:
        masks.append(flags(inward(marks)))
    lists += plan(pb1, masks, steps[1:], n_pb, n_ka, key_blocks, rows, relay) if last else []
    guest = [None] * heads
    state = [None] * heads
    over = [None] * heads
    mode = "send" if relay else "last"

    def run(c, step, sources):
        head = me1 * heads + c
        kind = mode if step == last else "keep"
        seen = guest[c] if step else None
        name = f"attend_{c}_{step}"
        return attend(lists[step], head, queries, seen, sources, state[c], kind, sets, name)

    done = None
    for step in range(1, last + 1):
        for c in range(heads):
            if step == 1 and c == early:
                sorted_ahead = sort([ahead[i] for i in ahead_from])
                arrived = [None, None]
                for i, x in zip(ahead_from, sorted_ahead):
                    arrived[i] = blocks(x)
            elif step == 1:
                arrived = [exchange(owns[c], odd, 1) for odd in (0, 1)]
            else:
                over[c] = after(over[c], done)
                arrived = [exchange(over[c][1], 0, step), exchange(over[c][0], 1, step)]
            sources = [owns[c]] if step == 1 else [x for x in over[c] if x is not None]
            if relay and step == (2 if c else 1):
                q = lax.dynamic_slice_in_dim(queries, (me * heads + c) * HEAD_DIM, HEAD_DIM, 1)
                guest[c] = inward(after(q, done if c else arrived[0]))
            state[c] = run(c, step - 1, sources)
            done = state[c][0]
            over[c] = arrived

    whole = None
    for c in range(heads):
        sources = [x for x in over[c] if x is not None] if last else [owns[c]]
        found = run(c, last, sources)
        if relay:
            outer = ((pb == 0) | (pb == n_pb - 1)).astype(jnp.int32)[None]
            out = merge(outer, found[:3], outward(found[3]), outward(found[4]), f"merge_{c}")
        else:
            out = found[0]
        pieces = [out] + [swap(out, k) for k in range(2, n_ka, 2)]
        others = [swap(x, 1) for x in pieces]
        pieces = [x for two in zip(pieces, others) for x in two]
        whole = place(me1, pieces, whole, c, heads)
    return whole


def solution(mesh):
    n_pb, n_ka = mesh.shape["pb"], mesh.shape["ka"]
    return jax.shard_map(
        functools.partial(local, n_pb, n_ka),
        mesh=mesh,
        in_specs=(P("pb", None), P(("ka", "pb"), None), P(("ka", "pb"), None), P("pb", "ka")),
        out_specs=P("pb", None),
        check_vma=False,
    )
```

```python
import functools
import math

import jax
import jax.numpy as jnp
from jax import lax
from jax.experimental import pallas as pl
from jax.experimental.pallas import tpu as pltpu
from jax.sharding import PartitionSpec as P

HEADS = 16
HEAD_DIM = 128
BLOCK = 128
NEG = -1e30
EXP2_SCALE = math.log2(math.e) / math.sqrt(HEAD_DIM)
GROUP = 8
STAT_ROWS = 16
ROW_SHIFT = 16
VMEM_BYTES = 40 * 1024 * 1024

VMEM = pl.BlockSpec(memory_space=pltpu.VMEM)
SMEM = pl.BlockSpec(memory_space=pltpu.SMEM)
ANY = pl.BlockSpec(memory_space=pl.ANY)


def params():
    return pltpu.CompilerParams(vmem_limit_bytes=VMEM_BYTES)


def mask_rows(rows):
    return -(-rows // 16) * 16


def pack_kernel(n_ka, heads, marked, me_ref, k_ref, v_ref, mask_ref, *out_refs):
    key_blocks = k_ref.shape[0] // BLOCK
    for c in range(heads):
        for k in range(n_ka):
            col = pl.multiple_of(((me_ref[0] ^ k) * heads + c) * HEAD_DIM, HEAD_DIM)
            for t in range(key_blocks):
                rows, at = slice(t * BLOCK, (t + 1) * BLOCK), 2 * t * BLOCK
                out_refs[c][k, at : at + BLOCK] = k_ref[rows, pl.ds(col, HEAD_DIM)]
                out_refs[c][k, at + BLOCK : at + 2 * BLOCK] = v_ref[rows, pl.ds(col, HEAD_DIM)].T
    rows = mask_rows(mask_ref.shape[0])
    row = lax.broadcasted_iota(jnp.int32, (rows, HEAD_DIM), 0)
    column = lax.broadcasted_iota(jnp.int32, (rows, HEAD_DIM), 1)
    mask = jnp.zeros((rows, HEAD_DIM), jnp.int32)
    for i in range(mask_ref.shape[0]):
        for j in range(mask_ref.shape[1]):
            mask = jnp.where((row == i) & (column == j), mask_ref[i, j], mask)
    mask = mask.astype(jnp.float32).astype(k_ref.dtype)
    for c in marked:
        for k in range(n_ka):
            out_refs[c][k, 2 * key_blocks * BLOCK :] = mask


def pack(me, keys, values, mask, n_ka, heads, marked):
    sizes = [2 * keys.shape[0] + (mask_rows(mask.shape[0]) if c in marked else 0) for c in range(heads)]
    return pl.pallas_call(
        functools.partial(pack_kernel, n_ka, heads, marked),
        out_shape=[jax.ShapeDtypeStruct((n_ka, size, HEAD_DIM), keys.dtype) for size in sizes],
        in_specs=[SMEM, VMEM, VMEM, SMEM],
        out_specs=[VMEM] * heads,
        compiler_params=params(),
        name="pack",
    )(me, keys, values, mask)


def plan_kernel(steps, n_pb, n_slots, key_blocks, rows, relay, pb_ref, *refs):
    mask_refs, count_ref, live_refs = refs[: -len(steps) - 1], refs[-len(steps) - 1], refs[-len(steps) :]
    pb = pb_ref[0]
    sign = 1 - 2 * (pb & 1)
    inner = ((pb > 0) & (pb < n_pb - 1)).astype(jnp.int32)
    helper = ((pb == 1) | (pb == n_pb - 2)).astype(jnp.int32)
    for step, (sources, live) in enumerate(zip(steps, live_refs)):
        total = jnp.int32(0)
        for guest, mask_ref in enumerate(mask_refs):

            def row_step(r, base, guest=guest, mask_ref=mask_ref):
                count = jnp.int32(0)
                for s, (delta, open_to_guests) in enumerate(sources):
                    if guest and not open_to_guests:
                        continue
                    j = pb + delta * sign
                    inside = ((j >= 0) & (j < n_pb)).astype(jnp.int32)
                    if relay and abs(delta) > 1:
                        inside = inside * inner
                    if guest:
                        inside = inside * helper
                    j = jnp.clip(j, 0, n_pb - 1)
                    for slot in range(n_slots):
                        for t in range(key_blocks):
                            block = (s * n_slots + slot) * key_blocks + t
                            live[2 * base + count] = ((r + guest * rows) << ROW_SHIFT) + block
                            column = j * key_blocks + t
                            count += inside * mask_ref[(slot * rows + r) * (n_pb * key_blocks) + column]
                live[2 * base + count] = -1
                return base + ((count + 1) >> 1)

            total = lax.fori_loop(0, rows, row_step, total)
        for u in range(GROUP):
            live[2 * (total + u)] = 0
            live[2 * (total + u) + 1] = -1
        count_ref[step] = total


def plan(pb, masks, steps, n_pb, n_slots, key_blocks, rows, relay):
    sizes = [len(masks) * rows * ((len(step) * n_slots * key_blocks + 2) // 2) + GROUP for step in steps]
    out_shape = [jax.ShapeDtypeStruct((len(steps),), jnp.int32)]
    out_shape += [jax.ShapeDtypeStruct((2 * size,), jnp.int32) for size in sizes]
    counts, *lives = pl.pallas_call(
        functools.partial(plan_kernel, steps, n_pb, n_slots, key_blocks, rows, relay),
        out_shape=out_shape,
        in_specs=[SMEM] * (1 + len(masks)),
        out_specs=[SMEM] * len(out_shape),
        compiler_params=params(),
        name="plan",
    )(pb, *masks)
    return [(counts, i, live) for i, live in enumerate(lives)]


def in_parts(x):
    found = []
    for _ in range(3):
        found.append(x.astype(jnp.bfloat16).astype(jnp.float32))
        x = x - found[-1]
    return found


def attend_kernel(n_src, entry, first, mode, guests, count_ref, live_ref, head_ref, q_all, *refs):
    n_kv = n_src
    guest_ref, refs = (refs[0], refs[1:]) if guests else (None, refs)
    kv_refs, refs = refs[:n_kv], refs[n_kv:]
    state_in, refs = ((), refs) if first else (refs[:3], refs[3:])
    if mode == "last":
        (out_ref, kv, q_ref, qt_ref, *state, sems) = refs
    elif mode == "send":
        (*state, part_ref, kv, q_ref, qt_ref, sems) = refs
    else:
        (*state, kv, q_ref, qt_ref, sems) = refs
    m_ref, l_ref, acc_ref = state
    blocks = kv.shape[0] // n_src
    tokens = q_all.shape[0]
    rows = tokens // BLOCK
    copies = [
        pltpu.make_async_copy(kv_refs[s], kv.at[pl.ds(s * blocks, blocks)], sems.at[s]) for s in range(n_src)
    ]
    copies += [pltpu.make_async_copy(a, b, sems.at[n_src + i]) for i, (a, b) in enumerate(zip(state_in, state))]
    column = pl.multiple_of(head_ref[0] * HEAD_DIM, HEAD_DIM)
    q_own = q_all.at[:, pl.ds(column, HEAD_DIM)]
    copies.append(pltpu.make_async_copy(q_own, q_ref.at[pl.ds(0, tokens)], sems.at[n_src + 3]))
    if guests:
        copies.append(pltpu.make_async_copy(guest_ref, q_ref.at[pl.ds(tokens, tokens)], sems.at[n_src + 4]))
    for copy in copies:
        copy.start()
    if first:
        m_ref[...] = jnp.full(m_ref.shape, NEG, jnp.float32)
        l_ref[...] = jnp.zeros(l_ref.shape, jnp.float32)
        acc_ref[...] = jnp.zeros(acc_ref.shape, jnp.float32)
    for copy in copies:
        copy.wait()
    total = count_ref[entry]

    for r in range(rows * (2 if guests else 1)):
        qt_ref[r] = q_ref[r * BLOCK : (r + 1) * BLOCK, :].T
    nn = (((1,), (0,)), ((), ()))
    f32, bf16 = jnp.float32, jnp.bfloat16

    def group_step(g, _):
        found = []
        for u in range(GROUP):
            index = g * GROUP + u
            code0, code1 = live_ref[2 * index], live_ref[2 * index + 1]
            r = code0 >> ROW_SHIFT
            b0 = code0 & ((1 << ROW_SHIFT) - 1)
            b1 = jnp.maximum(code1, 0) & ((1 << ROW_SHIFT) - 1)
            x = lax.dot_general(jnp.concatenate([kv[b0, 0], kv[b1, 0]]), qt_ref[r], nn, preferred_element_type=f32)
            x0 = jnp.where(index < total, x[:BLOCK], NEG)
            x1 = jnp.where(code1 >= 0, x[BLOCK:], NEG)
            top = jnp.max(jnp.maximum(x0, x1), axis=0, keepdims=True)
            w0 = jnp.exp2((x0 - top) * EXP2_SCALE)
            w1 = jnp.exp2((x1 - top) * EXP2_SCALE)
            total_w = jnp.sum(w0 + w1, axis=0, keepdims=True)
            w = jnp.concatenate([w0.astype(bf16), w1.astype(bf16)])
            v = jnp.concatenate([kv[b0, 1], kv[b1, 1]], axis=1)
            found.append((r, top, total_w, lax.dot_general(v, w, nn, preferred_element_type=f32)))
        for r, top, total_w, part in found:
            m = m_ref[r]
            m_new = jnp.maximum(m, top)
            alpha = jnp.exp2((m - m_new) * EXP2_SCALE)
            beta = jnp.exp2((top - m_new) * EXP2_SCALE)
            m_ref[r] = m_new
            l_ref[r] = l_ref[r] * alpha + total_w * beta
            acc_ref[r] = acc_ref[r] * alpha + part * beta
        return 0

    lax.fori_loop(0, (total + GROUP - 1) // GROUP, group_step, 0)
    if mode == "last":
        for r in range(rows):
            out_ref[r * BLOCK : (r + 1) * BLOCK, :] = (acc_ref[r] / l_ref[r]).T.astype(out_ref.dtype)
    if mode == "send":
        for r in range(rows):
            l = l_ref[rows + r]
            part_ref[r, :HEAD_DIM] = (acc_ref[rows + r] / jnp.where(l > 0, l, 1.0)).astype(part_ref.dtype)
            words = in_parts(m_ref[rows + r]) + in_parts(l)
            words.append(jnp.zeros((STAT_ROWS - len(words), BLOCK), f32))
            part_ref[r, HEAD_DIM:] = jnp.concatenate(words).astype(part_ref.dtype)


def attend(listed, head, queries, guest, sources, state, mode, sets, name):
    counts, entry, live = listed
    tokens, dtype = queries.shape[0], queries.dtype
    rows = tokens // BLOCK
    first = state is None
    state = () if first else tuple(state)
    stat = (sets * rows, 1, BLOCK)
    shapes = [stat, stat, (sets * rows, HEAD_DIM, BLOCK)]
    if mode == "last":
        out_shape = [jax.ShapeDtypeStruct((tokens, HEAD_DIM), dtype)]
    else:
        out_shape = [jax.ShapeDtypeStruct(shape, jnp.float32) for shape in shapes]
    if mode == "send":
        out_shape.append(jax.ShapeDtypeStruct((rows, HEAD_DIM + STAT_ROWS, BLOCK), dtype))
    n_src = len(sources)
    blocks = sources[0].shape[0]
    guests = () if guest is None else (guest,)
    met = (1 + len(guests)) * rows
    scratch = [pltpu.VMEM((n_src * blocks,) + sources[0].shape[1:], dtype)]
    scratch += [pltpu.VMEM((met * BLOCK, HEAD_DIM), dtype), pltpu.VMEM((met, HEAD_DIM, BLOCK), dtype)]
    if mode == "last":
        scratch += [pltpu.VMEM(shape, jnp.float32) for shape in shapes]
    scratch.append(pltpu.SemaphoreType.DMA((n_src + 5,)))
    return pl.pallas_call(
        functools.partial(attend_kernel, n_src, entry, first, mode, bool(guests)),
        out_shape=out_shape,
        in_specs=[SMEM, SMEM, SMEM, ANY] + [ANY] * (len(guests) + n_src + len(state)),
        out_specs=[VMEM] * len(out_shape),
        scratch_shapes=scratch,
        compiler_params=params(),
        cost_estimate=pl.CostEstimate(flops=0, bytes_accessed=tokens * HEAD_DIM, transcendentals=0),
        name=name,
    )(counts, live, head, queries, *guests, *sources, *state)


def merge_kernel(outer_ref, m_ref, l_ref, acc_ref, part_ref, out_ref):
    outer = outer_ref[0] > 0
    for r in range(part_ref.shape[0]):
        m, l = m_ref[r], l_ref[r]
        words = part_ref[r, HEAD_DIM:].astype(jnp.float32)
        top = jnp.where(outer, words[0:1] + words[1:2] + words[2:3], NEG)
        extra = jnp.where(outer, words[3:4] + words[4:5] + words[5:6], 0.0)
        m_new = jnp.maximum(m, top)
        alpha = jnp.exp2((m - m_new) * EXP2_SCALE)
        beta = jnp.exp2((top - m_new) * EXP2_SCALE) * extra
        done = (acc_ref[r] * alpha + part_ref[r, :HEAD_DIM].astype(jnp.float32) * beta) / (l * alpha + beta)
        out_ref[r * BLOCK : (r + 1) * BLOCK, :] = done.T.astype(out_ref.dtype)


def merge(outer, state, part, name):
    rows = part.shape[0]
    half = lambda x: pl.BlockSpec((rows,) + x.shape[1:], lambda i: (0, 0, 0))
    return pl.pallas_call(
        merge_kernel,
        out_shape=jax.ShapeDtypeStruct((rows * BLOCK, HEAD_DIM), part.dtype),
        grid=(1,),
        in_specs=[SMEM] + [half(x) for x in state] + [VMEM],
        out_specs=VMEM,
        compiler_params=params(),
        name=name,
    )(outer, *state, part)


def place_kernel(n_ka, heads, c, me_ref, *refs):
    pieces, out_ref, sems = refs[:n_ka], refs[-2], refs[-1]
    copies = []
    for k in range(n_ka):
        col = pl.multiple_of(((me_ref[0] ^ k) * heads + c) * HEAD_DIM, HEAD_DIM)
        copies.append(pltpu.make_async_copy(pieces[k], out_ref.at[:, pl.ds(col, HEAD_DIM)], sems.at[k]))
    for copy in copies:
        copy.start()
    for copy in copies:
        copy.wait()


def place(me, pieces, whole, c, heads):
    n_ka = len(pieces)
    rows = pieces[0].shape[0]
    extra = () if whole is None else (whole,)
    return pl.pallas_call(
        functools.partial(place_kernel, n_ka, heads, c),
        out_shape=jax.ShapeDtypeStruct((rows, HEADS * HEAD_DIM), pieces[0].dtype),
        in_specs=[SMEM] + [ANY] * (n_ka + len(extra)),
        out_specs=ANY,
        scratch_shapes=[pltpu.SemaphoreType.DMA((n_ka,))],
        input_output_aliases={1 + n_ka: 0} if extra else {},
        compiler_params=params(),
        name="place",
    )(me, *pieces, *extra)


def local(n_pb, n_ka, queries, keys, values, block_mask):
    heads = HEADS // n_ka
    shard = keys.shape[0]
    key_blocks = shard // BLOCK
    rows = queries.shape[0] // BLOCK
    me = lax.axis_index("ka").astype(jnp.int32)
    pb = lax.axis_index("pb").astype(jnp.int32)
    me1, pb1 = me[None], pb[None]
    relay = n_pb >= 4 and n_pb % 2 == 0
    early = heads - 1 if heads > 1 and n_pb > 1 else None

    def swap(x, k):
        return lax.ppermute(x, "ka", [(i, i ^ k) for i in range(n_ka)])

    def hops(odd, step):
        found = []
        for low in range(odd, n_pb - 1, 2):
            found += [(low, low + 1)] if low - (step - 1) >= 0 else []
            found += [(low + 1, low)] if low + 1 + (step - 1) < n_pb else []
        if relay and step > 1:
            found = [(i, j) for i, j in found if 0 < j < n_pb - 1]
        return found

    def exchange(x, odd, step):
        found = hops(odd, step)
        return lax.ppermute(x, "pb", found) if found else None

    def inward(x):
        return lax.ppermute(x, "pb", [(0, 1), (n_pb - 1, n_pb - 2)])

    def outward(x):
        return lax.ppermute(x, "pb", [(1, 0), (n_pb - 2, n_pb - 1)])

    def sort(parts):
        mixed = []
        for k in range(0, n_ka, 2):
            two = [x[k : k + 2] for x in parts]
            joined = jnp.concatenate(two) if len(two) > 1 else two[0]
            joined = swap(joined, k) if k else joined
            mixed.append(joined.reshape((len(parts), 2) + joined.shape[1:]))
        theirs = swap(jnp.stack([x[:, 1] for x in mixed], axis=1), 1)
        return [jnp.concatenate([jnp.stack([x[i, 0] for x in mixed]), theirs[i]]) for i in range(len(parts))]

    def blocks(x):
        return x[:, : 2 * shard].reshape(n_ka * key_blocks, 2, BLOCK, HEAD_DIM)

    def after(arrays, done):
        return arrays if done is None else lax.optimization_barrier((arrays, done))[0]

    def flags(x):
        return x[:, :rows, : block_mask.shape[1]].astype(jnp.int32).reshape(-1)

    packed = pack(me1, keys, values, block_mask, n_ka, heads, (0,) if early is None else (0, early))
    ahead = [exchange(packed[early], odd, 1) for odd in (0, 1)] if early is not None else []
    ahead_from = [i for i, x in enumerate(ahead) if x is not None]

    owns = [None if c == early else sort([packed[c]])[0] for c in range(heads)]
    marks = owns[0][:, 2 * shard :]
    owns = [own if own is None else blocks(own) for own in owns]
    masks = [flags(marks)]

    steps = [((0, False),)]
    for step in range(1, n_pb):
        found = (((step, False),) if hops(0, step) else ()) + (((-step, True),) if hops(1, step) else ())
        if found:
            steps.append(found)
    last = len(steps) - 1
    sets = 2 if relay else 1
    lists = plan(pb1, masks, steps[:1], n_pb, n_ka, key_blocks, rows, relay)
    arrived_early = [None, None]
    if early is not None:
        first_over = exchange(owns[0], 0, 1), exchange(owns[0], 1, 1)
        own_early, *sorted_ahead = sort([packed[early]] + [ahead[i] for i in ahead_from])
        owns[early] = blocks(own_early)
        for i, x in zip(ahead_from, sorted_ahead):
            arrived_early[i] = blocks(x)
    if relay:
        masks.append(flags(sorted_ahead[0][:, 2 * shard :] if early is not None else inward(marks)))
    lists += plan(pb1, masks, steps[1:], n_pb, n_ka, key_blocks, rows, relay) if last else []
    guest = [None] * heads
    state = [None] * heads
    over = [None] * heads
    mode = "send" if relay else "last"

    def run(c, step, sources):
        head = me1 * heads + c
        kind = mode if step == last else "keep"
        seen = guest[c] if step else None
        name = f"attend_{c}_{step}"
        return attend(lists[step], head, queries, seen, sources, state[c], kind, sets, name)

    done = None
    for step in range(1, last + 1):
        for c in range(heads):
            if step == 1 and c == early:
                arrived = arrived_early
            elif step == 1:
                arrived = [exchange(owns[c], odd, 1) for odd in (0, 1)] if c or early is None else list(first_over)
            else:
                over[c] = after(over[c], done)
                arrived = [exchange(over[c][1], 0, step), exchange(over[c][0], 1, step)]
            sources = [owns[c]] if step == 1 else [x for x in over[c] if x is not None]
            if relay and step == (2 if c else 1):
                q = lax.dynamic_slice_in_dim(queries, (me * heads + c) * HEAD_DIM, HEAD_DIM, 1)
                guest[c] = inward(after(q, done if c else arrived[0]))
            state[c] = run(c, step - 1, sources)
            done = state[c][0]
            over[c] = arrived

    whole = None
    for c in range(heads):
        sources = [x for x in over[c] if x is not None] if last else [owns[c]]
        found = run(c, last, sources if whole is None else after(sources, out))
        if relay:
            outer = ((pb == 0) | (pb == n_pb - 1)).astype(jnp.int32)[None]
            out = merge(outer, found[:3], outward(found[3]), f"merge_{c}")
        else:
            out = found[0]
        pieces = [out] + [swap(out, k) for k in range(2, n_ka, 2)]
        others = [swap(x, 1) for x in pieces]
        pieces = [x for two in zip(pieces, others) for x in two]
        whole = place(me1, pieces, whole, c, heads)
    return whole


def solution(mesh):
    n_pb, n_ka = mesh.shape["pb"], mesh.shape["ka"]
    return jax.shard_map(
        functools.partial(local, n_pb, n_ka),
        mesh=mesh,
        in_specs=(P("pb", None), P(("ka", "pb"), None), P(("ka", "pb"), None), P("pb", "ka")),
        out_specs=P("pb", None),
        check_vma=False,
    )
```

```python
import functools
import math

import jax
import jax.numpy as jnp
from jax import lax
from jax.experimental import pallas as pl
from jax.experimental.pallas import tpu as pltpu
from jax.sharding import PartitionSpec as P

HEADS = 16
HEAD_DIM = 128
BLOCK = 128
NEG = -1e30
EXP2_SCALE = math.log2(math.e) / math.sqrt(HEAD_DIM)
GROUP = 8
STAT_ROWS = 16
ROW_SHIFT = 16
VMEM_BYTES = 40 * 1024 * 1024
MOST_VMEM_BYTES = 60 * 1024 * 1024

VMEM = pl.BlockSpec(memory_space=pltpu.VMEM)
SMEM = pl.BlockSpec(memory_space=pltpu.SMEM)
ANY = pl.BlockSpec(memory_space=pl.ANY)


def params(size=VMEM_BYTES):
    return pltpu.CompilerParams(vmem_limit_bytes=size)


def mask_rows(rows):
    return -(-rows // 16) * 16


def pack_kernel(n_ka, heads, me_ref, mask_ref, k_all, v_all, *refs):
    out_refs, (k_ref, v_ref, sems) = refs[:heads], refs[heads:]
    key_blocks = k_ref.shape[0] // BLOCK
    parts = sems.shape[1]
    width = k_ref.shape[1] // parts
    copies = []
    for i in range(parts):
        at = slice(i * width, (i + 1) * width)
        copies.append(pltpu.make_async_copy(k_all.at[:, at], k_ref.at[:, at], sems.at[0, i]))
        copies.append(pltpu.make_async_copy(v_all.at[:, at], v_ref.at[:, at], sems.at[1, i]))
    for copy in copies:
        copy.start()
    rows, used = mask_rows(mask_ref.shape[0]), mask_ref.shape[0]
    column = lax.broadcasted_iota(jnp.int32, (used, HEAD_DIM), 1)
    mask = jnp.zeros((used, HEAD_DIM), jnp.float32)
    for j in range(mask_ref.shape[1]):
        mask = jnp.where(column == j, mask_ref[:, j : j + 1].astype(jnp.float32), mask)
    if rows > used:
        mask = jnp.concatenate([mask, jnp.zeros((rows - used, HEAD_DIM), jnp.float32)])
    mask = mask.astype(k_ref.dtype)
    for k in range(n_ka):
        out_refs[0][k, 2 * key_blocks * BLOCK :] = mask
    for copy in copies:
        copy.wait()
    for c in range(heads):
        for k in range(n_ka):
            col = pl.multiple_of(((me_ref[0] ^ k) * heads + c) * HEAD_DIM, HEAD_DIM)
            for t in range(key_blocks):
                rows, at = slice(t * BLOCK, (t + 1) * BLOCK), 2 * t * BLOCK
                out_refs[c][k, at : at + BLOCK] = k_ref[rows, pl.ds(col, HEAD_DIM)]
                out_refs[c][k, at + BLOCK : at + 2 * BLOCK] = v_ref[rows, pl.ds(col, HEAD_DIM)].T


def mask_rows(rows):
    return -(-rows // 16) * 16


def pack(me, keys, values, mask, n_ka, heads):
    sizes = [2 * keys.shape[0] + (mask_rows(mask.shape[0]) if c == 0 else 0) for c in range(heads)]
    parts = 4
    return pl.pallas_call(
        functools.partial(pack_kernel, n_ka, heads),
        out_shape=[jax.ShapeDtypeStruct((n_ka, size, HEAD_DIM), keys.dtype) for size in sizes],
        in_specs=[SMEM, VMEM, ANY, ANY],
        out_specs=[VMEM] * heads,
        scratch_shapes=[
            pltpu.VMEM(keys.shape, keys.dtype),
            pltpu.VMEM(values.shape, values.dtype),
            pltpu.SemaphoreType.DMA((2, parts)),
        ],
        compiler_params=params(MOST_VMEM_BYTES),
        name="pack",
    )(me, mask, keys, values)


def turn_kernel(heads, me_ref, q_all, *refs):
    out_refs, (q_ref, sem) = refs[:heads], refs[heads:]
    column = pl.multiple_of(me_ref[0] * heads * HEAD_DIM, HEAD_DIM)
    copy = pltpu.make_async_copy(q_all.at[:, pl.ds(column, heads * HEAD_DIM)], q_ref, sem)
    copy.start()
    copy.wait()
    for c in range(heads):
        for r in range(out_refs[c].shape[0]):
            out_refs[c][r] = q_ref[r * BLOCK : (r + 1) * BLOCK, c * HEAD_DIM : (c + 1) * HEAD_DIM].T


def turn(me, queries, heads):
    tokens = queries.shape[0]
    shape = jax.ShapeDtypeStruct((tokens // BLOCK, HEAD_DIM, BLOCK), queries.dtype)
    return pl.pallas_call(
        functools.partial(turn_kernel, heads),
        out_shape=[shape] * heads,
        in_specs=[SMEM, ANY],
        out_specs=[VMEM] * heads,
        scratch_shapes=[pltpu.VMEM((tokens, heads * HEAD_DIM), queries.dtype), pltpu.SemaphoreType.DMA],
        compiler_params=params(MOST_VMEM_BYTES),
        name="turn",
    )(me, queries)


def plan_kernel(steps, n_pb, n_slots, key_blocks, rows, relay, pb_ref, *refs):
    mask_refs, count_ref, live_refs = refs[: -len(steps) - 1], refs[-len(steps) - 1], refs[-len(steps) :]
    pb = pb_ref[0]
    sign = 1 - 2 * (pb & 1)
    inner = ((pb > 0) & (pb < n_pb - 1)).astype(jnp.int32)
    helper = ((pb == 1) | (pb == n_pb - 2)).astype(jnp.int32)
    for step, (sources, live) in enumerate(zip(steps, live_refs)):
        total = jnp.int32(0)
        for guest, mask_ref in enumerate(mask_refs):

            def row_step(r, base, guest=guest, mask_ref=mask_ref):
                count = jnp.int32(0)
                for s, (delta, open_to_guests) in enumerate(sources):
                    if guest and not open_to_guests:
                        continue
                    j = pb + delta * sign
                    inside = ((j >= 0) & (j < n_pb)).astype(jnp.int32)
                    if relay and abs(delta) > 1:
                        inside = inside * inner
                    if guest:
                        inside = inside * helper
                    j = jnp.clip(j, 0, n_pb - 1)
                    for slot in range(n_slots):
                        for t in range(key_blocks):
                            block = (s * n_slots + slot) * key_blocks + t
                            live[2 * base + count] = ((r + guest * rows) << ROW_SHIFT) + block
                            column = j * key_blocks + t
                            count += inside * mask_ref[(slot * rows + r) * (n_pb * key_blocks) + column]
                live[2 * base + count] = -1
                return base + ((count + 1) >> 1)

            total = lax.fori_loop(0, rows, row_step, total)
        for u in range(GROUP):
            live[2 * (total + u)] = 0
            live[2 * (total + u) + 1] = -1
        count_ref[step] = total


def plan(pb, masks, steps, n_pb, n_slots, key_blocks, rows, relay):
    sizes = [len(masks) * rows * ((len(step) * n_slots * key_blocks + 2) // 2) + GROUP for step in steps]
    out_shape = [jax.ShapeDtypeStruct((len(steps),), jnp.int32)]
    out_shape += [jax.ShapeDtypeStruct((2 * size,), jnp.int32) for size in sizes]
    counts, *lives = pl.pallas_call(
        functools.partial(plan_kernel, steps, n_pb, n_slots, key_blocks, rows, relay),
        out_shape=out_shape,
        in_specs=[SMEM] * (1 + len(masks)),
        out_specs=[SMEM] * len(out_shape),
        compiler_params=params(),
        name="plan",
    )(pb, *masks)
    return [(counts, i, live) for i, live in enumerate(lives)]


def in_parts(x):
    found = []
    for _ in range(3):
        found.append(x.astype(jnp.bfloat16).astype(jnp.float32))
        x = x - found[-1]
    return found


def attend_kernel(n_src, entry, first, mode, guests, count_ref, live_ref, q_own, *refs):
    n_kv = n_src
    guest_ref, refs = (refs[0], refs[1:]) if guests else (None, refs)
    kv_refs, refs = refs[:n_kv], refs[n_kv:]
    state_in, refs = ((), refs) if first else (refs[:3], refs[3:])
    if mode == "last":
        (out_ref, kv, q_ref, *state, sems) = refs
    elif mode == "send":
        (*state, part_ref, kv, q_ref, sems) = refs
    else:
        (*state, kv, q_ref, sems) = refs
    m_ref, l_ref, acc_ref = state
    blocks = kv.shape[0] // n_src
    rows = q_own.shape[0]
    copies = [
        pltpu.make_async_copy(kv_refs[s], kv.at[pl.ds(s * blocks, blocks)], sems.at[s]) for s in range(n_src)
    ]
    copies += [pltpu.make_async_copy(a, b, sems.at[n_src + i]) for i, (a, b) in enumerate(zip(state_in, state))]
    copies.append(pltpu.make_async_copy(q_own, q_ref.at[pl.ds(0, rows)], sems.at[n_src + 3]))
    if guests:
        copies.append(pltpu.make_async_copy(guest_ref.at[pl.ds(0, rows)], q_ref.at[pl.ds(rows, rows)], sems.at[n_src + 4]))
    for copy in copies:
        copy.start()
    if first:
        m_ref[...] = jnp.full(m_ref.shape, NEG, jnp.float32)
        l_ref[...] = jnp.zeros(l_ref.shape, jnp.float32)
        acc_ref[...] = jnp.zeros(acc_ref.shape, jnp.float32)
    for copy in copies:
        copy.wait()
    total = count_ref[entry]
    nn = (((1,), (0,)), ((), ()))
    f32, bf16 = jnp.float32, jnp.bfloat16

    def group_step(g, _):
        found = []
        for u in range(GROUP):
            index = g * GROUP + u
            code0, code1 = live_ref[2 * index], live_ref[2 * index + 1]
            r = code0 >> ROW_SHIFT
            b0 = code0 & ((1 << ROW_SHIFT) - 1)
            b1 = jnp.maximum(code1, 0) & ((1 << ROW_SHIFT) - 1)
            x = lax.dot_general(jnp.concatenate([kv[b0, 0], kv[b1, 0]]), q_ref[r], nn, preferred_element_type=f32)
            x0 = jnp.where(index < total, x[:BLOCK], NEG)
            x1 = jnp.where(code1 >= 0, x[BLOCK:], NEG)
            top = jnp.max(jnp.maximum(x0, x1), axis=0, keepdims=True)
            w0 = jnp.exp2((x0 - top) * EXP2_SCALE)
            w1 = jnp.exp2((x1 - top) * EXP2_SCALE)
            total_w = jnp.sum(w0 + w1, axis=0, keepdims=True)
            w = jnp.concatenate([w0.astype(bf16), w1.astype(bf16)])
            v = jnp.concatenate([kv[b0, 1], kv[b1, 1]], axis=1)
            found.append((r, top, total_w, lax.dot_general(v, w, nn, preferred_element_type=f32)))
        for r, top, total_w, part in found:
            m = m_ref[r]
            m_new = jnp.maximum(m, top)
            alpha = jnp.exp2((m - m_new) * EXP2_SCALE)
            beta = jnp.exp2((top - m_new) * EXP2_SCALE)
            m_ref[r] = m_new
            l_ref[r] = l_ref[r] * alpha + total_w * beta
            acc_ref[r] = acc_ref[r] * alpha + part * beta
        return 0

    lax.fori_loop(0, (total + GROUP - 1) // GROUP, group_step, 0)
    if mode == "last":
        for r in range(rows):
            out_ref[r * BLOCK : (r + 1) * BLOCK, :] = (acc_ref[r] / l_ref[r]).T.astype(out_ref.dtype)
    if mode == "send":
        for r in range(rows):
            l = l_ref[rows + r]
            part_ref[r, :HEAD_DIM] = (acc_ref[rows + r] / jnp.where(l > 0, l, 1.0)).astype(part_ref.dtype)
            words = in_parts(m_ref[rows + r]) + in_parts(l)
            words.append(jnp.zeros((STAT_ROWS - len(words), BLOCK), f32))
            part_ref[r, HEAD_DIM:] = jnp.concatenate(words).astype(part_ref.dtype)


def attend(listed, q, guest, sources, state, mode, sets, name):
    counts, entry, live = listed
    rows, dtype = q.shape[0], q.dtype
    first = state is None
    state = () if first else tuple(state)
    stat = (sets * rows, 1, BLOCK)
    shapes = [stat, stat, (sets * rows, HEAD_DIM, BLOCK)]
    if mode == "last":
        out_shape = [jax.ShapeDtypeStruct((rows * BLOCK, HEAD_DIM), dtype)]
    else:
        out_shape = [jax.ShapeDtypeStruct(shape, jnp.float32) for shape in shapes]
    if mode == "send":
        out_shape.append(jax.ShapeDtypeStruct((rows, HEAD_DIM + STAT_ROWS, BLOCK), dtype))
    n_src = len(sources)
    blocks = sources[0].shape[0]
    guests = () if guest is None else (guest,)
    scratch = [pltpu.VMEM((n_src * blocks,) + sources[0].shape[1:], dtype)]
    scratch += [pltpu.VMEM(((1 + len(guests)) * rows, HEAD_DIM, BLOCK), dtype)]
    if mode == "last":
        scratch += [pltpu.VMEM(shape, jnp.float32) for shape in shapes]
    scratch.append(pltpu.SemaphoreType.DMA((n_src + 5,)))
    return pl.pallas_call(
        functools.partial(attend_kernel, n_src, entry, first, mode, bool(guests)),
        out_shape=out_shape,
        in_specs=[SMEM, SMEM, ANY] + [ANY] * (len(guests) + n_src + len(state)),
        out_specs=[VMEM] * len(out_shape),
        scratch_shapes=scratch,
        compiler_params=params(),
        cost_estimate=pl.CostEstimate(flops=0, bytes_accessed=q.size, transcendentals=0),
        name=name,
    )(counts, live, q, *guests, *sources, *state)


def merge_kernel(outer_ref, m_ref, l_ref, acc_ref, part_ref, out_ref):
    outer = outer_ref[0] > 0
    for r in range(part_ref.shape[0]):
        m, l = m_ref[r], l_ref[r]
        words = part_ref[r, HEAD_DIM:].astype(jnp.float32)
        top = jnp.where(outer, words[0:1] + words[1:2] + words[2:3], NEG)
        extra = jnp.where(outer, words[3:4] + words[4:5] + words[5:6], 0.0)
        m_new = jnp.maximum(m, top)
        alpha = jnp.exp2((m - m_new) * EXP2_SCALE)
        beta = jnp.exp2((top - m_new) * EXP2_SCALE) * extra
        done = (acc_ref[r] * alpha + part_ref[r, :HEAD_DIM].astype(jnp.float32) * beta) / (l * alpha + beta)
        out_ref[r * BLOCK : (r + 1) * BLOCK, :] = done.T.astype(out_ref.dtype)


def merge(outer, state, part, name):
    rows = part.shape[0]
    half = lambda x: pl.BlockSpec((rows,) + x.shape[1:], lambda i: (0, 0, 0))
    return pl.pallas_call(
        merge_kernel,
        out_shape=jax.ShapeDtypeStruct((rows * BLOCK, HEAD_DIM), part.dtype),
        grid=(1,),
        in_specs=[SMEM] + [half(x) for x in state] + [VMEM],
        out_specs=VMEM,
        compiler_params=params(),
        name=name,
    )(outer, *state, part)


def place_kernel(n_ka, heads, me_ref, *refs):
    pieces, out_ref, sems = refs[: n_ka * heads], refs[-2], refs[-1]
    copies = []
    for k in range(n_ka):
        for c in range(heads):
            col = pl.multiple_of(((me_ref[0] ^ k) * heads + c) * HEAD_DIM, HEAD_DIM)
            copies.append(
                pltpu.make_async_copy(pieces[c * n_ka + k], out_ref.at[:, pl.ds(col, HEAD_DIM)], sems.at[c, k])
            )
    for copy in copies:
        copy.start()
    for copy in copies:
        copy.wait()


def place(me, pieces, n_ka, heads):
    rows = pieces[0].shape[0]
    return pl.pallas_call(
        functools.partial(place_kernel, n_ka, heads),
        out_shape=jax.ShapeDtypeStruct((rows, HEADS * HEAD_DIM), pieces[0].dtype),
        in_specs=[SMEM] + [ANY] * (n_ka * heads),
        out_specs=ANY,
        scratch_shapes=[pltpu.SemaphoreType.DMA((heads, n_ka))],
        compiler_params=params(),
        name="place",
    )(me, *pieces)


def local(n_pb, n_ka, queries, keys, values, block_mask):
    heads = HEADS // n_ka
    shard = keys.shape[0]
    key_blocks = shard // BLOCK
    rows = queries.shape[0] // BLOCK
    me = lax.axis_index("ka").astype(jnp.int32)
    pb = lax.axis_index("pb").astype(jnp.int32)
    me1, pb1 = me[None], pb[None]
    relay = n_pb >= 4 and n_pb % 2 == 0
    def swap(x, k):
        return lax.ppermute(x, "ka", [(i, i ^ k) for i in range(n_ka)])

    def hops(odd, step):
        found = []
        for low in range(odd, n_pb - 1, 2):
            found += [(low, low + 1)] if low - (step - 1) >= 0 else []
            found += [(low + 1, low)] if low + 1 + (step - 1) < n_pb else []
        if relay and step > 1:
            found = [(i, j) for i, j in found if 0 < j < n_pb - 1]
        return found

    def exchange(x, odd, step):
        found = hops(odd, step)
        return lax.ppermute(x, "pb", found) if found else None

    def inward(x):
        return lax.ppermute(x, "pb", [(0, 1), (n_pb - 1, n_pb - 2)])

    def outward(x):
        return lax.ppermute(x, "pb", [(1, 0), (n_pb - 2, n_pb - 1)])

    def sort(x):
        mixed = [x[:2]] + [swap(x[k : k + 2], k) for k in range(2, n_ka, 2)]
        theirs = swap(jnp.stack([x[1] for x in mixed]), 1)
        return jnp.concatenate([jnp.stack([x[0] for x in mixed]), theirs]), mixed[-1]

    def blocks(x):
        return x[:, : 2 * shard].reshape(n_ka * key_blocks, 2, BLOCK, HEAD_DIM)

    def after(arrays, done):
        return arrays if done is None else lax.optimization_barrier((arrays, done))[0]

    def flags(x):
        return x[:, :rows, : block_mask.shape[1]].astype(jnp.int32).reshape(-1)

    packed = pack(me1, keys, values, block_mask, n_ka, heads)
    owns, moved = [], None
    for c in range(heads):
        own, moved = sort(after(packed[c], moved))
        owns.append(blocks(own))
        if c == 0:
            marks = own[:, 2 * shard :]
    q = turn(me1, queries, heads)

    steps = [((0, False),)]
    for step in range(1, n_pb):
        found = (((step, False),) if hops(0, step) else ()) + (((-step, True),) if hops(1, step) else ())
        if step == 1:
            steps[0] += found
        elif found:
            steps.append(found)
    last = len(steps) - 1
    over = [[exchange(own, odd, 1) for odd in (0, 1)] for own in owns]
    masks = [flags(marks)]
    guest = [None] * heads
    if relay:
        first = jnp.concatenate([q[0], marks.reshape(-1, HEAD_DIM, BLOCK)])
        first = inward(after(first, over[0][0]))
        masks.append(flags(first[rows:].reshape(marks.shape)))
        guest = [first] + [inward(after(x, first)) for x in q[1:]]
    lists = plan(pb1, masks, steps, n_pb, n_ka, key_blocks, rows, relay)
    state = [None] * heads

    def run(c, step, sources):
        kind = "keep" if step < last else "send" if relay else "last"
        sources = [x for x in sources if x is not None]
        name = f"attend_{c}_{step}"
        return attend(lists[step], q[c], guest[c], sources, state[c], kind, 2 if relay else 1, name)

    for step in range(last):
        for c in range(heads):
            sources = ([owns[c]] if step == 0 else []) + over[c]
            over[c] = [exchange(over[c][1], 0, step + 2), exchange(over[c][0], 1, step + 2)]
            state[c] = run(c, step, sources)

    pieces = []
    out = None
    for c in range(heads):
        found = run(c, last, ([] if last else [owns[c]]) + after(over[c], out))
        if relay:
            outer = ((pb == 0) | (pb == n_pb - 1)).astype(jnp.int32)[None]
            out = merge(outer, found[:3], outward(found[3]), f"merge_{c}")
        else:
            out = found[0]
        mine = [out] + [swap(out, k) for k in range(2, n_ka, 2)]
        others = [swap(x, 1) for x in mine]
        pieces += [x for two in zip(mine, others) for x in two]
    return place(me1, pieces, n_ka, heads)


def solution(mesh):
    n_pb, n_ka = mesh.shape["pb"], mesh.shape["ka"]
    return jax.shard_map(
        functools.partial(local, n_pb, n_ka),
        mesh=mesh,
        in_specs=(P("pb", None), P(("ka", "pb"), None), P(("ka", "pb"), None), P("pb", "ka")),
        out_specs=P("pb", None),
        check_vma=False,
    )
```

```python
import functools
import math

import jax
import jax.numpy as jnp
from jax import lax
from jax.experimental import pallas as pl
from jax.experimental.pallas import tpu as pltpu
from jax.sharding import PartitionSpec as P

HEADS = 16
HEAD_DIM = 128
BLOCK = 128
NEG = -1e30
EXP2_SCALE = math.log2(math.e) / math.sqrt(HEAD_DIM)
GROUP = 8
STAT_ROWS = 16
ROW_SHIFT = 16
VMEM_BYTES = 40 * 1024 * 1024
MOST_VMEM_BYTES = 60 * 1024 * 1024

VMEM = pl.BlockSpec(memory_space=pltpu.VMEM)
SMEM = pl.BlockSpec(memory_space=pltpu.SMEM)
ANY = pl.BlockSpec(memory_space=pl.ANY)


def params(size=VMEM_BYTES):
    return pltpu.CompilerParams(vmem_limit_bytes=size)


def mask_rows(rows):
    return -(-rows // 16) * 16


def pack_kernel(n_ka, heads, c, marked, me_ref, *refs):
    mask_ref, refs = (refs[0], refs[1:]) if marked else (None, refs)
    k_all, v_all, *out_refs, v_ref, sems = refs
    key_blocks = k_all.shape[0] // BLOCK
    copies = []
    for k in range(n_ka):
        out_ref = out_refs[k // 2]
        col = pl.multiple_of(((me_ref[0] ^ k) * heads + c) * HEAD_DIM, HEAD_DIM)
        for t in range(key_blocks):
            rows, at = pl.ds(t * BLOCK, BLOCK), pl.ds(2 * t * BLOCK, BLOCK)
            sem = sems.at[k * key_blocks + t]
            copies.append(
                (
                    pltpu.make_async_copy(k_all.at[rows, pl.ds(col, HEAD_DIM)], out_ref.at[k % 2, at], sem.at[0]),
                    pltpu.make_async_copy(v_all.at[rows, pl.ds(col, HEAD_DIM)], v_ref.at[k, t], sem.at[1]),
                )
            )
    for pair in copies:
        for copy in pair:
            copy.start()
    if marked:
        for k in range(n_ka):
            out_refs[k // 2][k % 2, 2 * key_blocks * BLOCK :] = mask_ref[...]
    for k in range(n_ka):
        for t in range(key_blocks):
            copies[k * key_blocks + t][1].wait()
            out_refs[k // 2][k % 2, (2 * t + 1) * BLOCK : (2 * t + 2) * BLOCK] = v_ref[k, t].T
    for pair in copies:
        pair[0].wait()


def pack(me, keys, values, mask, n_ka, heads, c):
    key_blocks = keys.shape[0] // BLOCK
    size = 2 * keys.shape[0] + (0 if mask is None else mask.shape[0])
    masks = () if mask is None else (mask,)
    return pl.pallas_call(
        functools.partial(pack_kernel, n_ka, heads, c, bool(masks)),
        out_shape=[jax.ShapeDtypeStruct((2, size, HEAD_DIM), keys.dtype)] * (n_ka // 2),
        in_specs=[SMEM] + [VMEM] * len(masks) + [ANY, ANY],
        out_specs=[VMEM] * (n_ka // 2),
        scratch_shapes=[
            pltpu.VMEM((n_ka, key_blocks, BLOCK, HEAD_DIM), values.dtype),
            pltpu.SemaphoreType.DMA((n_ka * key_blocks, 2)),
        ],
        compiler_params=params(MOST_VMEM_BYTES),
        cost_estimate=pl.CostEstimate(flops=0, bytes_accessed=keys.size, transcendentals=0),
        name=f"pack_{c}",
    )(me, *masks, keys, values)


def turn_kernel(heads, me_ref, q_all, out_ref, q_ref, sem):
    column = pl.multiple_of(me_ref[0] * heads * HEAD_DIM, HEAD_DIM)
    copy = pltpu.make_async_copy(q_all.at[:, pl.ds(column, heads * HEAD_DIM)], q_ref, sem)
    copy.start()
    copy.wait()
    rows = out_ref.shape[1]
    for c in range(heads):
        for r in range(rows):
            out_ref[c, r] = q_ref[r * BLOCK : (r + 1) * BLOCK, c * HEAD_DIM : (c + 1) * HEAD_DIM].T


def turn(me, queries, heads):
    tokens = queries.shape[0]
    return pl.pallas_call(
        functools.partial(turn_kernel, heads),
        out_shape=jax.ShapeDtypeStruct((heads, tokens // BLOCK, HEAD_DIM, BLOCK), queries.dtype),
        in_specs=[SMEM, ANY],
        out_specs=VMEM,
        scratch_shapes=[pltpu.VMEM((tokens, heads * HEAD_DIM), queries.dtype), pltpu.SemaphoreType.DMA],
        compiler_params=params(MOST_VMEM_BYTES),
        cost_estimate=pl.CostEstimate(flops=0, bytes_accessed=queries.size // HEADS, transcendentals=0),
        name="turn",
    )(me, queries)


def plan_kernel(steps, n_pb, n_slots, key_blocks, rows, relay, pb_ref, *refs):
    mask_refs, count_ref, live_refs = refs[: -len(steps) - 1], refs[-len(steps) - 1], refs[-len(steps) :]
    pb = pb_ref[0]
    sign = 1 - 2 * (pb & 1)
    inner = ((pb > 0) & (pb < n_pb - 1)).astype(jnp.int32)
    helper = ((pb == 1) | (pb == n_pb - 2)).astype(jnp.int32)
    for step, (sources, live) in enumerate(zip(steps, live_refs)):
        total = jnp.int32(0)
        for guest, mask_ref in enumerate(mask_refs):

            def row_step(r, base, guest=guest, mask_ref=mask_ref):
                count = jnp.int32(0)
                for s, (delta, open_to_guests) in enumerate(sources):
                    if guest and not open_to_guests:
                        continue
                    j = pb + delta * sign
                    inside = ((j >= 0) & (j < n_pb)).astype(jnp.int32)
                    if relay and abs(delta) > 1:
                        inside = inside * inner
                    if guest:
                        inside = inside * helper
                    j = jnp.clip(j, 0, n_pb - 1)
                    for slot in range(n_slots):
                        for t in range(key_blocks):
                            block = (s * n_slots + slot) * key_blocks + t
                            live[2 * base + count] = ((r + guest * rows) << ROW_SHIFT) + block
                            column = j * key_blocks + t
                            count += inside * mask_ref[(slot * n_pb * key_blocks + column) * rows + r]
                live[2 * base + count] = -1
                return base + ((count + 1) >> 1)

            total = lax.fori_loop(0, rows, row_step, total)
        for u in range(GROUP):
            live[2 * (total + u)] = 0
            live[2 * (total + u) + 1] = -1
        count_ref[step] = total


def plan(pb, masks, steps, n_pb, n_slots, key_blocks, rows, relay):
    sizes = [len(masks) * rows * ((len(step) * n_slots * key_blocks + 2) // 2) + GROUP for step in steps]
    out_shape = [jax.ShapeDtypeStruct((len(steps),), jnp.int32)]
    out_shape += [jax.ShapeDtypeStruct((2 * size,), jnp.int32) for size in sizes]
    counts, *lives = pl.pallas_call(
        functools.partial(plan_kernel, steps, n_pb, n_slots, key_blocks, rows, relay),
        out_shape=out_shape,
        in_specs=[SMEM] * (1 + len(masks)),
        out_specs=[SMEM] * len(out_shape),
        compiler_params=params(),
        name="plan",
    )(pb, *masks)
    return [(counts, i, live) for i, live in enumerate(lives)]


def in_parts(x):
    found = []
    for _ in range(3):
        found.append(x.astype(jnp.bfloat16).astype(jnp.float32))
        x = x - found[-1]
    return found


def attend_kernel(c, n_src, entry, first, mode, guests, count_ref, live_ref, q_own, *refs):
    n_kv = n_src
    guest_ref, refs = (refs[0], refs[1:]) if guests else (None, refs)
    kv_refs, refs = refs[:n_kv], refs[n_kv:]
    state_in, refs = ((), refs) if first else (refs[:3], refs[3:])
    if mode == "last":
        (out_ref, kv, q_ref, *state, sems) = refs
    elif mode == "send":
        (*state, part_ref, kv, q_ref, sems) = refs
    else:
        (*state, kv, q_ref, sems) = refs
    m_ref, l_ref, acc_ref = state
    blocks = kv.shape[0] // n_src
    rows = q_own.shape[1]
    copies = [
        pltpu.make_async_copy(kv_refs[s], kv.at[pl.ds(s * blocks, blocks)], sems.at[s]) for s in range(n_src)
    ]
    copies += [pltpu.make_async_copy(a, b, sems.at[n_src + i]) for i, (a, b) in enumerate(zip(state_in, state))]
    copies.append(pltpu.make_async_copy(q_own.at[c], q_ref.at[pl.ds(0, rows)], sems.at[n_src + 3]))
    if guests:
        copies.append(pltpu.make_async_copy(guest_ref.at[c], q_ref.at[pl.ds(rows, rows)], sems.at[n_src + 4]))
    for copy in copies:
        copy.start()
    if first:
        m_ref[...] = jnp.full(m_ref.shape, NEG, jnp.float32)
        l_ref[...] = jnp.zeros(l_ref.shape, jnp.float32)
        acc_ref[...] = jnp.zeros(acc_ref.shape, jnp.float32)
    for copy in copies:
        copy.wait()
    total = count_ref[entry]
    nn = (((1,), (0,)), ((), ()))
    f32, bf16 = jnp.float32, jnp.bfloat16

    def group_step(g, _):
        found = []
        for u in range(GROUP):
            index = g * GROUP + u
            code0, code1 = live_ref[2 * index], live_ref[2 * index + 1]
            r = code0 >> ROW_SHIFT
            b0 = code0 & ((1 << ROW_SHIFT) - 1)
            b1 = jnp.maximum(code1, 0) & ((1 << ROW_SHIFT) - 1)
            x = lax.dot_general(jnp.concatenate([kv[b0, 0], kv[b1, 0]]), q_ref[r], nn, preferred_element_type=f32)
            x0 = jnp.where(index < total, x[:BLOCK], NEG)
            x1 = jnp.where(code1 >= 0, x[BLOCK:], NEG)
            top = jnp.max(jnp.maximum(x0, x1), axis=0, keepdims=True)
            w0 = jnp.exp2((x0 - top) * EXP2_SCALE)
            w1 = jnp.exp2((x1 - top) * EXP2_SCALE)
            total_w = jnp.sum(w0 + w1, axis=0, keepdims=True)
            w = jnp.concatenate([w0.astype(bf16), w1.astype(bf16)])
            v = jnp.concatenate([kv[b0, 1], kv[b1, 1]], axis=1)
            found.append((r, top, total_w, lax.dot_general(v, w, nn, preferred_element_type=f32)))
        for r, top, total_w, part in found:
            m = m_ref[r]
            m_new = jnp.maximum(m, top)
            alpha = jnp.exp2((m - m_new) * EXP2_SCALE)
            beta = jnp.exp2((top - m_new) * EXP2_SCALE)
            m_ref[r] = m_new
            l_ref[r] = l_ref[r] * alpha + total_w * beta
            acc_ref[r] = acc_ref[r] * alpha + part * beta
        return 0

    lax.fori_loop(0, (total + GROUP - 1) // GROUP, group_step, 0)
    if mode == "last":
        for r in range(rows):
            out_ref[r * BLOCK : (r + 1) * BLOCK, :] = (acc_ref[r] / l_ref[r]).T.astype(out_ref.dtype)
    if mode == "send":
        for r in range(rows):
            l = l_ref[rows + r]
            part_ref[r, :HEAD_DIM] = (acc_ref[rows + r] / jnp.where(l > 0, l, 1.0)).astype(part_ref.dtype)
            words = in_parts(m_ref[rows + r]) + in_parts(l)
            words.append(jnp.zeros((STAT_ROWS - len(words), BLOCK), f32))
            part_ref[r, HEAD_DIM:] = jnp.concatenate(words).astype(part_ref.dtype)


def attend(c, listed, q, guest, sources, state, mode, sets, name):
    counts, entry, live = listed
    rows, dtype = q.shape[1], q.dtype
    first = state is None
    state = () if first else tuple(state)
    stat = (sets * rows, 1, BLOCK)
    shapes = [stat, stat, (sets * rows, HEAD_DIM, BLOCK)]
    if mode == "last":
        out_shape = [jax.ShapeDtypeStruct((rows * BLOCK, HEAD_DIM), dtype)]
    else:
        out_shape = [jax.ShapeDtypeStruct(shape, jnp.float32) for shape in shapes]
    if mode == "send":
        out_shape.append(jax.ShapeDtypeStruct((rows, HEAD_DIM + STAT_ROWS, BLOCK), dtype))
    n_src = len(sources)
    blocks = sources[0].shape[0]
    guests = () if guest is None else (guest,)
    scratch = [pltpu.VMEM((n_src * blocks,) + sources[0].shape[1:], dtype)]
    scratch += [pltpu.VMEM(((1 + len(guests)) * rows, HEAD_DIM, BLOCK), dtype)]
    if mode == "last":
        scratch += [pltpu.VMEM(shape, jnp.float32) for shape in shapes]
    scratch.append(pltpu.SemaphoreType.DMA((n_src + 5,)))
    return pl.pallas_call(
        functools.partial(attend_kernel, c, n_src, entry, first, mode, bool(guests)),
        out_shape=out_shape,
        in_specs=[SMEM, SMEM, ANY] + [ANY] * (len(guests) + n_src + len(state)),
        out_specs=[VMEM] * len(out_shape),
        scratch_shapes=scratch,
        compiler_params=params(),
        cost_estimate=pl.CostEstimate(flops=0, bytes_accessed=HEAD_DIM * BLOCK, transcendentals=0),
        name=name,
    )(counts, live, q, *guests, *sources, *state)


def merge_kernel(outer_ref, m_ref, l_ref, acc_ref, part_ref, out_ref):
    outer = outer_ref[0] > 0
    for r in range(part_ref.shape[0]):
        m, l = m_ref[r], l_ref[r]
        words = part_ref[r, HEAD_DIM:].astype(jnp.float32)
        top = jnp.where(outer, words[0:1] + words[1:2] + words[2:3], NEG)
        extra = jnp.where(outer, words[3:4] + words[4:5] + words[5:6], 0.0)
        m_new = jnp.maximum(m, top)
        alpha = jnp.exp2((m - m_new) * EXP2_SCALE)
        beta = jnp.exp2((top - m_new) * EXP2_SCALE) * extra
        done = (acc_ref[r] * alpha + part_ref[r, :HEAD_DIM].astype(jnp.float32) * beta) / (l * alpha + beta)
        out_ref[r * BLOCK : (r + 1) * BLOCK, :] = done.T.astype(out_ref.dtype)


def merge(outer, state, part, name):
    rows = part.shape[0]
    half = lambda x: pl.BlockSpec((rows,) + x.shape[1:], lambda i: (0, 0, 0))
    return pl.pallas_call(
        merge_kernel,
        out_shape=jax.ShapeDtypeStruct((rows * BLOCK, HEAD_DIM), part.dtype),
        grid=(1,),
        in_specs=[SMEM] + [half(x) for x in state] + [VMEM],
        out_specs=VMEM,
        compiler_params=params(),
        name=name,
    )(outer, *state, part)


def place_kernel(n_ka, heads, me_ref, *refs):
    pieces, out_ref, sems = refs[: n_ka * heads], refs[-2], refs[-1]
    copies = []
    for k in range(n_ka):
        for c in range(heads):
            col = pl.multiple_of(((me_ref[0] ^ k) * heads + c) * HEAD_DIM, HEAD_DIM)
            copies.append(
                pltpu.make_async_copy(pieces[c * n_ka + k], out_ref.at[:, pl.ds(col, HEAD_DIM)], sems.at[c, k])
            )
    for copy in copies:
        copy.start()
    for copy in copies:
        copy.wait()


def place(me, pieces, n_ka, heads):
    rows = pieces[0].shape[0]
    return pl.pallas_call(
        functools.partial(place_kernel, n_ka, heads),
        out_shape=jax.ShapeDtypeStruct((rows, HEADS * HEAD_DIM), pieces[0].dtype),
        in_specs=[SMEM] + [ANY] * (n_ka * heads),
        out_specs=ANY,
        scratch_shapes=[pltpu.SemaphoreType.DMA((heads, n_ka))],
        compiler_params=params(),
        name="place",
    )(me, *pieces)


def local(n_pb, n_ka, queries, keys, values, block_mask):
    heads = HEADS // n_ka
    shard = keys.shape[0]
    key_blocks = shard // BLOCK
    rows = queries.shape[0] // BLOCK
    me = lax.axis_index("ka").astype(jnp.int32)
    pb = lax.axis_index("pb").astype(jnp.int32)
    me1, pb1 = me[None], pb[None]
    relay = n_pb >= 4 and n_pb % 2 == 0
    def swap(x, k):
        return lax.ppermute(x, "ka", [(i, i ^ k) for i in range(n_ka)])

    def hops(odd, step):
        found = []
        for low in range(odd, n_pb - 1, 2):
            found += [(low, low + 1)] if low - (step - 1) >= 0 else []
            found += [(low + 1, low)] if low + 1 + (step - 1) < n_pb else []
        if relay and step > 1:
            found = [(i, j) for i, j in found if 0 < j < n_pb - 1]
        return found

    def exchange(x, odd, step):
        found = hops(odd, step)
        return lax.ppermute(x, "pb", found) if found else None

    def inward(x):
        return lax.ppermute(x, "pb", [(0, 1), (n_pb - 1, n_pb - 2)])

    def outward(x):
        return lax.ppermute(x, "pb", [(1, 0), (n_pb - 2, n_pb - 1)])

    def sort(x):
        mixed = [y if i == 0 else swap(y, 2 * i) for i, y in enumerate(x)]
        theirs = swap(jnp.stack([y[1] for y in mixed]), 1)
        return jnp.concatenate([jnp.stack([y[0] for y in mixed]), theirs]), theirs

    def blocks(x):
        return x[:, : 2 * shard].reshape(n_ka * key_blocks, 2, BLOCK, HEAD_DIM)

    def after(arrays, done):
        return arrays if done is None else lax.optimization_barrier((arrays, done))[0]

    def flags(x):
        return x[:, : block_mask.shape[1], :rows].astype(jnp.int32).reshape(-1)

    columns = block_mask.shape[1]
    mask = jnp.pad(block_mask.T.astype(keys.dtype), ((0, mask_rows(columns) - columns), (0, HEAD_DIM - rows)))
    owns, moved = [], None
    for c in range(heads):
        packed = pack(after(me1, q) if c else me1, keys, values, None if c else mask, n_ka, heads, c)
        if c == 0:
            q = turn(after(me1, packed), queries, heads)
            guest = inward(q) if relay else None
        own, moved = sort(after(packed, (moved, guest) if c else None))
        owns.append(blocks(own))
        if c == 0:
            marks = own[:, 2 * shard :]

    steps = [((0, False),)]
    for step in range(1, n_pb):
        found = (((step, False),) if hops(0, step) else ()) + (((-step, True),) if hops(1, step) else ())
        if step == 1:
            steps[0] += found
        elif found:
            steps.append(found)
    last = len(steps) - 1
    masks = [flags(marks)]
    guest_marks = inward(marks) if relay else None
    if relay:
        masks.append(flags(guest_marks))
    lists = plan(pb1, masks, steps, n_pb, n_ka, key_blocks, rows, relay)
    over = []
    for c in range(heads):
        own = after(owns[c], (over[0][1], guest_marks) if c else None)
        over.append([exchange(own, odd, 1) for odd in (0, 1)])
    state = [None] * heads

    def run(c, step, sources):
        kind = "keep" if step < last else "send" if relay else "last"
        sources = [x for x in sources if x is not None]
        name = f"attend_{c}_{step}"
        return attend(c, lists[step], q, guest, sources, state[c], kind, 2 if relay else 1, name)

    for step in range(last):
        for c in range(heads):
            sources = ([owns[c]] if step == 0 else []) + over[c]
            even, odd = over[c]
            if even is not None and odd is not None:
                even, odd = lax.optimization_barrier((even, odd))
            over[c] = [exchange(odd, 0, step + 2), exchange(even, 1, step + 2)]
            state[c] = run(c, step, sources)

    pieces = []
    sent = far = None
    for c in range(heads):
        found = run(c, last, ([] if last else [owns[c]]) + after(over[c], sent))
        if relay:
            outer = ((pb == 0) | (pb == n_pb - 1)).astype(jnp.int32)[None]
            out = merge(outer, found[:3], outward(after(found[3], far)), f"merge_{c}")
        else:
            out = found[0]
        mine = [out] + [swap(out, k) for k in range(2, n_ka, 2)]
        sent, far = mine[: n_ka // 4 + 1], mine[n_ka // 4 + 1 :]
        others = [swap(x, 1) for x in mine]
        pieces += [x for two in zip(mine, others) for x in two]
    return place(me1, pieces, n_ka, heads)


def solution(mesh):
    n_pb, n_ka = mesh.shape["pb"], mesh.shape["ka"]
    return jax.shard_map(
        functools.partial(local, n_pb, n_ka),
        mesh=mesh,
        in_specs=(P("pb", None), P(("ka", "pb"), None), P(("ka", "pb"), None), P("pb", "ka")),
        out_specs=P("pb", None),
        check_vma=False,
    )
```

```python
import functools
import math

import jax
import jax.numpy as jnp
from jax import lax
from jax.experimental import pallas as pl
from jax.experimental.pallas import tpu as pltpu
from jax.sharding import PartitionSpec as P

HEADS = 16
HEAD_DIM = 128
BLOCK = 128
NEG = -1e30
EXP2_SCALE = math.log2(math.e) / math.sqrt(HEAD_DIM)
GROUP = 8
STAT_ROWS = 16
ROW_SHIFT = 16
VMEM_BYTES = 40 * 1024 * 1024
MOST_VMEM_BYTES = 60 * 1024 * 1024

VMEM = pl.BlockSpec(memory_space=pltpu.VMEM)
SMEM = pl.BlockSpec(memory_space=pltpu.SMEM)
ANY = pl.BlockSpec(memory_space=pl.ANY)


def params(size=VMEM_BYTES):
    return pltpu.CompilerParams(vmem_limit_bytes=size)


def mask_rows(rows):
    return -(-rows // 16) * 16


def pack_kernel(n_ka, heads, c, marked, me_ref, *refs):
    mask_ref, refs = (refs[0], refs[1:]) if marked else (None, refs)
    k_all, v_all, *out_refs, v_ref, sems = refs
    key_blocks = k_all.shape[0] // BLOCK
    copies = []
    for k in range(n_ka):
        out_ref = out_refs[k // 2]
        col = pl.multiple_of(((me_ref[0] ^ k) * heads + c) * HEAD_DIM, HEAD_DIM)
        for t in range(key_blocks):
            rows, at = pl.ds(t * BLOCK, BLOCK), pl.ds(2 * t * BLOCK, BLOCK)
            sem = sems.at[k * key_blocks + t]
            copies.append(
                (
                    pltpu.make_async_copy(k_all.at[rows, pl.ds(col, HEAD_DIM)], out_ref.at[k % 2, at], sem.at[0]),
                    pltpu.make_async_copy(v_all.at[rows, pl.ds(col, HEAD_DIM)], v_ref.at[k, t], sem.at[1]),
                )
            )
    for pair in copies:
        for copy in pair:
            copy.start()
    if marked:
        shape = (mask_rows(mask_ref.shape[0]), HEAD_DIM)
        row, column = (lax.broadcasted_iota(jnp.int32, shape, i) for i in (0, 1))
        mask = jnp.zeros(shape, jnp.int32)
        for i in range(mask_ref.shape[0]):
            for j in range(mask_ref.shape[1]):
                mask = jnp.where((row == i) & (column == j), mask_ref[i, j], mask)
        mask = mask.astype(jnp.float32).astype(k_all.dtype)
        for k in range(n_ka):
            out_refs[k // 2][k % 2, 2 * key_blocks * BLOCK :] = mask
    for k in range(n_ka):
        for t in range(key_blocks):
            copies[k * key_blocks + t][1].wait()
            out_refs[k // 2][k % 2, (2 * t + 1) * BLOCK : (2 * t + 2) * BLOCK] = v_ref[k, t].T
    for pair in copies:
        pair[0].wait()


def pack(me, keys, values, mask, n_ka, heads, c):
    key_blocks = keys.shape[0] // BLOCK
    size = 2 * keys.shape[0] + (0 if mask is None else mask_rows(mask.shape[0]))
    masks = () if mask is None else (mask,)
    return pl.pallas_call(
        functools.partial(pack_kernel, n_ka, heads, c, bool(masks)),
        out_shape=[jax.ShapeDtypeStruct((2, size, HEAD_DIM), keys.dtype)] * (n_ka // 2),
        in_specs=[SMEM] + [SMEM] * len(masks) + [ANY, ANY],
        out_specs=[VMEM] * (n_ka // 2),
        scratch_shapes=[
            pltpu.VMEM((n_ka, key_blocks, BLOCK, HEAD_DIM), values.dtype),
            pltpu.SemaphoreType.DMA((n_ka * key_blocks, 2)),
        ],
        compiler_params=params(MOST_VMEM_BYTES),
        cost_estimate=pl.CostEstimate(flops=0, bytes_accessed=keys.size, transcendentals=0),
        name=f"pack_{c}",
    )(me, *masks, keys, values)


def turn_kernel(heads, me_ref, q_all, out_ref, q_ref, sem):
    column = pl.multiple_of(me_ref[0] * heads * HEAD_DIM, HEAD_DIM)
    copy = pltpu.make_async_copy(q_all.at[:, pl.ds(column, heads * HEAD_DIM)], q_ref, sem)
    copy.start()
    copy.wait()
    rows = out_ref.shape[1]
    for c in range(heads):
        for r in range(rows):
            out_ref[c, r] = q_ref[r * BLOCK : (r + 1) * BLOCK, c * HEAD_DIM : (c + 1) * HEAD_DIM].T


def turn(me, queries, heads):
    tokens = queries.shape[0]
    return pl.pallas_call(
        functools.partial(turn_kernel, heads),
        out_shape=jax.ShapeDtypeStruct((heads, tokens // BLOCK, HEAD_DIM, BLOCK), queries.dtype),
        in_specs=[SMEM, ANY],
        out_specs=VMEM,
        scratch_shapes=[pltpu.VMEM((tokens, heads * HEAD_DIM), queries.dtype), pltpu.SemaphoreType.DMA],
        compiler_params=params(MOST_VMEM_BYTES),
        cost_estimate=pl.CostEstimate(flops=0, bytes_accessed=queries.size // HEADS, transcendentals=0),
        name="turn",
    )(me, queries)


def plan_kernel(steps, n_pb, n_slots, key_blocks, rows, relay, pb_ref, *refs):
    mask_refs, count_ref, live_refs = refs[: -len(steps) - 1], refs[-len(steps) - 1], refs[-len(steps) :]
    pb = pb_ref[0]
    sign = 1 - 2 * (pb & 1)
    inner = ((pb > 0) & (pb < n_pb - 1)).astype(jnp.int32)
    helper = ((pb == 1) | (pb == n_pb - 2)).astype(jnp.int32)
    for step, (sources, live) in enumerate(zip(steps, live_refs)):
        total = jnp.int32(0)
        for guest, mask_ref in enumerate(mask_refs):

            def row_step(r, base, guest=guest, mask_ref=mask_ref):
                count = jnp.int32(0)
                for s, (delta, open_to_guests) in enumerate(sources):
                    if guest and not open_to_guests:
                        continue
                    j = pb + delta * sign
                    inside = ((j >= 0) & (j < n_pb)).astype(jnp.int32)
                    if relay and abs(delta) > 1:
                        inside = inside * inner
                    if guest:
                        inside = inside * helper
                    j = jnp.clip(j, 0, n_pb - 1)
                    for slot in range(n_slots):
                        for t in range(key_blocks):
                            block = (s * n_slots + slot) * key_blocks + t
                            live[2 * base + count] = ((r + guest * rows) << ROW_SHIFT) + block
                            column = j * key_blocks + t
                            count += inside * mask_ref[(slot * n_pb * key_blocks + column) * rows + r]
                live[2 * base + count] = -1
                return base + ((count + 1) >> 1)

            total = lax.fori_loop(0, rows, row_step, total)
        for u in range(GROUP):
            live[2 * (total + u)] = 0
            live[2 * (total + u) + 1] = -1
        count_ref[step] = total


def plan(pb, masks, steps, n_pb, n_slots, key_blocks, rows, relay):
    sizes = [len(masks) * rows * ((len(step) * n_slots * key_blocks + 2) // 2) + GROUP for step in steps]
    out_shape = [jax.ShapeDtypeStruct((len(steps),), jnp.int32)]
    out_shape += [jax.ShapeDtypeStruct((2 * size,), jnp.int32) for size in sizes]
    counts, *lives = pl.pallas_call(
        functools.partial(plan_kernel, steps, n_pb, n_slots, key_blocks, rows, relay),
        out_shape=out_shape,
        in_specs=[SMEM] * (1 + len(masks)),
        out_specs=[SMEM] * len(out_shape),
        compiler_params=params(),
        name="plan",
    )(pb, *masks)
    return [(counts, i, live) for i, live in enumerate(lives)]


def in_parts(x):
    found = []
    for _ in range(3):
        found.append(x.astype(jnp.bfloat16).astype(jnp.float32))
        x = x - found[-1]
    return found


def attend_kernel(c, n_src, entry, first, mode, guests, count_ref, live_ref, q_own, *refs):
    n_kv = n_src
    guest_ref, refs = (refs[0], refs[1:]) if guests else (None, refs)
    kv_refs, refs = refs[:n_kv], refs[n_kv:]
    state_in, refs = ((), refs) if first else (refs[:3], refs[3:])
    if mode == "last":
        (out_ref, kv, q_ref, *state, sems) = refs
    elif mode == "send":
        (*state, part_ref, kv, q_ref, sems) = refs
    else:
        (*state, kv, q_ref, sems) = refs
    m_ref, l_ref, acc_ref = state
    blocks = kv.shape[0] // n_src
    rows = q_own.shape[1]
    copies = [
        pltpu.make_async_copy(kv_refs[s], kv.at[pl.ds(s * blocks, blocks)], sems.at[s]) for s in range(n_src)
    ]
    copies += [pltpu.make_async_copy(a, b, sems.at[n_src + i]) for i, (a, b) in enumerate(zip(state_in, state))]
    copies.append(pltpu.make_async_copy(q_own.at[c], q_ref.at[pl.ds(0, rows)], sems.at[n_src + 3]))
    if guests:
        copies.append(pltpu.make_async_copy(guest_ref.at[c], q_ref.at[pl.ds(rows, rows)], sems.at[n_src + 4]))
    for copy in copies:
        copy.start()
    if first:
        m_ref[...] = jnp.full(m_ref.shape, NEG, jnp.float32)
        l_ref[...] = jnp.zeros(l_ref.shape, jnp.float32)
        acc_ref[...] = jnp.zeros(acc_ref.shape, jnp.float32)
    for copy in copies:
        copy.wait()
    total = count_ref[entry]
    nn = (((1,), (0,)), ((), ()))
    f32, bf16 = jnp.float32, jnp.bfloat16

    def group_step(g, _):
        found = []
        for u in range(GROUP):
            index = g * GROUP + u
            code0, code1 = live_ref[2 * index], live_ref[2 * index + 1]
            r = code0 >> ROW_SHIFT
            b0 = code0 & ((1 << ROW_SHIFT) - 1)
            b1 = jnp.maximum(code1, 0) & ((1 << ROW_SHIFT) - 1)
            x = lax.dot_general(jnp.concatenate([kv[b0, 0], kv[b1, 0]]), q_ref[r], nn, preferred_element_type=f32)
            x0 = jnp.where(index < total, x[:BLOCK], NEG)
            x1 = jnp.where(code1 >= 0, x[BLOCK:], NEG)
            top = jnp.max(jnp.maximum(x0, x1), axis=0, keepdims=True)
            w0 = jnp.exp2((x0 - top) * EXP2_SCALE)
            w1 = jnp.exp2((x1 - top) * EXP2_SCALE)
            total_w = jnp.sum(w0 + w1, axis=0, keepdims=True)
            w = jnp.concatenate([w0.astype(bf16), w1.astype(bf16)])
            v = jnp.concatenate([kv[b0, 1], kv[b1, 1]], axis=1)
            found.append((r, top, total_w, lax.dot_general(v, w, nn, preferred_element_type=f32)))
        for r, top, total_w, part in found:
            m = m_ref[r]
            m_new = jnp.maximum(m, top)
            alpha = jnp.exp2((m - m_new) * EXP2_SCALE)
            beta = jnp.exp2((top - m_new) * EXP2_SCALE)
            m_ref[r] = m_new
            l_ref[r] = l_ref[r] * alpha + total_w * beta
            acc_ref[r] = acc_ref[r] * alpha + part * beta
        return 0

    lax.fori_loop(0, (total + GROUP - 1) // GROUP, group_step, 0)
    if mode == "last":
        for r in range(rows):
            out_ref[r * BLOCK : (r + 1) * BLOCK, :] = (acc_ref[r] / l_ref[r]).T.astype(out_ref.dtype)
    if mode == "send":
        for r in range(rows):
            l = l_ref[rows + r]
            part_ref[r, :HEAD_DIM] = (acc_ref[rows + r] / jnp.where(l > 0, l, 1.0)).astype(part_ref.dtype)
            words = in_parts(m_ref[rows + r]) + in_parts(l)
            words.append(jnp.zeros((STAT_ROWS - len(words), BLOCK), f32))
            part_ref[r, HEAD_DIM:] = jnp.concatenate(words).astype(part_ref.dtype)


def attend(c, listed, q, guest, sources, state, mode, sets, name):
    counts, entry, live = listed
    rows, dtype = q.shape[1], q.dtype
    first = state is None
    state = () if first else tuple(state)
    stat = (sets * rows, 1, BLOCK)
    shapes = [stat, stat, (sets * rows, HEAD_DIM, BLOCK)]
    if mode == "last":
        out_shape = [jax.ShapeDtypeStruct((rows * BLOCK, HEAD_DIM), dtype)]
    else:
        out_shape = [jax.ShapeDtypeStruct(shape, jnp.float32) for shape in shapes]
    if mode == "send":
        out_shape.append(jax.ShapeDtypeStruct((rows, HEAD_DIM + STAT_ROWS, BLOCK), dtype))
    n_src = len(sources)
    blocks = sources[0].shape[0]
    guests = () if guest is None else (guest,)
    scratch = [pltpu.VMEM((n_src * blocks,) + sources[0].shape[1:], dtype)]
    scratch += [pltpu.VMEM(((1 + len(guests)) * rows, HEAD_DIM, BLOCK), dtype)]
    if mode == "last":
        scratch += [pltpu.VMEM(shape, jnp.float32) for shape in shapes]
    scratch.append(pltpu.SemaphoreType.DMA((n_src + 5,)))
    return pl.pallas_call(
        functools.partial(attend_kernel, c, n_src, entry, first, mode, bool(guests)),
        out_shape=out_shape,
        in_specs=[SMEM, SMEM, ANY] + [ANY] * (len(guests) + n_src + len(state)),
        out_specs=[VMEM] * len(out_shape),
        scratch_shapes=scratch,
        compiler_params=params(),
        cost_estimate=pl.CostEstimate(flops=0, bytes_accessed=HEAD_DIM * BLOCK, transcendentals=0),
        name=name,
    )(counts, live, q, *guests, *sources, *state)


def merge_kernel(outer_ref, m_ref, l_ref, acc_ref, part_ref, out_ref):
    outer = outer_ref[0] > 0
    for r in range(part_ref.shape[0]):
        m, l = m_ref[r], l_ref[r]
        words = part_ref[r, HEAD_DIM:].astype(jnp.float32)
        top = jnp.where(outer, words[0:1] + words[1:2] + words[2:3], NEG)
        extra = jnp.where(outer, words[3:4] + words[4:5] + words[5:6], 0.0)
        m_new = jnp.maximum(m, top)
        alpha = jnp.exp2((m - m_new) * EXP2_SCALE)
        beta = jnp.exp2((top - m_new) * EXP2_SCALE) * extra
        done = (acc_ref[r] * alpha + part_ref[r, :HEAD_DIM].astype(jnp.float32) * beta) / (l * alpha + beta)
        out_ref[r * BLOCK : (r + 1) * BLOCK, :] = done.T.astype(out_ref.dtype)


def merge(outer, state, part, name):
    rows = part.shape[0]
    half = lambda x: pl.BlockSpec((rows,) + x.shape[1:], lambda i: (0, 0, 0))
    return pl.pallas_call(
        merge_kernel,
        out_shape=jax.ShapeDtypeStruct((rows * BLOCK, HEAD_DIM), part.dtype),
        grid=(1,),
        in_specs=[SMEM] + [half(x) for x in state] + [VMEM],
        out_specs=VMEM,
        compiler_params=params(),
        name=name,
    )(outer, *state, part)


def place_kernel(n_ka, heads, me_ref, *refs):
    pieces, out_ref, sems = refs[: n_ka * heads], refs[-2], refs[-1]
    copies = []
    for k in range(n_ka):
        for c in range(heads):
            col = pl.multiple_of(((me_ref[0] ^ k) * heads + c) * HEAD_DIM, HEAD_DIM)
            copies.append(
                pltpu.make_async_copy(pieces[c * n_ka + k], out_ref.at[:, pl.ds(col, HEAD_DIM)], sems.at[c, k])
            )
    for copy in copies:
        copy.start()
    for copy in copies:
        copy.wait()


def place(me, pieces, n_ka, heads):
    rows = pieces[0].shape[0]
    return pl.pallas_call(
        functools.partial(place_kernel, n_ka, heads),
        out_shape=jax.ShapeDtypeStruct((rows, HEADS * HEAD_DIM), pieces[0].dtype),
        in_specs=[SMEM] + [ANY] * (n_ka * heads),
        out_specs=ANY,
        scratch_shapes=[pltpu.SemaphoreType.DMA((heads, n_ka))],
        compiler_params=params(),
        name="place",
    )(me, *pieces)


def local(n_pb, n_ka, queries, keys, values, block_mask):
    heads = HEADS // n_ka
    shard = keys.shape[0]
    key_blocks = shard // BLOCK
    rows = queries.shape[0] // BLOCK
    me = lax.axis_index("ka").astype(jnp.int32)
    pb = lax.axis_index("pb").astype(jnp.int32)
    me1, pb1 = me[None], pb[None]
    relay = n_pb >= 4 and n_pb % 2 == 0
    def swap(x, k):
        return lax.ppermute(x, "ka", [(i, i ^ k) for i in range(n_ka)])

    def hops(odd, step):
        found = []
        for low in range(odd, n_pb - 1, 2):
            found += [(low, low + 1)] if low - (step - 1) >= 0 else []
            found += [(low + 1, low)] if low + 1 + (step - 1) < n_pb else []
        if relay and step > 1:
            found = [(i, j) for i, j in found if 0 < j < n_pb - 1]
        return found

    def exchange(x, odd, step):
        found = hops(odd, step)
        return lax.ppermute(x, "pb", found) if found else None

    def inward(x):
        return lax.ppermute(x, "pb", [(0, 1), (n_pb - 1, n_pb - 2)])

    def outward(x):
        return lax.ppermute(x, "pb", [(1, 0), (n_pb - 2, n_pb - 1)])

    def sort(x, before=None):
        mixed = [y if i == 0 else swap(y, 2 * i) for i, y in enumerate(x)]
        mixed = after(mixed, before)
        theirs = swap(jnp.stack([y[1] for y in mixed]), 1)
        return jnp.concatenate([jnp.stack([y[0] for y in mixed]), theirs]), theirs

    def blocks(x):
        return x[:, : 2 * shard].reshape(n_ka * key_blocks, 2, BLOCK, HEAD_DIM)

    def after(arrays, done):
        return arrays if done is None else lax.optimization_barrier((arrays, done))[0]

    def flags(x):
        return x[:, : block_mask.shape[1], :rows].astype(jnp.int32).reshape(-1)

    owns, over = [], []
    for c in range(heads):
        packed = pack(after(me1, q) if c else me1, keys, values, None if c else block_mask.T, n_ka, heads, c)
        if c == 0:
            q = turn(after(me1, packed), queries, heads)
            guest = inward(q) if relay else None
            own, moved = sort(packed, q)
            marks = own[:, 2 * shard :]
            guest_marks = inward(marks) if relay else None
        else:
            own, moved = sort(after(packed, (moved, guest)), over[0])
        owns.append(blocks(own))
        own = after(owns[c], (over[0][1], guest_marks) if c else None)
        over.append([exchange(own, odd, 1) for odd in (0, 1)])

    steps = [((0, False),)]
    for step in range(1, n_pb):
        found = (((step, False),) if hops(0, step) else ()) + (((-step, True),) if hops(1, step) else ())
        if step == 1:
            steps[0] += found
        elif found:
            steps.append(found)
    last = len(steps) - 1
    masks = [flags(marks)]
    if relay:
        masks.append(flags(guest_marks))
    lists = plan(pb1, masks, steps, n_pb, n_ka, key_blocks, rows, relay)
    state = [None] * heads

    def run(c, step, sources):
        kind = "keep" if step < last else "send" if relay else "last"
        sources = [x for x in sources if x is not None]
        name = f"attend_{c}_{step}"
        return attend(c, lists[step], q, guest, sources, state[c], kind, 2 if relay else 1, name)

    for step in range(last):
        for c in range(heads):
            sources = ([owns[c]] if step == 0 else []) + over[c]
            even, odd = over[c]
            if even is not None and odd is not None:
                even, odd = lax.optimization_barrier((even, odd))
            over[c] = [exchange(odd, 0, step + 2), exchange(even, 1, step + 2)]
            state[c] = run(c, step, sources)

    pieces = []
    sent = far = None
    for c in range(heads):
        found = run(c, last, ([] if last else [owns[c]]) + after(over[c], sent))
        if relay:
            outer = ((pb == 0) | (pb == n_pb - 1)).astype(jnp.int32)[None]
            out = merge(outer, found[:3], outward(after(found[3], far)), f"merge_{c}")
        else:
            out = found[0]
        mine = [out] + [swap(out, k) for k in range(2, n_ka, 2)]
        sent, far = mine[: n_ka // 4 + 1], mine[n_ka // 4 + 1 :]
        others = [swap(x, 1) for x in mine]
        pieces += [x for two in zip(mine, others) for x in two]
    return place(me1, pieces, n_ka, heads)


def solution(mesh):
    n_pb, n_ka = mesh.shape["pb"], mesh.shape["ka"]
    return jax.shard_map(
        functools.partial(local, n_pb, n_ka),
        mesh=mesh,
        in_specs=(P("pb", None), P(("ka", "pb"), None), P(("ka", "pb"), None), P("pb", "ka")),
        out_specs=P("pb", None),
        check_vma=False,
    )
```

```python
import functools
import math

import jax
import jax.numpy as jnp
from jax import lax
from jax.experimental import pallas as pl
from jax.experimental.pallas import tpu as pltpu
from jax.sharding import PartitionSpec as P

HEADS = 16
HEAD_DIM = 128
BLOCK = 128
NEG = -1e30
EXP2_SCALE = math.log2(math.e) / math.sqrt(HEAD_DIM)
GROUP = 8
STAT_ROWS = 16
ROW_SHIFT = 16
VMEM_BYTES = 40 * 1024 * 1024
MOST_VMEM_BYTES = 60 * 1024 * 1024

VMEM = pl.BlockSpec(memory_space=pltpu.VMEM)
SMEM = pl.BlockSpec(memory_space=pltpu.SMEM)
ANY = pl.BlockSpec(memory_space=pl.ANY)


def params(size=VMEM_BYTES):
    return pltpu.CompilerParams(vmem_limit_bytes=size)


def mask_rows(rows):
    return -(-rows // 16) * 16


def pack_kernel(n_ka, heads, c, n_masks, me_ref, *refs):
    mask_refs, refs = refs[:n_masks], refs[n_masks:]
    k_all, v_all, *out_refs, v_ref, sems = refs
    key_blocks = k_all.shape[0] // BLOCK
    copies = []
    for k in range(n_ka):
        out_ref = out_refs[k // 2]
        col = pl.multiple_of(((me_ref[0] ^ k) * heads + c) * HEAD_DIM, HEAD_DIM)
        for t in range(key_blocks):
            rows, at = pl.ds(t * BLOCK, BLOCK), pl.ds(2 * t * BLOCK, BLOCK)
            sem = sems.at[k * key_blocks + t]
            copies.append(
                (
                    pltpu.make_async_copy(k_all.at[rows, pl.ds(col, HEAD_DIM)], out_ref.at[k % 2, at], sem.at[0]),
                    pltpu.make_async_copy(v_all.at[rows, pl.ds(col, HEAD_DIM)], v_ref.at[k, t], sem.at[1]),
                )
            )
    for pair in copies:
        for copy in pair:
            copy.start()
    for i, mask_ref in enumerate(mask_refs):
        size = mask_rows(mask_ref.shape[0])
        row, column = (lax.broadcasted_iota(jnp.int32, (size, HEAD_DIM), axis) for axis in (0, 1))
        mask = jnp.zeros((size, HEAD_DIM), jnp.int32)
        for a in range(mask_ref.shape[0]):
            for b in range(mask_ref.shape[1]):
                mask = jnp.where((row == a) & (column == b), mask_ref[a, b], mask)
        mask = mask.astype(jnp.float32).astype(k_all.dtype)
        at = 2 * key_blocks * BLOCK + i * size
        for k in range(n_ka):
            out_refs[k // 2][k % 2, at : at + size] = mask
    for k in range(n_ka):
        for t in range(key_blocks):
            copies[k * key_blocks + t][1].wait()
            out_refs[k // 2][k % 2, (2 * t + 1) * BLOCK : (2 * t + 2) * BLOCK] = v_ref[k, t].T
    for pair in copies:
        pair[0].wait()


def pack(me, keys, values, masks, n_ka, heads, c):
    key_blocks = keys.shape[0] // BLOCK
    size = 2 * keys.shape[0] + sum(mask_rows(mask.shape[0]) for mask in masks)
    return pl.pallas_call(
        functools.partial(pack_kernel, n_ka, heads, c, len(masks)),
        out_shape=[jax.ShapeDtypeStruct((2, size, HEAD_DIM), keys.dtype)] * (n_ka // 2),
        in_specs=[SMEM] + [SMEM] * len(masks) + [ANY, ANY],
        out_specs=[VMEM] * (n_ka // 2),
        scratch_shapes=[
            pltpu.VMEM((n_ka, key_blocks, BLOCK, HEAD_DIM), values.dtype),
            pltpu.SemaphoreType.DMA((n_ka * key_blocks, 2)),
        ],
        compiler_params=params(MOST_VMEM_BYTES),
        cost_estimate=pl.CostEstimate(flops=0, bytes_accessed=keys.size, transcendentals=0),
        name=f"pack_{c}",
    )(me, *masks, keys, values)


def turn_kernel(heads, me_ref, q_all, *refs):
    out_refs, (q_ref, sem) = refs[:heads], refs[heads:]
    column = pl.multiple_of(me_ref[0] * heads * HEAD_DIM, HEAD_DIM)
    copy = pltpu.make_async_copy(q_all.at[:, pl.ds(column, heads * HEAD_DIM)], q_ref, sem)
    copy.start()
    copy.wait()
    for c in range(heads):
        for r in range(out_refs[c].shape[0]):
            out_refs[c][r] = q_ref[r * BLOCK : (r + 1) * BLOCK, c * HEAD_DIM : (c + 1) * HEAD_DIM].T


def turn(me, queries, heads):
    tokens = queries.shape[0]
    return pl.pallas_call(
        functools.partial(turn_kernel, heads),
        out_shape=[jax.ShapeDtypeStruct((tokens // BLOCK, HEAD_DIM, BLOCK), queries.dtype)] * heads,
        in_specs=[SMEM, ANY],
        out_specs=[VMEM] * heads,
        scratch_shapes=[pltpu.VMEM((tokens, heads * HEAD_DIM), queries.dtype), pltpu.SemaphoreType.DMA],
        compiler_params=params(MOST_VMEM_BYTES),
        cost_estimate=pl.CostEstimate(flops=0, bytes_accessed=queries.size // HEADS, transcendentals=0),
        name="turn",
    )(me, queries)


def plan_kernel(steps, n_pb, n_slots, key_blocks, rows, relay, pb_ref, *refs):
    mask_refs, count_ref, live_refs = refs[: -len(steps) - 1], refs[-len(steps) - 1], refs[-len(steps) :]
    pb = pb_ref[0]
    sign = 1 - 2 * (pb & 1)
    inner = ((pb > 0) & (pb < n_pb - 1)).astype(jnp.int32)
    helper = ((pb == 1) | (pb == n_pb - 2)).astype(jnp.int32)
    for step, (sources, live) in enumerate(zip(steps, live_refs)):
        total = jnp.int32(0)
        for guest, mask_ref in enumerate(mask_refs):

            def row_step(r, base, guest=guest, mask_ref=mask_ref):
                count = jnp.int32(0)
                for s, (delta, open_to_guests) in enumerate(sources):
                    if guest and not open_to_guests:
                        continue
                    j = pb + delta * sign
                    inside = ((j >= 0) & (j < n_pb)).astype(jnp.int32)
                    if relay and abs(delta) > 1:
                        inside = inside * inner
                    if guest:
                        inside = inside * helper
                    j = jnp.clip(j, 0, n_pb - 1)
                    for slot in range(n_slots):
                        for t in range(key_blocks):
                            block = (s * n_slots + slot) * key_blocks + t
                            live[2 * base + count] = ((r + guest * rows) << ROW_SHIFT) + block
                            column = j * key_blocks + t
                            count += inside * mask_ref[(slot * n_pb * key_blocks + column) * rows + r]
                live[2 * base + count] = -1
                return base + ((count + 1) >> 1)

            total = lax.fori_loop(0, rows, row_step, total)
        for u in range(GROUP):
            live[2 * (total + u)] = 0
            live[2 * (total + u) + 1] = -1
        count_ref[step] = total


def plan(pb, masks, steps, n_pb, n_slots, key_blocks, rows, relay):
    sizes = [len(masks) * rows * ((len(step) * n_slots * key_blocks + 2) // 2) + GROUP for step in steps]
    out_shape = [jax.ShapeDtypeStruct((len(steps),), jnp.int32)]
    out_shape += [jax.ShapeDtypeStruct((2 * size,), jnp.int32) for size in sizes]
    counts, *lives = pl.pallas_call(
        functools.partial(plan_kernel, steps, n_pb, n_slots, key_blocks, rows, relay),
        out_shape=out_shape,
        in_specs=[SMEM] * (1 + len(masks)),
        out_specs=[SMEM] * len(out_shape),
        compiler_params=params(),
        name="plan",
    )(pb, *masks)
    return [(counts, i, live) for i, live in enumerate(lives)]


def in_parts(x):
    found = []
    for _ in range(3):
        found.append(x.astype(jnp.bfloat16).astype(jnp.float32))
        x = x - found[-1]
    return found


def attend_kernel(n_src, entry, first, mode, guests, count_ref, live_ref, q_own, *refs):
    n_kv = n_src
    guest_ref, refs = (refs[0], refs[1:]) if guests else (None, refs)
    kv_refs, refs = refs[:n_kv], refs[n_kv:]
    state_in, refs = ((), refs) if first else (refs[:3], refs[3:])
    if mode == "last":
        (out_ref, kv, q_ref, *state, sems) = refs
    elif mode == "send":
        (*state, part_ref, kv, q_ref, sems) = refs
    else:
        (*state, kv, q_ref, sems) = refs
    m_ref, l_ref, acc_ref = state
    blocks = kv.shape[0] // n_src
    rows = q_own.shape[0]
    copies = [
        pltpu.make_async_copy(kv_refs[s], kv.at[pl.ds(s * blocks, blocks)], sems.at[s]) for s in range(n_src)
    ]
    copies += [pltpu.make_async_copy(a, b, sems.at[n_src + i]) for i, (a, b) in enumerate(zip(state_in, state))]
    copies.append(pltpu.make_async_copy(q_own, q_ref.at[pl.ds(0, rows)], sems.at[n_src + 3]))
    if guests:
        copies.append(pltpu.make_async_copy(guest_ref, q_ref.at[pl.ds(rows, rows)], sems.at[n_src + 4]))
    for copy in copies:
        copy.start()
    if first:
        m_ref[...] = jnp.full(m_ref.shape, NEG, jnp.float32)
        l_ref[...] = jnp.zeros(l_ref.shape, jnp.float32)
        acc_ref[...] = jnp.zeros(acc_ref.shape, jnp.float32)
    for copy in copies:
        copy.wait()
    total = count_ref[entry]
    nn = (((1,), (0,)), ((), ()))
    f32, bf16 = jnp.float32, jnp.bfloat16

    def group_step(g, _):
        found = []
        for u in range(GROUP):
            index = g * GROUP + u
            code0, code1 = live_ref[2 * index], live_ref[2 * index + 1]
            r = code0 >> ROW_SHIFT
            b0 = code0 & ((1 << ROW_SHIFT) - 1)
            b1 = jnp.maximum(code1, 0) & ((1 << ROW_SHIFT) - 1)
            x = lax.dot_general(jnp.concatenate([kv[b0, 0], kv[b1, 0]]), q_ref[r], nn, preferred_element_type=f32)
            x0 = jnp.where(index < total, x[:BLOCK], NEG)
            x1 = jnp.where(code1 >= 0, x[BLOCK:], NEG)
            top = jnp.max(jnp.maximum(x0, x1), axis=0, keepdims=True)
            w0 = jnp.exp2((x0 - top) * EXP2_SCALE)
            w1 = jnp.exp2((x1 - top) * EXP2_SCALE)
            total_w = jnp.sum(w0 + w1, axis=0, keepdims=True)
            w = jnp.concatenate([w0.astype(bf16), w1.astype(bf16)])
            v = jnp.concatenate([kv[b0, 1], kv[b1, 1]], axis=1)
            found.append((r, top, total_w, lax.dot_general(v, w, nn, preferred_element_type=f32)))
        for r, top, total_w, part in found:
            m = m_ref[r]
            m_new = jnp.maximum(m, top)
            alpha = jnp.exp2((m - m_new) * EXP2_SCALE)
            beta = jnp.exp2((top - m_new) * EXP2_SCALE)
            m_ref[r] = m_new
            l_ref[r] = l_ref[r] * alpha + total_w * beta
            acc_ref[r] = acc_ref[r] * alpha + part * beta
        return 0

    lax.fori_loop(0, (total + GROUP - 1) // GROUP, group_step, 0)
    if mode == "last":
        for r in range(rows):
            out_ref[r * BLOCK : (r + 1) * BLOCK, :] = (acc_ref[r] / l_ref[r]).T.astype(out_ref.dtype)
    if mode == "send":
        for r in range(rows):
            l = l_ref[rows + r]
            part_ref[r, :HEAD_DIM] = (acc_ref[rows + r] / jnp.where(l > 0, l, 1.0)).astype(part_ref.dtype)
            words = in_parts(m_ref[rows + r]) + in_parts(l)
            words.append(jnp.zeros((STAT_ROWS - len(words), BLOCK), f32))
            part_ref[r, HEAD_DIM:] = jnp.concatenate(words).astype(part_ref.dtype)


def attend(listed, q, guest, sources, state, mode, sets, name):
    counts, entry, live = listed
    rows, dtype = q.shape[0], q.dtype
    first = state is None
    state = () if first else tuple(state)
    stat = (sets * rows, 1, BLOCK)
    shapes = [stat, stat, (sets * rows, HEAD_DIM, BLOCK)]
    if mode == "last":
        out_shape = [jax.ShapeDtypeStruct((rows * BLOCK, HEAD_DIM), dtype)]
    else:
        out_shape = [jax.ShapeDtypeStruct(shape, jnp.float32) for shape in shapes]
    if mode == "send":
        out_shape.append(jax.ShapeDtypeStruct((rows, HEAD_DIM + STAT_ROWS, BLOCK), dtype))
    n_src = len(sources)
    blocks = sources[0].shape[0]
    guests = () if guest is None else (guest,)
    scratch = [pltpu.VMEM((n_src * blocks,) + sources[0].shape[1:], dtype)]
    scratch += [pltpu.VMEM(((1 + len(guests)) * rows, HEAD_DIM, BLOCK), dtype)]
    if mode == "last":
        scratch += [pltpu.VMEM(shape, jnp.float32) for shape in shapes]
    scratch.append(pltpu.SemaphoreType.DMA((n_src + 5,)))
    return pl.pallas_call(
        functools.partial(attend_kernel, n_src, entry, first, mode, bool(guests)),
        out_shape=out_shape,
        in_specs=[SMEM, SMEM, ANY] + [ANY] * (len(guests) + n_src + len(state)),
        out_specs=[VMEM] * len(out_shape),
        scratch_shapes=scratch,
        compiler_params=params(),
        cost_estimate=pl.CostEstimate(flops=0, bytes_accessed=HEAD_DIM * BLOCK, transcendentals=0),
        name=name,
    )(counts, live, q, *guests, *sources, *state)


def merge_kernel(outer_ref, m_ref, l_ref, acc_ref, part_ref, out_ref):
    outer = outer_ref[0] > 0
    for r in range(part_ref.shape[0]):
        m, l = m_ref[r], l_ref[r]
        words = part_ref[r, HEAD_DIM:].astype(jnp.float32)
        top = jnp.where(outer, words[0:1] + words[1:2] + words[2:3], NEG)
        extra = jnp.where(outer, words[3:4] + words[4:5] + words[5:6], 0.0)
        m_new = jnp.maximum(m, top)
        alpha = jnp.exp2((m - m_new) * EXP2_SCALE)
        beta = jnp.exp2((top - m_new) * EXP2_SCALE) * extra
        done = (acc_ref[r] * alpha + part_ref[r, :HEAD_DIM].astype(jnp.float32) * beta) / (l * alpha + beta)
        out_ref[r * BLOCK : (r + 1) * BLOCK, :] = done.T.astype(out_ref.dtype)


def merge(outer, state, part, name):
    rows = part.shape[0]
    half = lambda x: pl.BlockSpec((rows,) + x.shape[1:], lambda i: (0, 0, 0))
    return pl.pallas_call(
        merge_kernel,
        out_shape=jax.ShapeDtypeStruct((rows * BLOCK, HEAD_DIM), part.dtype),
        grid=(1,),
        in_specs=[SMEM] + [half(x) for x in state] + [VMEM],
        out_specs=VMEM,
        compiler_params=params(),
        name=name,
    )(outer, *state, part)


def place_kernel(n_ka, heads, me_ref, *refs):
    pieces, out_ref, sems = refs[: n_ka * heads], refs[-2], refs[-1]
    copies = []
    for k in range(n_ka):
        for c in range(heads):
            col = pl.multiple_of(((me_ref[0] ^ k) * heads + c) * HEAD_DIM, HEAD_DIM)
            copies.append(
                pltpu.make_async_copy(pieces[c * n_ka + k], out_ref.at[:, pl.ds(col, HEAD_DIM)], sems.at[c, k])
            )
    for copy in copies:
        copy.start()
    for copy in copies:
        copy.wait()


def place(me, pieces, n_ka, heads):
    rows = pieces[0].shape[0]
    return pl.pallas_call(
        functools.partial(place_kernel, n_ka, heads),
        out_shape=jax.ShapeDtypeStruct((rows, HEADS * HEAD_DIM), pieces[0].dtype),
        in_specs=[SMEM] + [ANY] * (n_ka * heads),
        out_specs=ANY,
        scratch_shapes=[pltpu.SemaphoreType.DMA((heads, n_ka))],
        compiler_params=params(),
        name="place",
    )(me, *pieces)


def local(n_pb, n_ka, queries, keys, values, block_mask):
    heads = HEADS // n_ka
    shard = keys.shape[0]
    key_blocks = shard // BLOCK
    rows = queries.shape[0] // BLOCK
    me = lax.axis_index("ka").astype(jnp.int32)
    pb = lax.axis_index("pb").astype(jnp.int32)
    me1, pb1 = me[None], pb[None]
    relay = n_pb >= 4 and n_pb % 2 == 0
    def swap(x, k):
        return lax.ppermute(x, "ka", [(i, i ^ k) for i in range(n_ka)])

    def hops(odd, step):
        found = []
        for low in range(odd, n_pb - 1, 2):
            found += [(low, low + 1)] if low - (step - 1) >= 0 else []
            found += [(low + 1, low)] if low + 1 + (step - 1) < n_pb else []
        if relay and step > 1:
            found = [(i, j) for i, j in found if 0 < j < n_pb - 1]
        return found

    def exchange(x, odd, step):
        found = hops(odd, step)
        return lax.ppermute(x, "pb", found) if found else None

    def inward(x):
        return lax.ppermute(x, "pb", [(0, 1), (n_pb - 1, n_pb - 2)])

    def outward(x):
        return lax.ppermute(x, "pb", [(1, 0), (n_pb - 2, n_pb - 1)])

    def sort(x, before=None):
        mixed = [y if i == 0 else swap(y, 2 * i) for i, y in enumerate(x)]
        mixed = after(mixed, before)
        theirs = swap(jnp.stack([y[1] for y in mixed]), 1)
        return jnp.concatenate([jnp.stack([y[0] for y in mixed]), theirs])

    def blocks(x):
        return x[:, : 2 * shard].reshape(n_ka * key_blocks, 2, BLOCK, HEAD_DIM)

    def after(arrays, done):
        return arrays if done is None else lax.optimization_barrier((arrays, done))[0]

    def flags(x):
        return x[:, : block_mask.shape[1], :rows].astype(jnp.int32).reshape(-1)

    parts = (block_mask.T,) + ((inward(block_mask.T),) if relay else ())
    owns, over, guest = [], [], [None] * heads
    for c in range(heads):
        place_of = after(me1, (q, owns[0])) if c else me1
        packed = pack(place_of, keys, values, parts if c == heads - 1 else (), n_ka, heads, c)
        if c == 0:
            q = turn(after(me1, packed), queries, heads)
            own = sort(packed, (q, parts))
        else:
            own = sort(packed, over[0])
        owns.append(blocks(own))
        over.append([exchange(after(owns[c], (over[0][1], guest[0]) if c else None), odd, 1) for odd in (0, 1)])
        if relay:
            guest[c] = inward(after(q[c], over[c]))
    size = mask_rows(block_mask.shape[1])
    masks = [flags(own[:, 2 * shard + i * size :]) for i in range(len(parts))]

    steps = [((0, False),)]
    for step in range(1, n_pb):
        found = (((step, False),) if hops(0, step) else ()) + (((-step, True),) if hops(1, step) else ())
        if step == 1:
            steps[0] += found
        elif found:
            steps.append(found)
    last = len(steps) - 1
    lists = plan(pb1, masks, steps, n_pb, n_ka, key_blocks, rows, relay)
    state = [None] * heads

    def run(c, step, sources):
        kind = "keep" if step < last else "send" if relay else "last"
        sources = [x for x in sources if x is not None]
        name = f"attend_{c}_{step}"
        return attend(lists[step], q[c], guest[c], sources, state[c], kind, 2 if relay else 1, name)

    for step in range(last):
        for c in range(heads):
            sources = ([owns[c]] if step == 0 else []) + over[c]
            even, odd = over[c]
            if even is not None and odd is not None:
                even, odd = lax.optimization_barrier((even, odd))
            over[c] = [exchange(odd, 0, step + 2), exchange(even, 1, step + 2)]
            state[c] = run(c, step, sources)

    pieces = []
    sent = far = None
    for c in range(heads):
        found = run(c, last, ([] if last else [owns[c]]) + after(over[c], sent))
        if relay:
            outer = ((pb == 0) | (pb == n_pb - 1)).astype(jnp.int32)[None]
            out = merge(outer, found[:3], outward(after(found[3], far)), f"merge_{c}")
        else:
            out = found[0]
        mine = [out] + [swap(out, k) for k in range(2, n_ka, 2)]
        sent, far = mine[: n_ka // 4 + 1], mine[n_ka // 4 + 1 :]
        others = [swap(x, 1) for x in mine]
        pieces += [x for two in zip(mine, others) for x in two]
    return place(me1, pieces, n_ka, heads)


def solution(mesh):
    n_pb, n_ka = mesh.shape["pb"], mesh.shape["ka"]
    return jax.shard_map(
        functools.partial(local, n_pb, n_ka),
        mesh=mesh,
        in_specs=(P("pb", None), P(("ka", "pb"), None), P(("ka", "pb"), None), P("pb", "ka")),
        out_specs=P("pb", None),
        check_vma=False,
    )
```

```python
import functools
import math

import jax
import jax.numpy as jnp
from jax import lax
from jax.experimental import pallas as pl
from jax.experimental.pallas import tpu as pltpu
from jax.sharding import PartitionSpec as P

HEADS = 16
HEAD_DIM = 128
BLOCK = 128
NEG = -1e30
EXP2_SCALE = math.log2(math.e) / math.sqrt(HEAD_DIM)
GROUP = 8
STAT_ROWS = 16
ROW_SHIFT = 16
VMEM_BYTES = 40 * 1024 * 1024
MOST_VMEM_BYTES = 60 * 1024 * 1024

VMEM = pl.BlockSpec(memory_space=pltpu.VMEM)
SMEM = pl.BlockSpec(memory_space=pltpu.SMEM)
ANY = pl.BlockSpec(memory_space=pl.ANY)


def params(size=VMEM_BYTES):
    return pltpu.CompilerParams(vmem_limit_bytes=size)


def mask_rows(rows):
    return -(-rows // 16) * 16


def pack_kernel(n_ka, heads, c, n_masks, me_ref, *refs):
    mask_refs, refs = refs[:n_masks], refs[n_masks:]
    k_all, v_all, *out_refs, v_ref, sems = refs
    key_blocks = k_all.shape[0] // BLOCK
    copies = []
    for k in range(n_ka):
        out_ref = out_refs[k // 2]
        col = pl.multiple_of(((me_ref[0] ^ k) * heads + c) * HEAD_DIM, HEAD_DIM)
        for t in range(key_blocks):
            rows, at = pl.ds(t * BLOCK, BLOCK), pl.ds(2 * t * BLOCK, BLOCK)
            sem = sems.at[k * key_blocks + t]
            copies.append(
                (
                    pltpu.make_async_copy(k_all.at[rows, pl.ds(col, HEAD_DIM)], out_ref.at[k % 2, at], sem.at[0]),
                    pltpu.make_async_copy(v_all.at[rows, pl.ds(col, HEAD_DIM)], v_ref.at[k, t], sem.at[1]),
                )
            )
    for pair in copies:
        for copy in pair:
            copy.start()
    for i, mask_ref in enumerate(mask_refs):
        size = mask_rows(mask_ref.shape[0])
        row, column = (lax.broadcasted_iota(jnp.int32, (size, HEAD_DIM), axis) for axis in (0, 1))
        mask = jnp.zeros((size, HEAD_DIM), jnp.int32)
        for a in range(mask_ref.shape[0]):
            for b in range(mask_ref.shape[1]):
                mask = jnp.where((row == a) & (column == b), mask_ref[a, b], mask)
        mask = mask.astype(jnp.float32).astype(k_all.dtype)
        at = 2 * key_blocks * BLOCK + i * size
        for k in range(n_ka):
            out_refs[k // 2][k % 2, at : at + size] = mask
    for k in range(n_ka):
        for t in range(key_blocks):
            copies[k * key_blocks + t][1].wait()
            out_refs[k // 2][k % 2, (2 * t + 1) * BLOCK : (2 * t + 2) * BLOCK] = v_ref[k, t].T
    for pair in copies:
        pair[0].wait()


def pack(me, keys, values, masks, n_ka, heads, c):
    key_blocks = keys.shape[0] // BLOCK
    size = 2 * keys.shape[0] + sum(mask_rows(mask.shape[0]) for mask in masks)
    return pl.pallas_call(
        functools.partial(pack_kernel, n_ka, heads, c, len(masks)),
        out_shape=[jax.ShapeDtypeStruct((2, size, HEAD_DIM), keys.dtype)] * (n_ka // 2),
        in_specs=[SMEM] + [SMEM] * len(masks) + [ANY, ANY],
        out_specs=[VMEM] * (n_ka // 2),
        scratch_shapes=[
            pltpu.VMEM((n_ka, key_blocks, BLOCK, HEAD_DIM), values.dtype),
            pltpu.SemaphoreType.DMA((n_ka * key_blocks, 2)),
        ],
        compiler_params=params(MOST_VMEM_BYTES),
        cost_estimate=pl.CostEstimate(flops=0, bytes_accessed=keys.size, transcendentals=0),
        name=f"pack_{c}",
    )(me, *masks, keys, values)


def turn_kernel(heads, me_ref, q_all, *refs):
    out_refs, (q_ref, sem) = refs[:heads], refs[heads:]
    column = pl.multiple_of(me_ref[0] * heads * HEAD_DIM, HEAD_DIM)
    copy = pltpu.make_async_copy(q_all.at[:, pl.ds(column, heads * HEAD_DIM)], q_ref, sem)
    copy.start()
    copy.wait()
    for c in range(heads):
        for r in range(out_refs[c].shape[0]):
            out_refs[c][r] = q_ref[r * BLOCK : (r + 1) * BLOCK, c * HEAD_DIM : (c + 1) * HEAD_DIM].T


def turn(me, queries, heads):
    tokens = queries.shape[0]
    return pl.pallas_call(
        functools.partial(turn_kernel, heads),
        out_shape=[jax.ShapeDtypeStruct((tokens // BLOCK, HEAD_DIM, BLOCK), queries.dtype)] * heads,
        in_specs=[SMEM, ANY],
        out_specs=[VMEM] * heads,
        scratch_shapes=[pltpu.VMEM((tokens, heads * HEAD_DIM), queries.dtype), pltpu.SemaphoreType.DMA],
        compiler_params=params(MOST_VMEM_BYTES),
        cost_estimate=pl.CostEstimate(flops=0, bytes_accessed=queries.size // HEADS, transcendentals=0),
        name="turn",
    )(me, queries)


def plan_kernel(steps, n_pb, n_slots, key_blocks, rows, relay, pb_ref, *refs):
    mask_refs, count_ref, live_refs = refs[: -len(steps) - 1], refs[-len(steps) - 1], refs[-len(steps) :]
    pb = pb_ref[0]
    sign = 1 - 2 * (pb & 1)
    inner = ((pb > 0) & (pb < n_pb - 1)).astype(jnp.int32)
    helper = ((pb == 1) | (pb == n_pb - 2)).astype(jnp.int32)
    for step, (sources, live) in enumerate(zip(steps, live_refs)):
        total = jnp.int32(0)
        for guest, mask_ref in enumerate(mask_refs):

            def row_step(r, base, guest=guest, mask_ref=mask_ref):
                count = jnp.int32(0)
                for s, (delta, open_to_guests) in enumerate(sources):
                    if guest and not open_to_guests:
                        continue
                    j = pb + delta * sign
                    inside = ((j >= 0) & (j < n_pb)).astype(jnp.int32)
                    if relay and abs(delta) > 1:
                        inside = inside * inner
                    if guest:
                        inside = inside * helper
                    j = jnp.clip(j, 0, n_pb - 1)
                    for slot in range(n_slots):
                        for t in range(key_blocks):
                            block = (s * n_slots + slot) * key_blocks + t
                            live[2 * base + count] = ((r + guest * rows) << ROW_SHIFT) + block
                            column = j * key_blocks + t
                            count += inside * mask_ref[(slot * n_pb * key_blocks + column) * rows + r]
                live[2 * base + count] = -1
                return base + ((count + 1) >> 1)

            total = lax.fori_loop(0, rows, row_step, total)
        for u in range(GROUP):
            live[2 * (total + u)] = 0
            live[2 * (total + u) + 1] = -1
        count_ref[step] = total


def plan(pb, masks, steps, n_pb, n_slots, key_blocks, rows, relay):
    sizes = [len(masks) * rows * ((len(step) * n_slots * key_blocks + 2) // 2) + GROUP for step in steps]
    out_shape = [jax.ShapeDtypeStruct((len(steps),), jnp.int32)]
    out_shape += [jax.ShapeDtypeStruct((2 * size,), jnp.int32) for size in sizes]
    counts, *lives = pl.pallas_call(
        functools.partial(plan_kernel, steps, n_pb, n_slots, key_blocks, rows, relay),
        out_shape=out_shape,
        in_specs=[SMEM] * (1 + len(masks)),
        out_specs=[SMEM] * len(out_shape),
        compiler_params=params(),
        name="plan",
    )(pb, *masks)
    return [(counts, i, live) for i, live in enumerate(lives)]


def in_parts(x):
    found = []
    for _ in range(3):
        found.append(x.astype(jnp.bfloat16).astype(jnp.float32))
        x = x - found[-1]
    return found


def attend_kernel(n_src, entry, first, mode, guests, count_ref, live_ref, q_own, *refs):
    n_kv = n_src
    guest_ref, refs = (refs[0], refs[1:]) if guests else (None, refs)
    kv_refs, refs = refs[:n_kv], refs[n_kv:]
    state_in, refs = ((), refs) if first else (refs[:3], refs[3:])
    if mode == "last":
        (out_ref, kv, q_ref, *state, sems) = refs
    elif mode == "send":
        (*state, part_ref, kv, q_ref, sems) = refs
    else:
        (*state, kv, q_ref, sems) = refs
    m_ref, l_ref, acc_ref = state
    blocks = kv.shape[0] // n_src
    rows = q_own.shape[0]
    copies = [
        pltpu.make_async_copy(kv_refs[s], kv.at[pl.ds(s * blocks, blocks)], sems.at[s]) for s in range(n_src)
    ]
    copies += [pltpu.make_async_copy(a, b, sems.at[n_src + i]) for i, (a, b) in enumerate(zip(state_in, state))]
    copies.append(pltpu.make_async_copy(q_own, q_ref.at[pl.ds(0, rows)], sems.at[n_src + 3]))
    if guests:
        copies.append(pltpu.make_async_copy(guest_ref, q_ref.at[pl.ds(rows, rows)], sems.at[n_src + 4]))
    for copy in copies:
        copy.start()
    if first:
        m_ref[...] = jnp.full(m_ref.shape, NEG, jnp.float32)
        l_ref[...] = jnp.zeros(l_ref.shape, jnp.float32)
        acc_ref[...] = jnp.zeros(acc_ref.shape, jnp.float32)
    for copy in copies:
        copy.wait()
    total = count_ref[entry]
    nn = (((1,), (0,)), ((), ()))
    f32, bf16 = jnp.float32, jnp.bfloat16

    def group_step(g, _):
        found = []
        for u in range(GROUP):
            index = g * GROUP + u
            code0, code1 = live_ref[2 * index], live_ref[2 * index + 1]
            r = code0 >> ROW_SHIFT
            b0 = code0 & ((1 << ROW_SHIFT) - 1)
            b1 = jnp.maximum(code1, 0) & ((1 << ROW_SHIFT) - 1)
            x = lax.dot_general(jnp.concatenate([kv[b0, 0], kv[b1, 0]]), q_ref[r], nn, preferred_element_type=f32)
            x0 = jnp.where(index < total, x[:BLOCK], NEG)
            x1 = jnp.where(code1 >= 0, x[BLOCK:], NEG)
            top = jnp.max(jnp.maximum(x0, x1), axis=0, keepdims=True)
            w0 = jnp.exp2((x0 - top) * EXP2_SCALE)
            w1 = jnp.exp2((x1 - top) * EXP2_SCALE)
            total_w = jnp.sum(w0 + w1, axis=0, keepdims=True)
            w = jnp.concatenate([w0.astype(bf16), w1.astype(bf16)])
            v = jnp.concatenate([kv[b0, 1], kv[b1, 1]], axis=1)
            found.append((r, top, total_w, lax.dot_general(v, w, nn, preferred_element_type=f32)))
        for r, top, total_w, part in found:
            m = m_ref[r]
            m_new = jnp.maximum(m, top)
            alpha = jnp.exp2((m - m_new) * EXP2_SCALE)
            beta = jnp.exp2((top - m_new) * EXP2_SCALE)
            m_ref[r] = m_new
            l_ref[r] = l_ref[r] * alpha + total_w * beta
            acc_ref[r] = acc_ref[r] * alpha + part * beta
        return 0

    lax.fori_loop(0, (total + GROUP - 1) // GROUP, group_step, 0)
    if mode == "last":
        for r in range(rows):
            out_ref[r * BLOCK : (r + 1) * BLOCK, :] = (acc_ref[r] / l_ref[r]).T.astype(out_ref.dtype)
    if mode == "send":
        for r in range(rows):
            l = l_ref[rows + r]
            part_ref[r, :HEAD_DIM] = (acc_ref[rows + r] / jnp.where(l > 0, l, 1.0)).astype(part_ref.dtype)
            words = in_parts(m_ref[rows + r]) + in_parts(l)
            words.append(jnp.zeros((STAT_ROWS - len(words), BLOCK), f32))
            part_ref[r, HEAD_DIM:] = jnp.concatenate(words).astype(part_ref.dtype)


def attend(listed, q, guest, sources, state, mode, sets, name):
    counts, entry, live = listed
    rows, dtype = q.shape[0], q.dtype
    first = state is None
    state = () if first else tuple(state)
    stat = (sets * rows, 1, BLOCK)
    shapes = [stat, stat, (sets * rows, HEAD_DIM, BLOCK)]
    if mode == "last":
        out_shape = [jax.ShapeDtypeStruct((rows * BLOCK, HEAD_DIM), dtype)]
    else:
        out_shape = [jax.ShapeDtypeStruct(shape, jnp.float32) for shape in shapes]
    if mode == "send":
        out_shape.append(jax.ShapeDtypeStruct((rows, HEAD_DIM + STAT_ROWS, BLOCK), dtype))
    n_src = len(sources)
    blocks = sources[0].shape[0]
    guests = () if guest is None else (guest,)
    scratch = [pltpu.VMEM((n_src * blocks,) + sources[0].shape[1:], dtype)]
    scratch += [pltpu.VMEM(((1 + len(guests)) * rows, HEAD_DIM, BLOCK), dtype)]
    if mode == "last":
        scratch += [pltpu.VMEM(shape, jnp.float32) for shape in shapes]
    scratch.append(pltpu.SemaphoreType.DMA((n_src + 5,)))
    return pl.pallas_call(
        functools.partial(attend_kernel, n_src, entry, first, mode, bool(guests)),
        out_shape=out_shape,
        in_specs=[SMEM, SMEM, ANY] + [ANY] * (len(guests) + n_src + len(state)),
        out_specs=[VMEM] * len(out_shape),
        scratch_shapes=scratch,
        compiler_params=params(),
        cost_estimate=pl.CostEstimate(flops=0, bytes_accessed=HEAD_DIM * BLOCK, transcendentals=0),
        name=name,
    )(counts, live, q, *guests, *sources, *state)


def merge_kernel(outer_ref, m_ref, l_ref, acc_ref, part_ref, out_ref):
    outer = outer_ref[0] > 0
    for r in range(part_ref.shape[0]):
        m, l = m_ref[r], l_ref[r]
        words = part_ref[r, HEAD_DIM:].astype(jnp.float32)
        top = jnp.where(outer, words[0:1] + words[1:2] + words[2:3], NEG)
        extra = jnp.where(outer, words[3:4] + words[4:5] + words[5:6], 0.0)
        m_new = jnp.maximum(m, top)
        alpha = jnp.exp2((m - m_new) * EXP2_SCALE)
        beta = jnp.exp2((top - m_new) * EXP2_SCALE) * extra
        done = (acc_ref[r] * alpha + part_ref[r, :HEAD_DIM].astype(jnp.float32) * beta) / (l * alpha + beta)
        out_ref[r * BLOCK : (r + 1) * BLOCK, :] = done.T.astype(out_ref.dtype)


def merge(outer, state, part, name):
    rows = part.shape[0]
    half = lambda x: pl.BlockSpec((rows,) + x.shape[1:], lambda i: (0, 0, 0))
    return pl.pallas_call(
        merge_kernel,
        out_shape=jax.ShapeDtypeStruct((rows * BLOCK, HEAD_DIM), part.dtype),
        grid=(1,),
        in_specs=[SMEM] + [half(x) for x in state] + [VMEM],
        out_specs=VMEM,
        compiler_params=params(),
        name=name,
    )(outer, *state, part)


def place_kernel(n_ka, heads, me_ref, *refs):
    pieces, out_ref, sems = refs[: n_ka * heads], refs[-2], refs[-1]
    copies = []
    for k in range(n_ka):
        for c in range(heads):
            col = pl.multiple_of(((me_ref[0] ^ k) * heads + c) * HEAD_DIM, HEAD_DIM)
            copies.append(
                pltpu.make_async_copy(pieces[c * n_ka + k], out_ref.at[:, pl.ds(col, HEAD_DIM)], sems.at[c, k])
            )
    for copy in copies:
        copy.start()
    for copy in copies:
        copy.wait()


def place(me, pieces, n_ka, heads):
    rows = pieces[0].shape[0]
    return pl.pallas_call(
        functools.partial(place_kernel, n_ka, heads),
        out_shape=jax.ShapeDtypeStruct((rows, HEADS * HEAD_DIM), pieces[0].dtype),
        in_specs=[SMEM] + [ANY] * (n_ka * heads),
        out_specs=ANY,
        scratch_shapes=[pltpu.SemaphoreType.DMA((heads, n_ka))],
        compiler_params=params(),
        name="place",
    )(me, *pieces)


def local(n_pb, n_ka, queries, keys, values, block_mask):
    heads = HEADS // n_ka
    shard = keys.shape[0]
    key_blocks = shard // BLOCK
    rows = queries.shape[0] // BLOCK
    me = lax.axis_index("ka").astype(jnp.int32)
    pb = lax.axis_index("pb").astype(jnp.int32)
    me1, pb1 = me[None], pb[None]
    relay = n_pb >= 4 and n_pb % 2 == 0
    def swap(x, k):
        return lax.ppermute(x, "ka", [(i, i ^ k) for i in range(n_ka)])

    def hops(odd, step):
        found = []
        for low in range(odd, n_pb - 1, 2):
            found += [(low, low + 1)] if low - (step - 1) >= 0 else []
            found += [(low + 1, low)] if low + 1 + (step - 1) < n_pb else []
        if relay and step > 1:
            found = [(i, j) for i, j in found if 0 < j < n_pb - 1]
        return found

    def exchange(x, odd, step):
        found = hops(odd, step)
        return lax.ppermute(x, "pb", found) if found else None

    def inward(x):
        return lax.ppermute(x, "pb", [(0, 1), (n_pb - 1, n_pb - 2)])

    def outward(x):
        return lax.ppermute(x, "pb", [(1, 0), (n_pb - 2, n_pb - 1)])

    def sort(x, before=None):
        mixed = [y if i == 0 else swap(y, 2 * i) for i, y in enumerate(x)]
        mixed = after(mixed, before)
        theirs = swap(jnp.stack([y[1] for y in mixed]), 1)
        return jnp.concatenate([jnp.stack([y[0] for y in mixed]), theirs])

    def blocks(x):
        return x[:, : 2 * shard].reshape(n_ka * key_blocks, 2, BLOCK, HEAD_DIM)

    def after(arrays, done):
        return arrays if done is None else lax.optimization_barrier((arrays, done))[0]

    def flags(x):
        return x[:, : block_mask.shape[1], :rows].astype(jnp.int32).reshape(-1)

    parts = (block_mask.T,) + ((inward(block_mask.T),) if relay else ())
    owns, over, guest = [], [], [None] * heads
    for c in range(heads):
        place_of = after(me1, (q, owns[0])) if c else me1
        packed = pack(place_of, keys, values, parts if c == heads - 1 else (), n_ka, heads, c)
        if c == 0:
            q = turn(after(me1, packed), queries, heads)
            own = sort(packed, (q, parts))
        else:
            own = sort(packed, over[0])
        owns.append(blocks(own))
        even = exchange(owns[c], 0, 1)
        odd = exchange(after(owns[c], (over[0], even) if c else None), 1, 1)
        over.append([even, odd])
        if relay:
            guest[c] = inward(after(q[c], even if c else over[0]))
    size = mask_rows(block_mask.shape[1])
    masks = [flags(own[:, 2 * shard + i * size :]) for i in range(len(parts))]

    steps = [((0, False),)]
    for step in range(1, n_pb):
        found = (((step, False),) if hops(0, step) else ()) + (((-step, True),) if hops(1, step) else ())
        if step == 1:
            steps[0] += found
        elif found:
            steps.append(found)
    last = len(steps) - 1
    late = relay and last == 1
    if late:
        (own_source, even_source, odd_source), far_sources = steps
        steps += [(own_source, even_source), (odd_source,) + far_sources]
    lists = plan(pb1, masks, steps, n_pb, n_ka, key_blocks, rows, relay)
    state = [None] * heads

    def run(c, step, sources):
        kind = "keep" if step < last else "send" if relay else "last"
        sources = [x for x in sources if x is not None]
        name = f"attend_{c}_{step}"
        listed = lists[step + (2 if late and c else 0)]
        seen = None if late and c and step == 0 else guest[c]
        return attend(listed, q[c], seen, sources, state[c], kind, 2 if relay else 1, name)

    if late and heads > 1:
        guest[0] = after(guest[0], over[1][0])
    for step in range(last):
        for c in range(heads):
            sources = ([owns[c]] if step == 0 else []) + over[c]
            even, odd = over[c]
            if late and c:
                sources = sources[:2]
                over[c] = [odd, exchange(even, 1, step + 2)]
            else:
                if even is not None and odd is not None:
                    even, odd = lax.optimization_barrier((even, odd))
                over[c] = [exchange(odd, 0, step + 2), exchange(even, 1, step + 2)]
            state[c] = run(c, step, sources)

    pieces = []
    sent = far = None
    for c in range(heads):
        found = run(c, last, ([] if last else [owns[c]]) + after(over[c], sent))
        if relay:
            outer = ((pb == 0) | (pb == n_pb - 1)).astype(jnp.int32)[None]
            out = merge(outer, found[:3], outward(after(found[3], far)), f"merge_{c}")
        else:
            out = found[0]
        mine = [out] + [swap(out, k) for k in range(2, n_ka, 2)]
        sent, far = mine[: n_ka // 4 + 1], mine[n_ka // 4 + 1 :]
        others = [swap(x, 1) for x in mine]
        pieces += [x for two in zip(mine, others) for x in two]
    return place(me1, pieces, n_ka, heads)


def solution(mesh):
    n_pb, n_ka = mesh.shape["pb"], mesh.shape["ka"]
    return jax.shard_map(
        functools.partial(local, n_pb, n_ka),
        mesh=mesh,
        in_specs=(P("pb", None), P(("ka", "pb"), None), P(("ka", "pb"), None), P("pb", "ka")),
        out_specs=P("pb", None),
        check_vma=False,
    )
```

```python
import functools
import math

import jax
import jax.numpy as jnp
from jax import lax
from jax.experimental import pallas as pl
from jax.experimental.pallas import tpu as pltpu
from jax.sharding import PartitionSpec as P

HEADS = 16
HEAD_DIM = 128
BLOCK = 128
NEG = -1e30
EXP2_SCALE = math.log2(math.e) / math.sqrt(HEAD_DIM)
GROUP = 8
STAT_ROWS = 16
ROW_SHIFT = 16
VMEM_BYTES = 40 * 1024 * 1024
MOST_VMEM_BYTES = 60 * 1024 * 1024

VMEM = pl.BlockSpec(memory_space=pltpu.VMEM)
SMEM = pl.BlockSpec(memory_space=pltpu.SMEM)
ANY = pl.BlockSpec(memory_space=pl.ANY)


def params(size=VMEM_BYTES):
    return pltpu.CompilerParams(vmem_limit_bytes=size)


def mask_rows(rows):
    return -(-rows // 16) * 16


def pack_kernel(n_ka, heads, c, n_masks, me_ref, *refs):
    mask_refs, refs = refs[:n_masks], refs[n_masks:]
    k_all, v_all, *out_refs, v_ref, sems = refs
    key_blocks = k_all.shape[0] // BLOCK
    copies = []
    for k in range(n_ka):
        out_ref = out_refs[k // 2]
        col = pl.multiple_of(((me_ref[0] ^ k) * heads + c) * HEAD_DIM, HEAD_DIM)
        for t in range(key_blocks):
            rows, at = pl.ds(t * BLOCK, BLOCK), pl.ds(2 * t * BLOCK, BLOCK)
            sem = sems.at[k * key_blocks + t]
            copies.append(
                (
                    pltpu.make_async_copy(k_all.at[rows, pl.ds(col, HEAD_DIM)], out_ref.at[k % 2, at], sem.at[0]),
                    pltpu.make_async_copy(v_all.at[rows, pl.ds(col, HEAD_DIM)], v_ref.at[k, t], sem.at[1]),
                )
            )
    for pair in copies:
        for copy in pair:
            copy.start()
    for i, mask_ref in enumerate(mask_refs):
        size = mask_rows(mask_ref.shape[0])
        row, column = (lax.broadcasted_iota(jnp.int32, (size, HEAD_DIM), axis) for axis in (0, 1))
        mask = jnp.zeros((size, HEAD_DIM), jnp.int32)
        for a in range(mask_ref.shape[0]):
            for b in range(mask_ref.shape[1]):
                mask = jnp.where((row == a) & (column == b), mask_ref[a, b], mask)
        mask = mask.astype(jnp.float32).astype(k_all.dtype)
        at = 2 * key_blocks * BLOCK + i * size
        for k in range(n_ka):
            out_refs[k // 2][k % 2, at : at + size] = mask
    for k in range(n_ka):
        for t in range(key_blocks):
            copies[k * key_blocks + t][1].wait()
            out_refs[k // 2][k % 2, (2 * t + 1) * BLOCK : (2 * t + 2) * BLOCK] = v_ref[k, t].T
    for pair in copies:
        pair[0].wait()


def pack(me, keys, values, masks, n_ka, heads, c):
    key_blocks = keys.shape[0] // BLOCK
    size = 2 * keys.shape[0] + sum(mask_rows(mask.shape[0]) for mask in masks)
    return pl.pallas_call(
        functools.partial(pack_kernel, n_ka, heads, c, len(masks)),
        out_shape=[jax.ShapeDtypeStruct((2, size, HEAD_DIM), keys.dtype)] * (n_ka // 2),
        in_specs=[SMEM] + [SMEM] * len(masks) + [ANY, ANY],
        out_specs=[VMEM] * (n_ka // 2),
        scratch_shapes=[
            pltpu.VMEM((n_ka, key_blocks, BLOCK, HEAD_DIM), values.dtype),
            pltpu.SemaphoreType.DMA((n_ka * key_blocks, 2)),
        ],
        compiler_params=params(MOST_VMEM_BYTES),
        cost_estimate=pl.CostEstimate(flops=0, bytes_accessed=keys.size, transcendentals=0),
        name=f"pack_{c}",
    )(me, *masks, keys, values)


def turn_kernel(heads, me_ref, q_all, *refs):
    out_refs, (q_ref, sem) = refs[:heads], refs[heads:]
    column = pl.multiple_of(me_ref[0] * heads * HEAD_DIM, HEAD_DIM)
    copy = pltpu.make_async_copy(q_all.at[:, pl.ds(column, heads * HEAD_DIM)], q_ref, sem)
    copy.start()
    copy.wait()
    for c in range(heads):
        for r in range(out_refs[c].shape[0]):
            out_refs[c][r] = q_ref[r * BLOCK : (r + 1) * BLOCK, c * HEAD_DIM : (c + 1) * HEAD_DIM].T


def turn(me, queries, heads):
    tokens = queries.shape[0]
    return pl.pallas_call(
        functools.partial(turn_kernel, heads),
        out_shape=[jax.ShapeDtypeStruct((tokens // BLOCK, HEAD_DIM, BLOCK), queries.dtype)] * heads,
        in_specs=[SMEM, ANY],
        out_specs=[VMEM] * heads,
        scratch_shapes=[pltpu.VMEM((tokens, heads * HEAD_DIM), queries.dtype), pltpu.SemaphoreType.DMA],
        compiler_params=params(MOST_VMEM_BYTES),
        cost_estimate=pl.CostEstimate(flops=0, bytes_accessed=queries.size // HEADS, transcendentals=0),
        name="turn",
    )(me, queries)


def plan_kernel(steps, n_pb, n_slots, key_blocks, rows, relay, pb_ref, *refs):
    mask_refs, count_ref, live_refs = refs[: -len(steps) - 1], refs[-len(steps) - 1], refs[-len(steps) :]
    pb = pb_ref[0]
    sign = 1 - 2 * (pb & 1)
    inner = ((pb > 0) & (pb < n_pb - 1)).astype(jnp.int32)
    helper = ((pb == 1) | (pb == n_pb - 2)).astype(jnp.int32)
    for step, (sources, live) in enumerate(zip(steps, live_refs)):
        total = jnp.int32(0)
        for guest, mask_ref in enumerate(mask_refs):

            def row_step(r, base, guest=guest, mask_ref=mask_ref):
                count = jnp.int32(0)
                for s, (delta, open_to_guests) in enumerate(sources):
                    if guest and not open_to_guests:
                        continue
                    j = pb + delta * sign
                    inside = ((j >= 0) & (j < n_pb)).astype(jnp.int32)
                    if relay and abs(delta) > 1:
                        inside = inside * inner
                    if guest:
                        inside = inside * helper
                    j = jnp.clip(j, 0, n_pb - 1)
                    for slot in range(n_slots):
                        for t in range(key_blocks):
                            block = (s * n_slots + slot) * key_blocks + t
                            live[2 * base + count] = ((r + guest * rows) << ROW_SHIFT) + block
                            column = j * key_blocks + t
                            count += inside * mask_ref[(slot * n_pb * key_blocks + column) * rows + r]
                live[2 * base + count] = -1
                return base + ((count + 1) >> 1)

            total = lax.fori_loop(0, rows, row_step, total)
        for u in range(GROUP):
            live[2 * (total + u)] = 0
            live[2 * (total + u) + 1] = -1
        count_ref[step] = total


def plan(pb, masks, steps, n_pb, n_slots, key_blocks, rows, relay):
    sizes = [len(masks) * rows * ((len(step) * n_slots * key_blocks + 2) // 2) + GROUP for step in steps]
    out_shape = [jax.ShapeDtypeStruct((len(steps),), jnp.int32)]
    out_shape += [jax.ShapeDtypeStruct((2 * size,), jnp.int32) for size in sizes]
    counts, *lives = pl.pallas_call(
        functools.partial(plan_kernel, steps, n_pb, n_slots, key_blocks, rows, relay),
        out_shape=out_shape,
        in_specs=[SMEM] * (1 + len(masks)),
        out_specs=[SMEM] * len(out_shape),
        compiler_params=params(),
        name="plan",
    )(pb, *masks)
    return [(counts, i, live) for i, live in enumerate(lives)]


def in_parts(x):
    found = []
    for _ in range(3):
        found.append(x.astype(jnp.bfloat16).astype(jnp.float32))
        x = x - found[-1]
    return found


def attend_kernel(n_src, entry, first, mode, guests, count_ref, live_ref, q_own, *refs):
    n_kv = n_src
    guest_ref, refs = (refs[0], refs[1:]) if guests else (None, refs)
    kv_refs, refs = refs[:n_kv], refs[n_kv:]
    state_in, refs = ((), refs) if first else (refs[:3], refs[3:])
    if mode == "last":
        (out_ref, kv, q_ref, *state, sems) = refs
    elif mode == "send":
        (*state, part_ref, kv, q_ref, sems) = refs
    else:
        (*state, kv, q_ref, sems) = refs
    m_ref, l_ref, acc_ref = state
    blocks = kv.shape[0] // n_src
    rows = q_own.shape[0]
    copies = [
        pltpu.make_async_copy(kv_refs[s], kv.at[pl.ds(s * blocks, blocks)], sems.at[s]) for s in range(n_src)
    ]
    copies += [pltpu.make_async_copy(a, b, sems.at[n_src + i]) for i, (a, b) in enumerate(zip(state_in, state))]
    copies.append(pltpu.make_async_copy(q_own, q_ref.at[pl.ds(0, rows)], sems.at[n_src + 3]))
    if guests:
        copies.append(pltpu.make_async_copy(guest_ref, q_ref.at[pl.ds(rows, rows)], sems.at[n_src + 4]))
    for copy in copies:
        copy.start()
    if first:
        m_ref[...] = jnp.full(m_ref.shape, NEG, jnp.float32)
        l_ref[...] = jnp.zeros(l_ref.shape, jnp.float32)
        acc_ref[...] = jnp.zeros(acc_ref.shape, jnp.float32)
    for copy in copies:
        copy.wait()
    total = count_ref[entry]
    nn = (((1,), (0,)), ((), ()))
    f32, bf16 = jnp.float32, jnp.bfloat16

    def group_step(g, _):
        found = []
        for u in range(GROUP):
            index = g * GROUP + u
            code0, code1 = live_ref[2 * index], live_ref[2 * index + 1]
            r = code0 >> ROW_SHIFT
            b0 = code0 & ((1 << ROW_SHIFT) - 1)
            b1 = jnp.maximum(code1, 0) & ((1 << ROW_SHIFT) - 1)
            x = lax.dot_general(jnp.concatenate([kv[b0, 0], kv[b1, 0]]), q_ref[r], nn, preferred_element_type=f32)
            x0 = jnp.where(index < total, x[:BLOCK], NEG)
            x1 = jnp.where(code1 >= 0, x[BLOCK:], NEG)
            top = jnp.max(jnp.maximum(x0, x1), axis=0, keepdims=True)
            w0 = jnp.exp2((x0 - top) * EXP2_SCALE)
            w1 = jnp.exp2((x1 - top) * EXP2_SCALE)
            total_w = jnp.sum(w0 + w1, axis=0, keepdims=True)
            w = jnp.concatenate([w0.astype(bf16), w1.astype(bf16)])
            v = jnp.concatenate([kv[b0, 1], kv[b1, 1]], axis=1)
            found.append((r, top, total_w, lax.dot_general(v, w, nn, preferred_element_type=f32)))
        for r, top, total_w, part in found:
            m = m_ref[r]
            m_new = jnp.maximum(m, top)
            alpha = jnp.exp2((m - m_new) * EXP2_SCALE)
            beta = jnp.exp2((top - m_new) * EXP2_SCALE)
            m_ref[r] = m_new
            l_ref[r] = l_ref[r] * alpha + total_w * beta
            acc_ref[r] = acc_ref[r] * alpha + part * beta
        return 0

    lax.fori_loop(0, (total + GROUP - 1) // GROUP, group_step, 0)
    if mode == "last":
        for r in range(rows):
            out_ref[r * BLOCK : (r + 1) * BLOCK, :] = (acc_ref[r] / l_ref[r]).T.astype(out_ref.dtype)
    if mode == "send":
        for r in range(rows):
            l = l_ref[rows + r]
            part_ref[r, :HEAD_DIM] = (acc_ref[rows + r] / jnp.where(l > 0, l, 1.0)).astype(part_ref.dtype)
            words = in_parts(m_ref[rows + r]) + in_parts(l)
            words.append(jnp.zeros((STAT_ROWS - len(words), BLOCK), f32))
            part_ref[r, HEAD_DIM:] = jnp.concatenate(words).astype(part_ref.dtype)


def attend(listed, q, guest, sources, state, mode, sets, name):
    counts, entry, live = listed
    rows, dtype = q.shape[0], q.dtype
    first = state is None
    state = () if first else tuple(state)
    stat = (sets * rows, 1, BLOCK)
    shapes = [stat, stat, (sets * rows, HEAD_DIM, BLOCK)]
    if mode == "last":
        out_shape = [jax.ShapeDtypeStruct((rows * BLOCK, HEAD_DIM), dtype)]
    else:
        out_shape = [jax.ShapeDtypeStruct(shape, jnp.float32) for shape in shapes]
    if mode == "send":
        out_shape.append(jax.ShapeDtypeStruct((rows, HEAD_DIM + STAT_ROWS, BLOCK), dtype))
    n_src = len(sources)
    blocks = sources[0].shape[0]
    guests = () if guest is None else (guest,)
    scratch = [pltpu.VMEM((n_src * blocks,) + sources[0].shape[1:], dtype)]
    scratch += [pltpu.VMEM(((1 + len(guests)) * rows, HEAD_DIM, BLOCK), dtype)]
    if mode == "last":
        scratch += [pltpu.VMEM(shape, jnp.float32) for shape in shapes]
    scratch.append(pltpu.SemaphoreType.DMA((n_src + 5,)))
    return pl.pallas_call(
        functools.partial(attend_kernel, n_src, entry, first, mode, bool(guests)),
        out_shape=out_shape,
        in_specs=[SMEM, SMEM, ANY] + [ANY] * (len(guests) + n_src + len(state)),
        out_specs=[VMEM] * len(out_shape),
        scratch_shapes=scratch,
        compiler_params=params(),
        cost_estimate=pl.CostEstimate(flops=0, bytes_accessed=HEAD_DIM * BLOCK, transcendentals=0),
        name=name,
    )(counts, live, q, *guests, *sources, *state)


def merge_kernel(outer_ref, m_ref, l_ref, acc_ref, part_ref, out_ref):
    outer = outer_ref[0] > 0
    for r in range(part_ref.shape[0]):
        m, l = m_ref[r], l_ref[r]
        words = part_ref[r, HEAD_DIM:].astype(jnp.float32)
        top = jnp.where(outer, words[0:1] + words[1:2] + words[2:3], NEG)
        extra = jnp.where(outer, words[3:4] + words[4:5] + words[5:6], 0.0)
        m_new = jnp.maximum(m, top)
        alpha = jnp.exp2((m - m_new) * EXP2_SCALE)
        beta = jnp.exp2((top - m_new) * EXP2_SCALE) * extra
        done = (acc_ref[r] * alpha + part_ref[r, :HEAD_DIM].astype(jnp.float32) * beta) / (l * alpha + beta)
        out_ref[r * BLOCK : (r + 1) * BLOCK, :] = done.T.astype(out_ref.dtype)


def merge(outer, state, part, name):
    rows = part.shape[0]
    half = lambda x: pl.BlockSpec((rows,) + x.shape[1:], lambda i: (0, 0, 0))
    return pl.pallas_call(
        merge_kernel,
        out_shape=jax.ShapeDtypeStruct((rows * BLOCK, HEAD_DIM), part.dtype),
        grid=(1,),
        in_specs=[SMEM] + [half(x) for x in state] + [VMEM],
        out_specs=VMEM,
        compiler_params=params(),
        name=name,
    )(outer, *state, part)


def place_kernel(n_ka, heads, me_ref, *refs):
    pieces, out_ref, sems = refs[: n_ka * heads], refs[-2], refs[-1]
    copies = []
    for k in range(n_ka):
        for c in range(heads):
            col = pl.multiple_of(((me_ref[0] ^ k) * heads + c) * HEAD_DIM, HEAD_DIM)
            copies.append(
                pltpu.make_async_copy(pieces[c * n_ka + k], out_ref.at[:, pl.ds(col, HEAD_DIM)], sems.at[c, k])
            )
    for copy in copies:
        copy.start()
    for copy in copies:
        copy.wait()


def place(me, pieces, n_ka, heads):
    rows = pieces[0].shape[0]
    return pl.pallas_call(
        functools.partial(place_kernel, n_ka, heads),
        out_shape=jax.ShapeDtypeStruct((rows, HEADS * HEAD_DIM), pieces[0].dtype),
        in_specs=[SMEM] + [ANY] * (n_ka * heads),
        out_specs=ANY,
        scratch_shapes=[pltpu.SemaphoreType.DMA((heads, n_ka))],
        compiler_params=params(),
        name="place",
    )(me, *pieces)


def local(n_pb, n_ka, queries, keys, values, block_mask):
    heads = HEADS // n_ka
    shard = keys.shape[0]
    key_blocks = shard // BLOCK
    rows = queries.shape[0] // BLOCK
    me = lax.axis_index("ka").astype(jnp.int32)
    pb = lax.axis_index("pb").astype(jnp.int32)
    me1, pb1 = me[None], pb[None]
    relay = n_pb >= 4 and n_pb % 2 == 0
    def swap(x, k):
        return lax.ppermute(x, "ka", [(i, i ^ k) for i in range(n_ka)])

    def hops(odd, step):
        found = []
        for low in range(odd, n_pb - 1, 2):
            found += [(low, low + 1)] if low - (step - 1) >= 0 else []
            found += [(low + 1, low)] if low + 1 + (step - 1) < n_pb else []
        if relay and step > 1:
            found = [(i, j) for i, j in found if 0 < j < n_pb - 1]
        return found

    def exchange(x, odd, step):
        found = hops(odd, step)
        return lax.ppermute(x, "pb", found) if found else None

    def inward(x):
        return lax.ppermute(x, "pb", [(0, 1), (n_pb - 1, n_pb - 2)])

    def outward(x):
        return lax.ppermute(x, "pb", [(1, 0), (n_pb - 2, n_pb - 1)])

    def sort(x, before=None):
        mixed = [y if i == 0 else swap(y, 2 * i) for i, y in enumerate(x)]
        mixed = after(mixed, before)
        theirs = swap(jnp.stack([y[1] for y in mixed]), 1)
        return jnp.concatenate([jnp.stack([y[0] for y in mixed]), theirs])

    def blocks(x):
        return x[:, : 2 * shard].reshape(n_ka * key_blocks, 2, BLOCK, HEAD_DIM)

    def after(arrays, done):
        return arrays if done is None else lax.optimization_barrier((arrays, done))[0]

    def flags(x):
        return x[:, : block_mask.shape[1], :rows].astype(jnp.int32).reshape(-1)

    owns, over = [], []
    for c in range(heads):
        packed = pack(after(me1, packed) if c else me1, keys, values, () if c else (block_mask.T,), n_ka, heads, c)
        own = sort(packed, owns[-1] if c else None)
        owns.append(blocks(own))
        over.append([exchange(owns[c], odd, 1) for odd in (0, 1)])
        if c == 0:
            marks = own[:, 2 * shard :]
    q = turn(after(me1, owns), queries, heads)
    masks, guest = [flags(marks)], [None] * heads
    if relay:
        masks.append(flags(inward(marks)))
        guest = [inward(x) for x in q]

    steps = [((0, False),)]
    for step in range(1, n_pb):
        found = (((step, False),) if hops(0, step) else ()) + (((-step, True),) if hops(1, step) else ())
        if step == 1:
            steps[0] += found
        elif found:
            steps.append(found)
    last = len(steps) - 1
    lists = plan(pb1, masks, steps, n_pb, n_ka, key_blocks, rows, relay)
    state = [None] * heads

    def run(c, step, sources):
        kind = "keep" if step < last else "send" if relay else "last"
        sources = [x for x in sources if x is not None]
        name = f"attend_{c}_{step}"
        sources = after(sources, state[c - 1][0] if c else None)
        return attend(lists[step], q[c], guest[c], sources, state[c], kind, 2 if relay else 1, name)

    for step in range(last):
        for c in range(heads):
            sources = ([owns[c]] if step == 0 else []) + over[c]
            even, odd = over[c]
            if even is not None and odd is not None:
                even, odd = lax.optimization_barrier((even, odd))
            over[c] = [exchange(odd, 0, step + 2), exchange(even, 1, step + 2)]
            state[c] = run(c, step, sources)

    pieces = []
    for c in range(heads):
        found = state[c] = run(c, last, ([] if last else [owns[c]]) + over[c])
        if relay:
            outer = ((pb == 0) | (pb == n_pb - 1)).astype(jnp.int32)[None]
            out = merge(outer, found[:3], outward(found[3]), f"merge_{c}")
        else:
            out = found[0]
        mine = [out] + [swap(out, k) for k in range(2, n_ka, 2)]
        others = [swap(x, 1) for x in mine]
        pieces += [x for two in zip(mine, others) for x in two]
    return place(me1, pieces, n_ka, heads)


def solution(mesh):
    n_pb, n_ka = mesh.shape["pb"], mesh.shape["ka"]
    return jax.shard_map(
        functools.partial(local, n_pb, n_ka),
        mesh=mesh,
        in_specs=(P("pb", None), P(("ka", "pb"), None), P(("ka", "pb"), None), P("pb", "ka")),
        out_specs=P("pb", None),
        check_vma=False,
    )
```

```python
import functools
import math

import jax
import jax.numpy as jnp
from jax import lax
from jax.experimental import pallas as pl
from jax.experimental.pallas import tpu as pltpu
from jax.sharding import PartitionSpec as P

HEADS = 16
HEAD_DIM = 128
BLOCK = 128
NEG = -1e30
EXP2_SCALE = math.log2(math.e) / math.sqrt(HEAD_DIM)
GROUP = 8
STAT_ROWS = 16
ROW_SHIFT = 16
VMEM_BYTES = 40 * 1024 * 1024
MOST_VMEM_BYTES = 60 * 1024 * 1024

VMEM = pl.BlockSpec(memory_space=pltpu.VMEM)
SMEM = pl.BlockSpec(memory_space=pltpu.SMEM)
ANY = pl.BlockSpec(memory_space=pl.ANY)


def params(size=VMEM_BYTES):
    return pltpu.CompilerParams(vmem_limit_bytes=size)


def mask_rows(rows):
    return -(-rows // 16) * 16


def pack_kernel(n_ka, heads, c, n_masks, me_ref, *refs):
    mask_refs, refs = refs[:n_masks], refs[n_masks:]
    k_all, v_all, *out_refs, v_ref, sems = refs
    key_blocks = k_all.shape[0] // BLOCK
    copies = []
    for k in range(n_ka):
        out_ref = out_refs[k // 2]
        col = pl.multiple_of(((me_ref[0] ^ k) * heads + c) * HEAD_DIM, HEAD_DIM)
        for t in range(key_blocks):
            rows, at = pl.ds(t * BLOCK, BLOCK), pl.ds(2 * t * BLOCK, BLOCK)
            sem = sems.at[k * key_blocks + t]
            copies.append(
                (
                    pltpu.make_async_copy(k_all.at[rows, pl.ds(col, HEAD_DIM)], out_ref.at[k % 2, at], sem.at[0]),
                    pltpu.make_async_copy(v_all.at[rows, pl.ds(col, HEAD_DIM)], v_ref.at[k, t], sem.at[1]),
                )
            )
    for pair in copies:
        for copy in pair:
            copy.start()
    for i, mask_ref in enumerate(mask_refs):
        size = mask_rows(mask_ref.shape[0])
        row, column = (lax.broadcasted_iota(jnp.int32, (size, HEAD_DIM), axis) for axis in (0, 1))
        mask = jnp.zeros((size, HEAD_DIM), jnp.int32)
        for a in range(mask_ref.shape[0]):
            for b in range(mask_ref.shape[1]):
                mask = jnp.where((row == a) & (column == b), mask_ref[a, b], mask)
        mask = mask.astype(jnp.float32).astype(k_all.dtype)
        at = 2 * key_blocks * BLOCK + i * size
        for k in range(n_ka):
            out_refs[k // 2][k % 2, at : at + size] = mask
    for k in range(n_ka):
        for t in range(key_blocks):
            copies[k * key_blocks + t][1].wait()
            out_refs[k // 2][k % 2, (2 * t + 1) * BLOCK : (2 * t + 2) * BLOCK] = v_ref[k, t].T
    for pair in copies:
        pair[0].wait()


def pack(me, keys, values, masks, n_ka, heads, c):
    key_blocks = keys.shape[0] // BLOCK
    size = 2 * keys.shape[0] + sum(mask_rows(mask.shape[0]) for mask in masks)
    return pl.pallas_call(
        functools.partial(pack_kernel, n_ka, heads, c, len(masks)),
        out_shape=[jax.ShapeDtypeStruct((2, size, HEAD_DIM), keys.dtype)] * (n_ka // 2),
        in_specs=[SMEM] + [SMEM] * len(masks) + [ANY, ANY],
        out_specs=[VMEM] * (n_ka // 2),
        scratch_shapes=[
            pltpu.VMEM((n_ka, key_blocks, BLOCK, HEAD_DIM), values.dtype),
            pltpu.SemaphoreType.DMA((n_ka * key_blocks, 2)),
        ],
        compiler_params=params(MOST_VMEM_BYTES),
        cost_estimate=pl.CostEstimate(flops=0, bytes_accessed=keys.size, transcendentals=0),
        name=f"pack_{c}",
    )(me, *masks, keys, values)


def turn_kernel(heads, me_ref, q_all, *refs):
    out_refs, (q_ref, sem) = refs[:heads], refs[heads:]
    column = pl.multiple_of(me_ref[0] * heads * HEAD_DIM, HEAD_DIM)
    copy = pltpu.make_async_copy(q_all.at[:, pl.ds(column, heads * HEAD_DIM)], q_ref, sem)
    copy.start()
    copy.wait()
    for c in range(heads):
        for r in range(out_refs[c].shape[0]):
            out_refs[c][r] = q_ref[r * BLOCK : (r + 1) * BLOCK, c * HEAD_DIM : (c + 1) * HEAD_DIM].T


def turn(me, queries, heads):
    tokens = queries.shape[0]
    return pl.pallas_call(
        functools.partial(turn_kernel, heads),
        out_shape=[jax.ShapeDtypeStruct((tokens // BLOCK, HEAD_DIM, BLOCK), queries.dtype)] * heads,
        in_specs=[SMEM, ANY],
        out_specs=[VMEM] * heads,
        scratch_shapes=[pltpu.VMEM((tokens, heads * HEAD_DIM), queries.dtype), pltpu.SemaphoreType.DMA],
        compiler_params=params(MOST_VMEM_BYTES),
        cost_estimate=pl.CostEstimate(flops=0, bytes_accessed=queries.size // HEADS, transcendentals=0),
        name="turn",
    )(me, queries)


def plan_kernel(steps, n_pb, n_slots, key_blocks, rows, relay, pb_ref, *refs):
    mask_refs, count_ref, live_refs = refs[: -len(steps) - 1], refs[-len(steps) - 1], refs[-len(steps) :]
    pb = pb_ref[0]
    sign = 1 - 2 * (pb & 1)
    inner = ((pb > 0) & (pb < n_pb - 1)).astype(jnp.int32)
    helper = ((pb == 1) | (pb == n_pb - 2)).astype(jnp.int32)
    for step, (sources, live) in enumerate(zip(steps, live_refs)):
        total = jnp.int32(0)
        for guest, mask_ref in enumerate(mask_refs):

            def row_step(r, base, guest=guest, mask_ref=mask_ref):
                count = jnp.int32(0)
                for s, (delta, open_to_guests) in enumerate(sources):
                    if guest and not open_to_guests:
                        continue
                    j = pb + delta * sign
                    inside = ((j >= 0) & (j < n_pb)).astype(jnp.int32)
                    if relay and abs(delta) > 1:
                        inside = inside * inner
                    if guest:
                        inside = inside * helper
                    j = jnp.clip(j, 0, n_pb - 1)
                    for slot in range(n_slots):
                        for t in range(key_blocks):
                            block = (s * n_slots + slot) * key_blocks + t
                            live[2 * base + count] = ((r + guest * rows) << ROW_SHIFT) + block
                            column = j * key_blocks + t
                            count += inside * mask_ref[(slot * n_pb * key_blocks + column) * rows + r]
                live[2 * base + count] = -1
                return base + ((count + 1) >> 1)

            total = lax.fori_loop(0, rows, row_step, total)
        for u in range(GROUP):
            live[2 * (total + u)] = 0
            live[2 * (total + u) + 1] = -1
        count_ref[step] = total


def plan(pb, masks, steps, n_pb, n_slots, key_blocks, rows, relay):
    sizes = [len(masks) * rows * ((len(step) * n_slots * key_blocks + 2) // 2) + GROUP for step in steps]
    out_shape = [jax.ShapeDtypeStruct((len(steps),), jnp.int32)]
    out_shape += [jax.ShapeDtypeStruct((2 * size,), jnp.int32) for size in sizes]
    counts, *lives = pl.pallas_call(
        functools.partial(plan_kernel, steps, n_pb, n_slots, key_blocks, rows, relay),
        out_shape=out_shape,
        in_specs=[SMEM] * (1 + len(masks)),
        out_specs=[SMEM] * len(out_shape),
        compiler_params=params(),
        name="plan",
    )(pb, *masks)
    return [(counts, i, live) for i, live in enumerate(lives)]


def in_parts(x):
    found = []
    for _ in range(3):
        found.append(x.astype(jnp.bfloat16).astype(jnp.float32))
        x = x - found[-1]
    return found


def attend_kernel(n_src, entry, first, mode, guests, count_ref, live_ref, q_own, *refs):
    n_kv = n_src
    guest_ref, refs = (refs[0], refs[1:]) if guests else (None, refs)
    kv_refs, refs = refs[:n_kv], refs[n_kv:]
    state_in, refs = ((), refs) if first else (refs[:3], refs[3:])
    if mode == "last":
        (out_ref, kv, q_ref, *state, sems) = refs
    elif mode == "send":
        (*state, part_ref, kv, q_ref, sems) = refs
    else:
        (*state, kv, q_ref, sems) = refs
    m_ref, l_ref, acc_ref = state
    blocks = kv.shape[0] // n_src
    rows = q_own.shape[0]
    copies = [
        pltpu.make_async_copy(kv_refs[s], kv.at[pl.ds(s * blocks, blocks)], sems.at[s]) for s in range(n_src)
    ]
    copies += [pltpu.make_async_copy(a, b, sems.at[n_src + i]) for i, (a, b) in enumerate(zip(state_in, state))]
    copies.append(pltpu.make_async_copy(q_own, q_ref.at[pl.ds(0, rows)], sems.at[n_src + 3]))
    if guests:
        copies.append(pltpu.make_async_copy(guest_ref, q_ref.at[pl.ds(rows, rows)], sems.at[n_src + 4]))
    for copy in copies:
        copy.start()
    if first:
        m_ref[...] = jnp.full(m_ref.shape, NEG, jnp.float32)
        l_ref[...] = jnp.zeros(l_ref.shape, jnp.float32)
        acc_ref[...] = jnp.zeros(acc_ref.shape, jnp.float32)
    for copy in copies:
        copy.wait()
    total = count_ref[entry]
    nn = (((1,), (0,)), ((), ()))
    f32, bf16 = jnp.float32, jnp.bfloat16

    def group_step(g, _):
        found = []
        for u in range(GROUP):
            index = g * GROUP + u
            code0, code1 = live_ref[2 * index], live_ref[2 * index + 1]
            r = code0 >> ROW_SHIFT
            b0 = code0 & ((1 << ROW_SHIFT) - 1)
            b1 = jnp.maximum(code1, 0) & ((1 << ROW_SHIFT) - 1)
            x = lax.dot_general(jnp.concatenate([kv[b0, 0], kv[b1, 0]]), q_ref[r], nn, preferred_element_type=f32)
            x0 = jnp.where(index < total, x[:BLOCK], NEG)
            x1 = jnp.where(code1 >= 0, x[BLOCK:], NEG)
            top = jnp.max(jnp.maximum(x0, x1), axis=0, keepdims=True)
            w0 = jnp.exp2((x0 - top) * EXP2_SCALE)
            w1 = jnp.exp2((x1 - top) * EXP2_SCALE)
            total_w = jnp.sum(w0 + w1, axis=0, keepdims=True)
            w = jnp.concatenate([w0.astype(bf16), w1.astype(bf16)])
            v = jnp.concatenate([kv[b0, 1], kv[b1, 1]], axis=1)
            found.append((r, top, total_w, lax.dot_general(v, w, nn, preferred_element_type=f32)))
        for r, top, total_w, part in found:
            m = m_ref[r]
            m_new = jnp.maximum(m, top)
            alpha = jnp.exp2((m - m_new) * EXP2_SCALE)
            beta = jnp.exp2((top - m_new) * EXP2_SCALE)
            m_ref[r] = m_new
            l_ref[r] = l_ref[r] * alpha + total_w * beta
            acc_ref[r] = acc_ref[r] * alpha + part * beta
        return 0

    lax.fori_loop(0, (total + GROUP - 1) // GROUP, group_step, 0)
    if mode == "last":
        for r in range(rows):
            out_ref[r * BLOCK : (r + 1) * BLOCK, :] = (acc_ref[r] / l_ref[r]).T.astype(out_ref.dtype)
    if mode == "send":
        for r in range(rows):
            l = l_ref[rows + r]
            part_ref[r, :HEAD_DIM] = (acc_ref[rows + r] / jnp.where(l > 0, l, 1.0)).astype(part_ref.dtype)
            words = in_parts(m_ref[rows + r]) + in_parts(l)
            words.append(jnp.zeros((STAT_ROWS - len(words), BLOCK), f32))
            part_ref[r, HEAD_DIM:] = jnp.concatenate(words).astype(part_ref.dtype)


def attend(listed, q, guest, sources, state, mode, sets, name):
    counts, entry, live = listed
    rows, dtype = q.shape[0], q.dtype
    first = state is None
    state = () if first else tuple(state)
    stat = (sets * rows, 1, BLOCK)
    shapes = [stat, stat, (sets * rows, HEAD_DIM, BLOCK)]
    if mode == "last":
        out_shape = [jax.ShapeDtypeStruct((rows * BLOCK, HEAD_DIM), dtype)]
    else:
        out_shape = [jax.ShapeDtypeStruct(shape, jnp.float32) for shape in shapes]
    if mode == "send":
        out_shape.append(jax.ShapeDtypeStruct((rows, HEAD_DIM + STAT_ROWS, BLOCK), dtype))
    n_src = len(sources)
    blocks = sources[0].shape[0]
    guests = () if guest is None else (guest,)
    scratch = [pltpu.VMEM((n_src * blocks,) + sources[0].shape[1:], dtype)]
    scratch += [pltpu.VMEM(((1 + len(guests)) * rows, HEAD_DIM, BLOCK), dtype)]
    if mode == "last":
        scratch += [pltpu.VMEM(shape, jnp.float32) for shape in shapes]
    scratch.append(pltpu.SemaphoreType.DMA((n_src + 5,)))
    return pl.pallas_call(
        functools.partial(attend_kernel, n_src, entry, first, mode, bool(guests)),
        out_shape=out_shape,
        in_specs=[SMEM, SMEM, ANY] + [ANY] * (len(guests) + n_src + len(state)),
        out_specs=[VMEM] * len(out_shape),
        scratch_shapes=scratch,
        compiler_params=params(),
        cost_estimate=pl.CostEstimate(flops=0, bytes_accessed=HEAD_DIM * BLOCK, transcendentals=0),
        name=name,
    )(counts, live, q, *guests, *sources, *state)


def merge_kernel(outer_ref, m_ref, l_ref, acc_ref, part_ref, out_ref):
    outer = outer_ref[0] > 0
    for r in range(part_ref.shape[0]):
        m, l = m_ref[r], l_ref[r]
        words = part_ref[r, HEAD_DIM:].astype(jnp.float32)
        top = jnp.where(outer, words[0:1] + words[1:2] + words[2:3], NEG)
        extra = jnp.where(outer, words[3:4] + words[4:5] + words[5:6], 0.0)
        m_new = jnp.maximum(m, top)
        alpha = jnp.exp2((m - m_new) * EXP2_SCALE)
        beta = jnp.exp2((top - m_new) * EXP2_SCALE) * extra
        done = (acc_ref[r] * alpha + part_ref[r, :HEAD_DIM].astype(jnp.float32) * beta) / (l * alpha + beta)
        out_ref[r * BLOCK : (r + 1) * BLOCK, :] = done.T.astype(out_ref.dtype)


def merge(outer, state, part, name):
    rows = part.shape[0]
    half = lambda x: pl.BlockSpec((rows,) + x.shape[1:], lambda i: (0, 0, 0))
    return pl.pallas_call(
        merge_kernel,
        out_shape=jax.ShapeDtypeStruct((rows * BLOCK, HEAD_DIM), part.dtype),
        grid=(1,),
        in_specs=[SMEM] + [half(x) for x in state] + [VMEM],
        out_specs=VMEM,
        compiler_params=params(),
        name=name,
    )(outer, *state, part)


def place_kernel(n_ka, heads, me_ref, *refs):
    pieces, out_ref, sems = refs[: n_ka * heads], refs[-2], refs[-1]
    copies = []
    for k in range(n_ka):
        for c in range(heads):
            col = pl.multiple_of(((me_ref[0] ^ k) * heads + c) * HEAD_DIM, HEAD_DIM)
            copies.append(
                pltpu.make_async_copy(pieces[c * n_ka + k], out_ref.at[:, pl.ds(col, HEAD_DIM)], sems.at[c, k])
            )
    for copy in copies:
        copy.start()
    for copy in copies:
        copy.wait()


def place(me, pieces, n_ka, heads):
    rows = pieces[0].shape[0]
    return pl.pallas_call(
        functools.partial(place_kernel, n_ka, heads),
        out_shape=jax.ShapeDtypeStruct((rows, HEADS * HEAD_DIM), pieces[0].dtype),
        in_specs=[SMEM] + [ANY] * (n_ka * heads),
        out_specs=ANY,
        scratch_shapes=[pltpu.SemaphoreType.DMA((heads, n_ka))],
        compiler_params=params(),
        name="place",
    )(me, *pieces)


def local(n_pb, n_ka, queries, keys, values, block_mask):
    heads = HEADS // n_ka
    shard = keys.shape[0]
    key_blocks = shard // BLOCK
    rows = queries.shape[0] // BLOCK
    me = lax.axis_index("ka").astype(jnp.int32)
    pb = lax.axis_index("pb").astype(jnp.int32)
    me1, pb1 = me[None], pb[None]
    relay = n_pb >= 4 and n_pb % 2 == 0
    def swap(x, k):
        return lax.ppermute(x, "ka", [(i, i ^ k) for i in range(n_ka)])

    def hops(odd, step):
        found = []
        for low in range(odd, n_pb - 1, 2):
            found += [(low, low + 1)] if low - (step - 1) >= 0 else []
            found += [(low + 1, low)] if low + 1 + (step - 1) < n_pb else []
        if relay and step > 1:
            found = [(i, j) for i, j in found if 0 < j < n_pb - 1]
        return found

    def exchange(x, odd, step):
        found = hops(odd, step)
        return lax.ppermute(x, "pb", found) if found else None

    def inward(x):
        return lax.ppermute(x, "pb", [(0, 1), (n_pb - 1, n_pb - 2)])

    def outward(x):
        return lax.ppermute(x, "pb", [(1, 0), (n_pb - 2, n_pb - 1)])

    def sort(x, before=None):
        mixed = [y if i == 0 else swap(y, 2 * i) for i, y in enumerate(x)]
        mixed = after(mixed, before)
        theirs = swap(jnp.stack([y[1] for y in mixed]), 1)
        return jnp.concatenate([jnp.stack([y[0] for y in mixed]), theirs]), mixed

    def blocks(x):
        return x[:, : 2 * shard].reshape(n_ka * key_blocks, 2, BLOCK, HEAD_DIM)

    def after(arrays, done):
        return arrays if done is None else lax.optimization_barrier((arrays, done))[0]

    def flags(x):
        return x[:, : block_mask.shape[1], :rows].astype(jnp.int32).reshape(-1)

    parts = (block_mask.T,) + ((inward(block_mask.T),) if relay else ())
    owns, over, guest = [], [], [None] * heads
    for c in range(heads):
        place_of = after(me1, (q, mixed)) if c else me1
        packed = pack(place_of, keys, values, parts if c == heads - 1 else (), n_ka, heads, c)
        if c == 0:
            q = turn(after(me1, packed), queries, heads)
            own, mixed = sort(packed, (q, parts))
        else:
            own, mixed = sort(after(packed, owns[0]), over[0])
        owns.append(blocks(own))
        before = ((over[0], guest[0]), over[0]) if c else (None, None)
        over.append([exchange(after(owns[c], before[odd]), odd, 1) for odd in (0, 1)])
        if relay:
            guest[c] = inward(after(q[c], over[0]))
    size = mask_rows(block_mask.shape[1])
    masks = [flags(own[:, 2 * shard + i * size :]) for i in range(len(parts))]

    steps = [((0, False),)]
    for step in range(1, n_pb):
        found = (((step, False),) if hops(0, step) else ()) + (((-step, True),) if hops(1, step) else ())
        if step == 1:
            steps[0] += found
        elif found:
            steps.append(found)
    last = len(steps) - 1
    lists = plan(pb1, masks, steps, n_pb, n_ka, key_blocks, rows, relay)
    state = [None] * heads

    def run(c, step, sources):
        kind = "keep" if step < last else "send" if relay else "last"
        sources = [x for x in sources if x is not None]
        name = f"attend_{c}_{step}"
        return attend(lists[step], q[c], guest[c], sources, state[c], kind, 2 if relay else 1, name)

    for step in range(last):
        for c in range(heads):
            sources = ([owns[c]] if step == 0 else []) + over[c]
            even, odd = over[c]
            if even is not None and odd is not None:
                even, odd = after((even, odd), guest[c] if c else (even, odd))
            over[c] = [exchange(odd, 0, step + 2), exchange(even, 1, step + 2)]
            state[c] = run(c, step, sources)

    pieces = []
    sent = far = None
    for c in range(heads):
        found = run(c, last, ([] if last else [owns[c]]) + after(over[c], sent))
        if relay:
            outer = ((pb == 0) | (pb == n_pb - 1)).astype(jnp.int32)[None]
            out = merge(outer, found[:3], outward(after(found[3], far)), f"merge_{c}")
        else:
            out = found[0]
        mine = [out] + [swap(out, k) for k in range(2, n_ka, 2)]
        sent, far = mine[: n_ka // 4 + 1], mine[n_ka // 4 + 1 :]
        others = [swap(x, 1) for x in mine]
        pieces += [x for two in zip(mine, others) for x in two]
    return place(me1, pieces, n_ka, heads)


def solution(mesh):
    n_pb, n_ka = mesh.shape["pb"], mesh.shape["ka"]
    return jax.shard_map(
        functools.partial(local, n_pb, n_ka),
        mesh=mesh,
        in_specs=(P("pb", None), P(("ka", "pb"), None), P(("ka", "pb"), None), P("pb", "ka")),
        out_specs=P("pb", None),
        check_vma=False,
    )
```

```python
import functools
import math

import jax
import jax.numpy as jnp
from jax import lax
from jax.experimental import pallas as pl
from jax.experimental.pallas import tpu as pltpu
from jax.sharding import PartitionSpec as P

HEADS = 16
HEAD_DIM = 128
BLOCK = 128
NEG = -1e30
EXP2_SCALE = math.log2(math.e) / math.sqrt(HEAD_DIM)
GROUP = 8
STAT_ROWS = 16
ROW_SHIFT = 16
VMEM_BYTES = 40 * 1024 * 1024
MOST_VMEM_BYTES = 60 * 1024 * 1024

VMEM = pl.BlockSpec(memory_space=pltpu.VMEM)
SMEM = pl.BlockSpec(memory_space=pltpu.SMEM)
ANY = pl.BlockSpec(memory_space=pl.ANY)


def params(size=VMEM_BYTES):
    return pltpu.CompilerParams(vmem_limit_bytes=size)


def mask_rows(rows):
    return -(-rows // 16) * 16


def pack_kernel(n_ka, heads, c, n_masks, me_ref, *refs):
    mask_refs, refs = refs[:n_masks], refs[n_masks:]
    k_all, v_all, *out_refs, v_ref, sems = refs
    key_blocks = k_all.shape[0] // BLOCK
    copies = []
    for k in range(n_ka):
        out_ref = out_refs[k // 2]
        col = pl.multiple_of(((me_ref[0] ^ k) * heads + c) * HEAD_DIM, HEAD_DIM)
        for t in range(key_blocks):
            rows, at = pl.ds(t * BLOCK, BLOCK), pl.ds(2 * t * BLOCK, BLOCK)
            sem = sems.at[k * key_blocks + t]
            copies.append(
                (
                    pltpu.make_async_copy(k_all.at[rows, pl.ds(col, HEAD_DIM)], out_ref.at[k % 2, at], sem.at[0]),
                    pltpu.make_async_copy(v_all.at[rows, pl.ds(col, HEAD_DIM)], v_ref.at[k, t], sem.at[1]),
                )
            )
    for pair in copies:
        for copy in pair:
            copy.start()
    for i, mask_ref in enumerate(mask_refs):
        size = mask_rows(mask_ref.shape[0])
        row, column = (lax.broadcasted_iota(jnp.int32, (size, HEAD_DIM), axis) for axis in (0, 1))
        mask = jnp.zeros((size, HEAD_DIM), jnp.int32)
        for a in range(mask_ref.shape[0]):
            for b in range(mask_ref.shape[1]):
                mask = jnp.where((row == a) & (column == b), mask_ref[a, b], mask)
        mask = mask.astype(jnp.float32).astype(k_all.dtype)
        at = 2 * key_blocks * BLOCK + i * size
        for k in range(n_ka):
            out_refs[k // 2][k % 2, at : at + size] = mask
    for k in range(n_ka):
        for t in range(key_blocks):
            copies[k * key_blocks + t][1].wait()
            out_refs[k // 2][k % 2, (2 * t + 1) * BLOCK : (2 * t + 2) * BLOCK] = v_ref[k, t].T
    for pair in copies:
        pair[0].wait()


def pack(me, keys, values, masks, n_ka, heads, c):
    key_blocks = keys.shape[0] // BLOCK
    size = 2 * keys.shape[0] + sum(mask_rows(mask.shape[0]) for mask in masks)
    return pl.pallas_call(
        functools.partial(pack_kernel, n_ka, heads, c, len(masks)),
        out_shape=[jax.ShapeDtypeStruct((2, size, HEAD_DIM), keys.dtype)] * (n_ka // 2),
        in_specs=[SMEM] + [SMEM] * len(masks) + [ANY, ANY],
        out_specs=[VMEM] * (n_ka // 2),
        scratch_shapes=[
            pltpu.VMEM((n_ka, key_blocks, BLOCK, HEAD_DIM), values.dtype),
            pltpu.SemaphoreType.DMA((n_ka * key_blocks, 2)),
        ],
        compiler_params=params(MOST_VMEM_BYTES),
        cost_estimate=pl.CostEstimate(flops=0, bytes_accessed=keys.size, transcendentals=0),
        name=f"pack_{c}",
    )(me, *masks, keys, values)


def turn_kernel(heads, me_ref, q_all, *refs):
    out_ref, q_ref, sem = refs
    column = pl.multiple_of(me_ref[0] * heads * HEAD_DIM, HEAD_DIM)
    copy = pltpu.make_async_copy(q_all.at[:, pl.ds(column, heads * HEAD_DIM)], q_ref, sem)
    copy.start()
    copy.wait()
    for c in range(heads):
        for r in range(out_ref.shape[1]):
            out_ref[c, r] = q_ref[r * BLOCK : (r + 1) * BLOCK, c * HEAD_DIM : (c + 1) * HEAD_DIM].T


def turn(me, queries, heads):
    tokens = queries.shape[0]
    return pl.pallas_call(
        functools.partial(turn_kernel, heads),
        out_shape=jax.ShapeDtypeStruct((heads, tokens // BLOCK, HEAD_DIM, BLOCK), queries.dtype),
        in_specs=[SMEM, ANY],
        out_specs=VMEM,
        scratch_shapes=[pltpu.VMEM((tokens, heads * HEAD_DIM), queries.dtype), pltpu.SemaphoreType.DMA],
        compiler_params=params(MOST_VMEM_BYTES),
        cost_estimate=pl.CostEstimate(flops=0, bytes_accessed=queries.size // HEADS, transcendentals=0),
        name="turn",
    )(me, queries)


def plan_kernel(steps, n_pb, n_slots, key_blocks, rows, relay, pb_ref, *refs):
    mask_refs, count_ref, live_refs = refs[: -len(steps) - 1], refs[-len(steps) - 1], refs[-len(steps) :]
    pb = pb_ref[0]
    sign = 1 - 2 * (pb & 1)
    inner = ((pb > 0) & (pb < n_pb - 1)).astype(jnp.int32)
    helper = ((pb == 1) | (pb == n_pb - 2)).astype(jnp.int32)
    for step, (sources, live) in enumerate(zip(steps, live_refs)):
        total = jnp.int32(0)
        for guest, mask_ref in enumerate(mask_refs):

            def row_step(r, base, guest=guest, mask_ref=mask_ref):
                count = jnp.int32(0)
                for s, (delta, open_to_guests) in enumerate(sources):
                    if guest and not open_to_guests:
                        continue
                    j = pb + delta * sign
                    inside = ((j >= 0) & (j < n_pb)).astype(jnp.int32)
                    if relay and abs(delta) > 1:
                        inside = inside * inner
                    if guest:
                        inside = inside * helper
                    j = jnp.clip(j, 0, n_pb - 1)
                    for slot in range(n_slots):
                        for t in range(key_blocks):
                            block = (s * n_slots + slot) * key_blocks + t
                            live[2 * base + count] = ((r + guest * rows) << ROW_SHIFT) + block
                            column = j * key_blocks + t
                            count += inside * mask_ref[(slot * n_pb * key_blocks + column) * rows + r]
                live[2 * base + count] = -1
                return base + ((count + 1) >> 1)

            total = lax.fori_loop(0, rows, row_step, total)
        for u in range(GROUP):
            live[2 * (total + u)] = 0
            live[2 * (total + u) + 1] = -1
        count_ref[step] = total


def plan(pb, masks, steps, n_pb, n_slots, key_blocks, rows, relay):
    sizes = [len(masks) * rows * ((len(step) * n_slots * key_blocks + 2) // 2) + GROUP for step in steps]
    out_shape = [jax.ShapeDtypeStruct((len(steps),), jnp.int32)]
    out_shape += [jax.ShapeDtypeStruct((2 * size,), jnp.int32) for size in sizes]
    counts, *lives = pl.pallas_call(
        functools.partial(plan_kernel, steps, n_pb, n_slots, key_blocks, rows, relay),
        out_shape=out_shape,
        in_specs=[SMEM] * (1 + len(masks)),
        out_specs=[SMEM] * len(out_shape),
        compiler_params=params(),
        name="plan",
    )(pb, *masks)
    return [(counts, i, live) for i, live in enumerate(lives)]


def in_parts(x):
    found = []
    for _ in range(3):
        found.append(x.astype(jnp.bfloat16).astype(jnp.float32))
        x = x - found[-1]
    return found


def attend_kernel(c, n_src, entry, first, mode, guests, count_ref, live_ref, q_own, *refs):
    n_kv = n_src
    guest_ref, refs = (refs[0], refs[1:]) if guests else (None, refs)
    kv_refs, refs = refs[:n_kv], refs[n_kv:]
    state_in, refs = ((), refs) if first else (refs[:3], refs[3:])
    if mode == "last":
        (out_ref, kv, q_ref, *state, sems) = refs
    elif mode == "send":
        (*state, part_ref, kv, q_ref, sems) = refs
    else:
        (*state, kv, q_ref, sems) = refs
    m_ref, l_ref, acc_ref = state
    blocks = kv.shape[0] // n_src
    rows = q_own.shape[1]
    copies = [
        pltpu.make_async_copy(kv_refs[s], kv.at[pl.ds(s * blocks, blocks)], sems.at[s]) for s in range(n_src)
    ]
    copies += [pltpu.make_async_copy(a, b, sems.at[n_src + i]) for i, (a, b) in enumerate(zip(state_in, state))]
    copies.append(pltpu.make_async_copy(q_own.at[c], q_ref.at[pl.ds(0, rows)], sems.at[n_src + 3]))
    if guests:
        copies.append(pltpu.make_async_copy(guest_ref.at[c], q_ref.at[pl.ds(rows, rows)], sems.at[n_src + 4]))
    for copy in copies:
        copy.start()
    if first:
        m_ref[...] = jnp.full(m_ref.shape, NEG, jnp.float32)
        l_ref[...] = jnp.zeros(l_ref.shape, jnp.float32)
        acc_ref[...] = jnp.zeros(acc_ref.shape, jnp.float32)
    for copy in copies:
        copy.wait()
    total = count_ref[entry]
    nn = (((1,), (0,)), ((), ()))
    f32, bf16 = jnp.float32, jnp.bfloat16

    def group_step(g, _):
        found = []
        for u in range(GROUP):
            index = g * GROUP + u
            code0, code1 = live_ref[2 * index], live_ref[2 * index + 1]
            r = code0 >> ROW_SHIFT
            b0 = code0 & ((1 << ROW_SHIFT) - 1)
            b1 = jnp.maximum(code1, 0) & ((1 << ROW_SHIFT) - 1)
            x = lax.dot_general(jnp.concatenate([kv[b0, 0], kv[b1, 0]]), q_ref[r], nn, preferred_element_type=f32)
            x0 = jnp.where(index < total, x[:BLOCK], NEG)
            x1 = jnp.where(code1 >= 0, x[BLOCK:], NEG)
            top = jnp.max(jnp.maximum(x0, x1), axis=0, keepdims=True)
            w0 = jnp.exp2((x0 - top) * EXP2_SCALE)
            w1 = jnp.exp2((x1 - top) * EXP2_SCALE)
            total_w = jnp.sum(w0 + w1, axis=0, keepdims=True)
            w = jnp.concatenate([w0.astype(bf16), w1.astype(bf16)])
            v = jnp.concatenate([kv[b0, 1], kv[b1, 1]], axis=1)
            found.append((r, top, total_w, lax.dot_general(v, w, nn, preferred_element_type=f32)))
        for r, top, total_w, part in found:
            m = m_ref[r]
            m_new = jnp.maximum(m, top)
            alpha = jnp.exp2((m - m_new) * EXP2_SCALE)
            beta = jnp.exp2((top - m_new) * EXP2_SCALE)
            m_ref[r] = m_new
            l_ref[r] = l_ref[r] * alpha + total_w * beta
            acc_ref[r] = acc_ref[r] * alpha + part * beta
        return 0

    lax.fori_loop(0, (total + GROUP - 1) // GROUP, group_step, 0)
    if mode == "last":
        for r in range(rows):
            out_ref[r * BLOCK : (r + 1) * BLOCK, :] = (acc_ref[r] / l_ref[r]).T.astype(out_ref.dtype)
    if mode == "send":
        for r in range(rows):
            l = l_ref[rows + r]
            part_ref[r, :HEAD_DIM] = (acc_ref[rows + r] / jnp.where(l > 0, l, 1.0)).astype(part_ref.dtype)
            words = in_parts(m_ref[rows + r]) + in_parts(l)
            words.append(jnp.zeros((STAT_ROWS - len(words), BLOCK), f32))
            part_ref[r, HEAD_DIM:] = jnp.concatenate(words).astype(part_ref.dtype)


def attend(c, listed, q, guest, sources, state, mode, sets, name):
    counts, entry, live = listed
    rows, dtype = q.shape[1], q.dtype
    first = state is None
    state = () if first else tuple(state)
    stat = (sets * rows, 1, BLOCK)
    shapes = [stat, stat, (sets * rows, HEAD_DIM, BLOCK)]
    if mode == "last":
        out_shape = [jax.ShapeDtypeStruct((rows * BLOCK, HEAD_DIM), dtype)]
    else:
        out_shape = [jax.ShapeDtypeStruct(shape, jnp.float32) for shape in shapes]
    if mode == "send":
        out_shape.append(jax.ShapeDtypeStruct((rows, HEAD_DIM + STAT_ROWS, BLOCK), dtype))
    n_src = len(sources)
    blocks = sources[0].shape[0]
    guests = () if guest is None else (guest,)
    scratch = [pltpu.VMEM((n_src * blocks,) + sources[0].shape[1:], dtype)]
    scratch += [pltpu.VMEM(((1 + len(guests)) * rows, HEAD_DIM, BLOCK), dtype)]
    if mode == "last":
        scratch += [pltpu.VMEM(shape, jnp.float32) for shape in shapes]
    scratch.append(pltpu.SemaphoreType.DMA((n_src + 5,)))
    return pl.pallas_call(
        functools.partial(attend_kernel, c, n_src, entry, first, mode, bool(guests)),
        out_shape=out_shape,
        in_specs=[SMEM, SMEM, ANY] + [ANY] * (len(guests) + n_src + len(state)),
        out_specs=[VMEM] * len(out_shape),
        scratch_shapes=scratch,
        compiler_params=params(),
        cost_estimate=pl.CostEstimate(flops=0, bytes_accessed=HEAD_DIM * BLOCK, transcendentals=0),
        name=name,
    )(counts, live, q, *guests, *sources, *state)


def merge_kernel(outer_ref, m_ref, l_ref, acc_ref, part_ref, out_ref):
    outer = outer_ref[0] > 0
    for r in range(part_ref.shape[0]):
        m, l = m_ref[r], l_ref[r]
        words = part_ref[r, HEAD_DIM:].astype(jnp.float32)
        top = jnp.where(outer, words[0:1] + words[1:2] + words[2:3], NEG)
        extra = jnp.where(outer, words[3:4] + words[4:5] + words[5:6], 0.0)
        m_new = jnp.maximum(m, top)
        alpha = jnp.exp2((m - m_new) * EXP2_SCALE)
        beta = jnp.exp2((top - m_new) * EXP2_SCALE) * extra
        done = (acc_ref[r] * alpha + part_ref[r, :HEAD_DIM].astype(jnp.float32) * beta) / (l * alpha + beta)
        out_ref[r * BLOCK : (r + 1) * BLOCK, :] = done.T.astype(out_ref.dtype)


def merge(outer, state, part, name):
    rows = part.shape[0]
    half = lambda x: pl.BlockSpec((rows,) + x.shape[1:], lambda i: (0, 0, 0))
    return pl.pallas_call(
        merge_kernel,
        out_shape=jax.ShapeDtypeStruct((rows * BLOCK, HEAD_DIM), part.dtype),
        grid=(1,),
        in_specs=[SMEM] + [half(x) for x in state] + [VMEM],
        out_specs=VMEM,
        compiler_params=params(),
        name=name,
    )(outer, *state, part)


def place_kernel(n_ka, heads, me_ref, *refs):
    pieces, out_ref, sems = refs[: n_ka * heads], refs[-2], refs[-1]
    copies = []
    for k in range(n_ka):
        for c in range(heads):
            col = pl.multiple_of(((me_ref[0] ^ k) * heads + c) * HEAD_DIM, HEAD_DIM)
            copies.append(
                pltpu.make_async_copy(pieces[c * n_ka + k], out_ref.at[:, pl.ds(col, HEAD_DIM)], sems.at[c, k])
            )
    for copy in copies:
        copy.start()
    for copy in copies:
        copy.wait()


def place(me, pieces, n_ka, heads):
    rows = pieces[0].shape[0]
    return pl.pallas_call(
        functools.partial(place_kernel, n_ka, heads),
        out_shape=jax.ShapeDtypeStruct((rows, HEADS * HEAD_DIM), pieces[0].dtype),
        in_specs=[SMEM] + [ANY] * (n_ka * heads),
        out_specs=ANY,
        scratch_shapes=[pltpu.SemaphoreType.DMA((heads, n_ka))],
        compiler_params=params(),
        name="place",
    )(me, *pieces)


def local(n_pb, n_ka, queries, keys, values, block_mask):
    heads = HEADS // n_ka
    shard = keys.shape[0]
    key_blocks = shard // BLOCK
    rows = queries.shape[0] // BLOCK
    me = lax.axis_index("ka").astype(jnp.int32)
    pb = lax.axis_index("pb").astype(jnp.int32)
    me1, pb1 = me[None], pb[None]
    relay = n_pb >= 4 and n_pb % 2 == 0
    def swap(x, k):
        return lax.ppermute(x, "ka", [(i, i ^ k) for i in range(n_ka)])

    def hops(odd, step):
        found = []
        for low in range(odd, n_pb - 1, 2):
            found += [(low, low + 1)] if low - (step - 1) >= 0 else []
            found += [(low + 1, low)] if low + 1 + (step - 1) < n_pb else []
        if relay and step > 1:
            found = [(i, j) for i, j in found if 0 < j < n_pb - 1]
        return found

    def exchange(x, odd, step):
        found = hops(odd, step)
        return lax.ppermute(x, "pb", found) if found else None

    def relayed(arrived, step, before):
        even, odd = after(tuple(arrived), before)
        return [exchange(odd, 0, step), exchange(even, 1, step)]

    def inward(x):
        return lax.ppermute(x, "pb", [(0, 1), (n_pb - 1, n_pb - 2)])

    def outward(x):
        return lax.ppermute(x, "pb", [(1, 0), (n_pb - 2, n_pb - 1)])

    def sort(x, before=None):
        mixed = [y if i == 0 else swap(y, 2 * i) for i, y in enumerate(x)]
        mixed = after(mixed, before)
        theirs = swap(jnp.stack([y[1] for y in mixed]), 1)
        return jnp.concatenate([jnp.stack([y[0] for y in mixed]), theirs]), mixed

    def blocks(x):
        return x[:, : 2 * shard].reshape(n_ka * key_blocks, 2, BLOCK, HEAD_DIM)

    def after(arrays, done):
        return arrays if done is None else lax.optimization_barrier((arrays, done))[0]

    def flags(x):
        return x[:, : block_mask.shape[1], :rows].astype(jnp.int32).reshape(-1)

    steps = [((0, False),)]
    for step in range(1, n_pb):
        found = (((step, False),) if hops(0, step) else ()) + (((-step, True),) if hops(1, step) else ())
        if step == 1:
            steps[0] += found
        elif found:
            steps.append(found)
    last = len(steps) - 1
    parts = (block_mask.T,) + ((inward(block_mask.T),) if relay else ())
    owns, over, guest = [], [], None
    for c in range(heads):
        place_of = after(me1, (q, mixed)) if c else me1
        packed = pack(place_of, keys, values, parts if c == heads - 1 else (), n_ka, heads, c)
        if c == 0:
            q = turn(after(me1, packed), queries, heads)
            own, mixed = sort(packed, (q, parts))
        else:
            own, mixed = sort(after(packed, owns[0]), over[0])
        owns.append(blocks(own))
        if c == heads - 1:
            size = mask_rows(block_mask.shape[1])
            masks = [flags(own[:, 2 * shard + i * size :]) for i in range(len(parts))]
            lists = plan(pb1, masks, steps, n_pb, n_ka, key_blocks, rows, relay)
        before = ((second, guest, lists[0][0] if c == heads - 1 else None), over[0]) if c else (None, None)
        over.append([exchange(after(owns[c], before[odd]), odd, 1) for odd in (0, 1)])
        if c == 0:
            guest = inward(after(q, over[0])) if relay else None
            second = relayed(over[0], 2, over[0])
    state = [None] * heads

    def run(c, step, sources):
        kind = "keep" if step < last else "send" if relay else "last"
        sources = [x for x in sources if x is not None]
        name = f"attend_{c}_{step}"
        return attend(c, lists[step], q, guest, sources, state[c], kind, 2 if relay else 1, name)

    for step in range(last):
        for c in range(heads):
            sources = ([owns[c]] if step == 0 else []) + over[c]
            over[c] = relayed(over[c], step + 2, over[c]) if step or c else second
            state[c] = run(c, step, sources)

    pieces = []
    sent = far = None
    for c in range(heads):
        found = run(c, last, ([] if last else [owns[c]]) + after(over[c], sent))
        if relay:
            outer = ((pb == 0) | (pb == n_pb - 1)).astype(jnp.int32)[None]
            out = merge(outer, found[:3], outward(after(found[3], far)), f"merge_{c}")
        else:
            out = found[0]
        mine = [out] + [swap(out, k) for k in range(2, n_ka, 2)]
        sent, far = mine[: n_ka // 4 + 1], mine[n_ka // 4 + 1 :]
        others = [swap(x, 1) for x in mine]
        pieces += [x for two in zip(mine, others) for x in two]
    return place(me1, pieces, n_ka, heads)


def solution(mesh):
    n_pb, n_ka = mesh.shape["pb"], mesh.shape["ka"]
    return jax.shard_map(
        functools.partial(local, n_pb, n_ka),
        mesh=mesh,
        in_specs=(P("pb", None), P(("ka", "pb"), None), P(("ka", "pb"), None), P("pb", "ka")),
        out_specs=P("pb", None),
        check_vma=False,
    )
```

```python
import functools
import math

import jax
import jax.numpy as jnp
from jax import lax
from jax.experimental import pallas as pl
from jax.experimental.pallas import tpu as pltpu
from jax.sharding import PartitionSpec as P

HEADS = 16
HEAD_DIM = 128
BLOCK = 128
NEG = -1e30
EXP2_SCALE = math.log2(math.e) / math.sqrt(HEAD_DIM)
GROUP = 8
STAT_ROWS = 16
ROW_SHIFT = 16
VMEM_BYTES = 40 * 1024 * 1024
MOST_VMEM_BYTES = 60 * 1024 * 1024

VMEM = pl.BlockSpec(memory_space=pltpu.VMEM)
SMEM = pl.BlockSpec(memory_space=pltpu.SMEM)
ANY = pl.BlockSpec(memory_space=pl.ANY)


def params(size=VMEM_BYTES):
    return pltpu.CompilerParams(vmem_limit_bytes=size)


def pack_kernel(n_ka, heads, me_ref, *refs):
    k_all, v_all, *out_refs, v_ref, sems = refs
    key_blocks = k_all.shape[0] // BLOCK
    pieces = [(k, c, t) for k in range(n_ka) for c in range(heads) for t in range(key_blocks)]
    copies = []
    for i, (k, c, t) in enumerate(pieces):
        col = pl.multiple_of(((me_ref[0] ^ k) * heads + c) * HEAD_DIM, HEAD_DIM)
        rows, at = pl.ds(t * BLOCK, BLOCK), pl.ds(2 * t * BLOCK, BLOCK)
        to = out_refs[k // 2].at[c, k % 2, at]
        copies.append(
            (
                pltpu.make_async_copy(k_all.at[rows, pl.ds(col, HEAD_DIM)], to, sems.at[i, 0]),
                pltpu.make_async_copy(v_all.at[rows, pl.ds(col, HEAD_DIM)], v_ref.at[i], sems.at[i, 1]),
            )
        )
    for pair in copies:
        for copy in pair:
            copy.start()
    for i, (k, c, t) in enumerate(pieces):
        copies[i][1].wait()
        out_refs[k // 2][c, k % 2, (2 * t + 1) * BLOCK : (2 * t + 2) * BLOCK] = v_ref[i].T
    for pair in copies:
        pair[0].wait()


def pack(me, keys, values, n_ka, heads):
    count = n_ka * heads * (keys.shape[0] // BLOCK)
    shape = (heads, 2, 2 * keys.shape[0], HEAD_DIM)
    return pl.pallas_call(
        functools.partial(pack_kernel, n_ka, heads),
        out_shape=[jax.ShapeDtypeStruct(shape, keys.dtype)] * (n_ka // 2),
        in_specs=[SMEM, ANY, ANY],
        out_specs=[VMEM] * (n_ka // 2),
        scratch_shapes=[pltpu.VMEM((count, BLOCK, HEAD_DIM), values.dtype), pltpu.SemaphoreType.DMA((count, 2))],
        compiler_params=params(MOST_VMEM_BYTES),
        cost_estimate=pl.CostEstimate(flops=0, bytes_accessed=keys.size, transcendentals=0),
        name="pack",
    )(me, keys, values)


def turn_kernel(heads, me_ref, q_all, *refs):
    out_refs, (q_ref, sem) = refs[:heads], refs[heads:]
    column = pl.multiple_of(me_ref[0] * heads * HEAD_DIM, HEAD_DIM)
    copy = pltpu.make_async_copy(q_all.at[:, pl.ds(column, heads * HEAD_DIM)], q_ref, sem)
    copy.start()
    copy.wait()
    for c in range(heads):
        for r in range(out_refs[c].shape[0]):
            out_refs[c][r] = q_ref[r * BLOCK : (r + 1) * BLOCK, c * HEAD_DIM : (c + 1) * HEAD_DIM].T


def turn(me, queries, heads):
    tokens = queries.shape[0]
    return pl.pallas_call(
        functools.partial(turn_kernel, heads),
        out_shape=[jax.ShapeDtypeStruct((tokens // BLOCK, HEAD_DIM, BLOCK), queries.dtype)] * heads,
        in_specs=[SMEM, ANY],
        out_specs=[VMEM] * heads,
        scratch_shapes=[pltpu.VMEM((tokens, heads * HEAD_DIM), queries.dtype), pltpu.SemaphoreType.DMA],
        compiler_params=params(MOST_VMEM_BYTES),
        cost_estimate=pl.CostEstimate(flops=0, bytes_accessed=queries.size // HEADS, transcendentals=0),
        name="turn",
    )(me, queries)


def plan_kernel(steps, n_pb, n_slots, key_blocks, rows, relay, pb_ref, *refs):
    mask_refs, count_ref, live_refs = refs[: -len(steps) - 1], refs[-len(steps) - 1], refs[-len(steps) :]
    pb = pb_ref[0]
    sign = 1 - 2 * (pb & 1)
    inner = ((pb > 0) & (pb < n_pb - 1)).astype(jnp.int32)
    helper = ((pb == 1) | (pb == n_pb - 2)).astype(jnp.int32)
    for step, (sources, live) in enumerate(zip(steps, live_refs)):
        total = jnp.int32(0)
        for guest, mask_ref in enumerate(mask_refs):

            def row_step(r, base, guest=guest, mask_ref=mask_ref):
                count = jnp.int32(0)
                for s, (delta, open_to_guests) in enumerate(sources):
                    if guest and not open_to_guests:
                        continue
                    j = pb + delta * sign
                    inside = ((j >= 0) & (j < n_pb)).astype(jnp.int32)
                    if relay and abs(delta) > 1:
                        inside = inside * inner
                    if guest:
                        inside = inside * helper
                    j = jnp.clip(j, 0, n_pb - 1)
                    for slot in range(n_slots):
                        for t in range(key_blocks):
                            block = (s * n_slots + slot) * key_blocks + t
                            live[2 * base + count] = ((r + guest * rows) << ROW_SHIFT) + block
                            column = j * key_blocks + t
                            count += inside * mask_ref[(slot * n_pb * key_blocks + column) * rows + r]
                live[2 * base + count] = -1
                return base + ((count + 1) >> 1)

            total = lax.fori_loop(0, rows, row_step, total)
        for u in range(GROUP):
            live[2 * (total + u)] = 0
            live[2 * (total + u) + 1] = -1
        count_ref[step] = total


def plan(pb, masks, steps, n_pb, n_slots, key_blocks, rows, relay):
    sizes = [len(masks) * rows * ((len(step) * n_slots * key_blocks + 2) // 2) + GROUP for step in steps]
    out_shape = [jax.ShapeDtypeStruct((len(steps),), jnp.int32)]
    out_shape += [jax.ShapeDtypeStruct((2 * size,), jnp.int32) for size in sizes]
    counts, *lives = pl.pallas_call(
        functools.partial(plan_kernel, steps, n_pb, n_slots, key_blocks, rows, relay),
        out_shape=out_shape,
        in_specs=[SMEM] * (1 + len(masks)),
        out_specs=[SMEM] * len(out_shape),
        compiler_params=params(),
        name="plan",
    )(pb, *masks)
    return [(counts, i, live) for i, live in enumerate(lives)]


def in_parts(x):
    found = []
    for _ in range(3):
        found.append(x.astype(jnp.bfloat16).astype(jnp.float32))
        x = x - found[-1]
    return found


def attend_kernel(n_src, entry, first, mode, guests, count_ref, live_ref, q_own, *refs):
    n_kv = n_src
    guest_ref, refs = (refs[0], refs[1:]) if guests else (None, refs)
    kv_refs, refs = refs[:n_kv], refs[n_kv:]
    state_in, refs = ((), refs) if first else (refs[:3], refs[3:])
    if mode == "last":
        (out_ref, kv, q_ref, *state, sems) = refs
    elif mode == "send":
        (*state, part_ref, kv, q_ref, sems) = refs
    else:
        (*state, kv, q_ref, sems) = refs
    m_ref, l_ref, acc_ref = state
    blocks = kv.shape[0] // n_src
    rows = q_own.shape[0]
    copies = [
        pltpu.make_async_copy(kv_refs[s], kv.at[pl.ds(s * blocks, blocks)], sems.at[s]) for s in range(n_src)
    ]
    copies += [pltpu.make_async_copy(a, b, sems.at[n_src + i]) for i, (a, b) in enumerate(zip(state_in, state))]
    copies.append(pltpu.make_async_copy(q_own, q_ref.at[pl.ds(0, rows)], sems.at[n_src + 3]))
    if guests:
        copies.append(pltpu.make_async_copy(guest_ref, q_ref.at[pl.ds(rows, rows)], sems.at[n_src + 4]))
    for copy in copies:
        copy.start()
    if first:
        m_ref[...] = jnp.full(m_ref.shape, NEG, jnp.float32)
        l_ref[...] = jnp.zeros(l_ref.shape, jnp.float32)
        acc_ref[...] = jnp.zeros(acc_ref.shape, jnp.float32)
    for copy in copies:
        copy.wait()
    total = count_ref[entry]
    nn = (((1,), (0,)), ((), ()))
    f32, bf16 = jnp.float32, jnp.bfloat16

    def group_step(g, _):
        found = []
        for u in range(GROUP):
            index = g * GROUP + u
            code0, code1 = live_ref[2 * index], live_ref[2 * index + 1]
            r = code0 >> ROW_SHIFT
            b0 = code0 & ((1 << ROW_SHIFT) - 1)
            b1 = jnp.maximum(code1, 0) & ((1 << ROW_SHIFT) - 1)
            x = lax.dot_general(jnp.concatenate([kv[b0, 0], kv[b1, 0]]), q_ref[r], nn, preferred_element_type=f32)
            x0 = jnp.where(index < total, x[:BLOCK], NEG)
            x1 = jnp.where(code1 >= 0, x[BLOCK:], NEG)
            top = jnp.max(jnp.maximum(x0, x1), axis=0, keepdims=True)
            w0 = jnp.exp2((x0 - top) * EXP2_SCALE)
            w1 = jnp.exp2((x1 - top) * EXP2_SCALE)
            total_w = jnp.sum(w0 + w1, axis=0, keepdims=True)
            w = jnp.concatenate([w0.astype(bf16), w1.astype(bf16)])
            v = jnp.concatenate([kv[b0, 1], kv[b1, 1]], axis=1)
            found.append((r, top, total_w, lax.dot_general(v, w, nn, preferred_element_type=f32)))
        for r, top, total_w, part in found:
            m = m_ref[r]
            m_new = jnp.maximum(m, top)
            alpha = jnp.exp2((m - m_new) * EXP2_SCALE)
            beta = jnp.exp2((top - m_new) * EXP2_SCALE)
            m_ref[r] = m_new
            l_ref[r] = l_ref[r] * alpha + total_w * beta
            acc_ref[r] = acc_ref[r] * alpha + part * beta
        return 0

    lax.fori_loop(0, (total + GROUP - 1) // GROUP, group_step, 0)
    if mode == "last":
        for r in range(rows):
            out_ref[r * BLOCK : (r + 1) * BLOCK, :] = (acc_ref[r] / l_ref[r]).T.astype(out_ref.dtype)
    if mode == "send":
        for r in range(rows):
            l = l_ref[rows + r]
            part_ref[r, :HEAD_DIM] = (acc_ref[rows + r] / jnp.where(l > 0, l, 1.0)).astype(part_ref.dtype)
            words = in_parts(m_ref[rows + r]) + in_parts(l)
            words.append(jnp.zeros((STAT_ROWS - len(words), BLOCK), f32))
            part_ref[r, HEAD_DIM:] = jnp.concatenate(words).astype(part_ref.dtype)


def attend(listed, q, guest, sources, state, mode, sets, name):
    counts, entry, live = listed
    rows, dtype = q.shape[0], q.dtype
    first = state is None
    state = () if first else tuple(state)
    stat = (sets * rows, 1, BLOCK)
    shapes = [stat, stat, (sets * rows, HEAD_DIM, BLOCK)]
    if mode == "last":
        out_shape = [jax.ShapeDtypeStruct((rows * BLOCK, HEAD_DIM), dtype)]
    else:
        out_shape = [jax.ShapeDtypeStruct(shape, jnp.float32) for shape in shapes]
    if mode == "send":
        out_shape.append(jax.ShapeDtypeStruct((rows, HEAD_DIM + STAT_ROWS, BLOCK), dtype))
    n_src = len(sources)
    blocks = sources[0].shape[0]
    guests = () if guest is None else (guest,)
    scratch = [pltpu.VMEM((n_src * blocks,) + sources[0].shape[1:], dtype)]
    scratch += [pltpu.VMEM(((1 + len(guests)) * rows, HEAD_DIM, BLOCK), dtype)]
    if mode == "last":
        scratch += [pltpu.VMEM(shape, jnp.float32) for shape in shapes]
    scratch.append(pltpu.SemaphoreType.DMA((n_src + 5,)))
    return pl.pallas_call(
        functools.partial(attend_kernel, n_src, entry, first, mode, bool(guests)),
        out_shape=out_shape,
        in_specs=[SMEM, SMEM, ANY] + [ANY] * (len(guests) + n_src + len(state)),
        out_specs=[VMEM] * len(out_shape),
        scratch_shapes=scratch,
        compiler_params=params(),
        cost_estimate=pl.CostEstimate(flops=0, bytes_accessed=HEAD_DIM * BLOCK, transcendentals=0),
        name=name,
    )(counts, live, q, *guests, *sources, *state)


def merge_kernel(outer_ref, m_ref, l_ref, acc_ref, part_ref, out_ref):
    outer = outer_ref[0] > 0
    for r in range(part_ref.shape[0]):
        m, l = m_ref[r], l_ref[r]
        words = part_ref[r, HEAD_DIM:].astype(jnp.float32)
        top = jnp.where(outer, words[0:1] + words[1:2] + words[2:3], NEG)
        extra = jnp.where(outer, words[3:4] + words[4:5] + words[5:6], 0.0)
        m_new = jnp.maximum(m, top)
        alpha = jnp.exp2((m - m_new) * EXP2_SCALE)
        beta = jnp.exp2((top - m_new) * EXP2_SCALE) * extra
        done = (acc_ref[r] * alpha + part_ref[r, :HEAD_DIM].astype(jnp.float32) * beta) / (l * alpha + beta)
        out_ref[r * BLOCK : (r + 1) * BLOCK, :] = done.T.astype(out_ref.dtype)


def merge(outer, state, part, name):
    rows = part.shape[0]
    half = lambda x: pl.BlockSpec((rows,) + x.shape[1:], lambda i: (0, 0, 0))
    return pl.pallas_call(
        merge_kernel,
        out_shape=jax.ShapeDtypeStruct((rows * BLOCK, HEAD_DIM), part.dtype),
        grid=(1,),
        in_specs=[SMEM] + [half(x) for x in state] + [VMEM],
        out_specs=VMEM,
        compiler_params=params(),
        name=name,
    )(outer, *state, part)


def place_kernel(n_ka, heads, me_ref, *refs):
    pieces, out_ref, sems = refs[: n_ka * heads], refs[-2], refs[-1]
    copies = []
    for k in range(n_ka):
        for c in range(heads):
            col = pl.multiple_of(((me_ref[0] ^ k) * heads + c) * HEAD_DIM, HEAD_DIM)
            copies.append(
                pltpu.make_async_copy(pieces[c * n_ka + k], out_ref.at[:, pl.ds(col, HEAD_DIM)], sems.at[c, k])
            )
    for copy in copies:
        copy.start()
    for copy in copies:
        copy.wait()


def place(me, pieces, n_ka, heads):
    rows = pieces[0].shape[0]
    return pl.pallas_call(
        functools.partial(place_kernel, n_ka, heads),
        out_shape=jax.ShapeDtypeStruct((rows, HEADS * HEAD_DIM), pieces[0].dtype),
        in_specs=[SMEM] + [ANY] * (n_ka * heads),
        out_specs=ANY,
        scratch_shapes=[pltpu.SemaphoreType.DMA((heads, n_ka))],
        compiler_params=params(),
        name="place",
    )(me, *pieces)


def local(n_pb, n_ka, queries, keys, values, block_mask):
    heads = HEADS // n_ka
    shard = keys.shape[0]
    key_blocks = shard // BLOCK
    rows = queries.shape[0] // BLOCK
    me = lax.axis_index("ka").astype(jnp.int32)
    pb = lax.axis_index("pb").astype(jnp.int32)
    me1, pb1 = me[None], pb[None]
    relay = n_pb >= 4 and n_pb % 2 == 0
    def swap(x, k):
        return lax.ppermute(x, "ka", [(i, i ^ k) for i in range(n_ka)])

    def hops(odd, step):
        found = []
        for low in range(odd, n_pb - 1, 2):
            found += [(low, low + 1)] if low - (step - 1) >= 0 else []
            found += [(low + 1, low)] if low + 1 + (step - 1) < n_pb else []
        if relay and step > 1:
            found = [(i, j) for i, j in found if 0 < j < n_pb - 1]
        return found

    def exchange(x, odd, step):
        found = hops(odd, step)
        return lax.ppermute(x, "pb", found) if found else None

    def inward(x):
        return lax.ppermute(x, "pb", [(0, 1), (n_pb - 1, n_pb - 2)])

    def outward(x):
        return lax.ppermute(x, "pb", [(1, 0), (n_pb - 2, n_pb - 1)])

    def sort(x, before):
        mixed = after([y if i == 0 else swap(y, 2 * i) for i, y in enumerate(x)], before)
        theirs = swap(jnp.stack([y[:, 1] for y in mixed], axis=1), 1)
        found = [jnp.concatenate([jnp.stack([y[c, 0] for y in mixed]), theirs[c]]) for c in range(heads)]
        return [y.reshape(n_ka * key_blocks, 2, BLOCK, HEAD_DIM) for y in found]

    def after(arrays, done):
        return arrays if done is None else lax.optimization_barrier((arrays, done))[0]

    packed = pack(me1, keys, values, n_ka, heads)
    q = turn(after(me1, packed), queries, heads)
    owns = sort(packed, q)
    over = [[exchange(own, odd, 1) for odd in (0, 1)] for own in owns]

    marks = jnp.stack([block_mask.T] + ([inward(block_mask.T)] if relay else []))[None]
    bit = 1
    while bit < n_ka:
        marks = jnp.concatenate([marks, swap(marks, bit)])
        bit *= 2
    marks = marks.reshape((n_ka // 2, 2) + marks.shape[1:]).swapaxes(0, 1).reshape(marks.shape)
    masks = [marks[:, i].reshape(-1) for i in range(marks.shape[1])]
    guest = [inward(after(x, over[0])) if relay else None for x in q]

    steps = [((0, False),)]
    for step in range(1, n_pb):
        found = (((step, False),) if hops(0, step) else ()) + (((-step, True),) if hops(1, step) else ())
        if step == 1:
            steps[0] += found
        elif found:
            steps.append(found)
    last = len(steps) - 1
    lists = plan(pb1, masks, steps, n_pb, n_ka, key_blocks, rows, relay)
    state = [None] * heads

    def run(c, step, sources):
        kind = "keep" if step < last else "send" if relay else "last"
        sources = [x for x in sources if x is not None]
        name = f"attend_{c}_{step}"
        return attend(lists[step], q[c], guest[c], sources, state[c], kind, 2 if relay else 1, name)

    for step in range(last):
        for c in range(heads):
            sources = ([owns[c]] if step == 0 else []) + over[c]
            even, odd = after(tuple(over[c]), over[c]) if step else after(tuple(over[c]), lists[0][0])
            over[c] = [exchange(odd, 0, step + 2), exchange(even, 1, step + 2)]
            state[c] = run(c, step, sources)

    pieces = []
    sent = far = None
    for c in range(heads):
        found = run(c, last, ([] if last else [owns[c]]) + after(over[c], sent))
        if relay:
            outer = ((pb == 0) | (pb == n_pb - 1)).astype(jnp.int32)[None]
            out = merge(outer, found[:3], outward(after(found[3], far)), f"merge_{c}")
        else:
            out = found[0]
        mine = [out] + [swap(out, k) for k in range(2, n_ka, 2)]
        sent, far = mine[: n_ka // 4 + 1], mine[n_ka // 4 + 1 :]
        others = [swap(x, 1) for x in mine]
        pieces += [x for two in zip(mine, others) for x in two]
    return place(me1, pieces, n_ka, heads)


def solution(mesh):
    n_pb, n_ka = mesh.shape["pb"], mesh.shape["ka"]
    return jax.shard_map(
        functools.partial(local, n_pb, n_ka),
        mesh=mesh,
        in_specs=(P("pb", None), P(("ka", "pb"), None), P(("ka", "pb"), None), P("pb", "ka")),
        out_specs=P("pb", None),
        check_vma=False,
    )
```

```python
import functools
import math

import jax
import jax.numpy as jnp
from jax import lax
from jax.experimental import pallas as pl
from jax.experimental.pallas import tpu as pltpu
from jax.sharding import PartitionSpec as P

HEADS = 16
HEAD_DIM = 128
BLOCK = 128
NEG = -1e30
EXP2_SCALE = math.log2(math.e) / math.sqrt(HEAD_DIM)
GROUP = 8
STAT_ROWS = 16
ROW_SHIFT = 16
VMEM_BYTES = 40 * 1024 * 1024
MOST_VMEM_BYTES = 60 * 1024 * 1024

VMEM = pl.BlockSpec(memory_space=pltpu.VMEM)
SMEM = pl.BlockSpec(memory_space=pltpu.SMEM)
ANY = pl.BlockSpec(memory_space=pl.ANY)


def params(size=VMEM_BYTES):
    return pltpu.CompilerParams(vmem_limit_bytes=size)


def mask_rows(rows):
    return -(-rows // 16) * 16


def pack_kernel(n_ka, heads, c, n_masks, me_ref, *refs):
    mask_refs, refs = refs[:n_masks], refs[n_masks:]
    k_all, v_all, *out_refs, v_ref, sems = refs
    key_blocks = k_all.shape[0] // BLOCK
    copies = []
    for k in range(n_ka):
        out_ref = out_refs[k // 2]
        col = pl.multiple_of(((me_ref[0] ^ k) * heads + c) * HEAD_DIM, HEAD_DIM)
        for t in range(key_blocks):
            rows, at = pl.ds(t * BLOCK, BLOCK), pl.ds(2 * t * BLOCK, BLOCK)
            sem = sems.at[k * key_blocks + t]
            copies.append(
                (
                    pltpu.make_async_copy(k_all.at[rows, pl.ds(col, HEAD_DIM)], out_ref.at[k % 2, at], sem.at[0]),
                    pltpu.make_async_copy(v_all.at[rows, pl.ds(col, HEAD_DIM)], v_ref.at[k, t], sem.at[1]),
                )
            )
    for pair in copies:
        for copy in pair:
            copy.start()
    for i, mask_ref in enumerate(mask_refs):
        size = mask_rows(mask_ref.shape[0])
        row, column = (lax.broadcasted_iota(jnp.int32, (size, HEAD_DIM), axis) for axis in (0, 1))
        mask = jnp.zeros((size, HEAD_DIM), jnp.int32)
        for a in range(mask_ref.shape[0]):
            for b in range(mask_ref.shape[1]):
                mask = jnp.where((row == a) & (column == b), mask_ref[a, b], mask)
        mask = mask.astype(jnp.float32).astype(k_all.dtype)
        at = 2 * key_blocks * BLOCK + i * size
        for k in range(n_ka):
            out_refs[k // 2][k % 2, at : at + size] = mask
    for k in range(n_ka):
        for t in range(key_blocks):
            copies[k * key_blocks + t][1].wait()
            out_refs[k // 2][k % 2, (2 * t + 1) * BLOCK : (2 * t + 2) * BLOCK] = v_ref[k, t].T
    for pair in copies:
        pair[0].wait()


def pack(me, keys, values, masks, n_ka, heads, c):
    key_blocks = keys.shape[0] // BLOCK
    size = 2 * keys.shape[0] + sum(mask_rows(mask.shape[0]) for mask in masks)
    return pl.pallas_call(
        functools.partial(pack_kernel, n_ka, heads, c, len(masks)),
        out_shape=[jax.ShapeDtypeStruct((2, size, HEAD_DIM), keys.dtype)] * (n_ka // 2),
        in_specs=[SMEM] + [SMEM] * len(masks) + [ANY, ANY],
        out_specs=[VMEM] * (n_ka // 2),
        scratch_shapes=[
            pltpu.VMEM((n_ka, key_blocks, BLOCK, HEAD_DIM), values.dtype),
            pltpu.SemaphoreType.DMA((n_ka * key_blocks, 2)),
        ],
        compiler_params=params(MOST_VMEM_BYTES),
        cost_estimate=pl.CostEstimate(flops=0, bytes_accessed=keys.size, transcendentals=0),
        name=f"pack_{c}",
    )(me, *masks, keys, values)


def turn_kernel(heads, me_ref, q_all, *refs):
    out_refs, (q_ref, sem) = refs[:heads], refs[heads:]
    column = pl.multiple_of(me_ref[0] * heads * HEAD_DIM, HEAD_DIM)
    copy = pltpu.make_async_copy(q_all.at[:, pl.ds(column, heads * HEAD_DIM)], q_ref, sem)
    copy.start()
    copy.wait()
    for c in range(heads):
        for r in range(out_refs[c].shape[0]):
            out_refs[c][r] = q_ref[r * BLOCK : (r + 1) * BLOCK, c * HEAD_DIM : (c + 1) * HEAD_DIM].T


def turn(me, queries, heads):
    tokens = queries.shape[0]
    return pl.pallas_call(
        functools.partial(turn_kernel, heads),
        out_shape=[jax.ShapeDtypeStruct((tokens // BLOCK, HEAD_DIM, BLOCK), queries.dtype)] * heads,
        in_specs=[SMEM, ANY],
        out_specs=[VMEM] * heads,
        scratch_shapes=[pltpu.VMEM((tokens, heads * HEAD_DIM), queries.dtype), pltpu.SemaphoreType.DMA],
        compiler_params=params(MOST_VMEM_BYTES),
        cost_estimate=pl.CostEstimate(flops=0, bytes_accessed=queries.size // HEADS, transcendentals=0),
        name="turn",
    )(me, queries)


def plan_kernel(steps, n_pb, n_slots, key_blocks, rows, relay, pb_ref, *refs):
    mask_refs, count_ref, live_refs = refs[: -len(steps) - 1], refs[-len(steps) - 1], refs[-len(steps) :]
    pb = pb_ref[0]
    sign = 1 - 2 * (pb & 1)
    inner = ((pb > 0) & (pb < n_pb - 1)).astype(jnp.int32)
    helper = ((pb == 1) | (pb == n_pb - 2)).astype(jnp.int32)
    for step, (sources, live) in enumerate(zip(steps, live_refs)):
        total = jnp.int32(0)
        for guest, mask_ref in enumerate(mask_refs):

            def row_step(r, base, guest=guest, mask_ref=mask_ref):
                count = jnp.int32(0)
                for s, (delta, open_to_guests) in enumerate(sources):
                    if guest and not open_to_guests:
                        continue
                    j = pb + delta * sign
                    inside = ((j >= 0) & (j < n_pb)).astype(jnp.int32)
                    if relay and abs(delta) > 1:
                        inside = inside * inner
                    if guest:
                        inside = inside * helper
                    j = jnp.clip(j, 0, n_pb - 1)
                    for slot in range(n_slots):
                        for t in range(key_blocks):
                            block = (s * n_slots + slot) * key_blocks + t
                            live[2 * base + count] = ((r + guest * rows) << ROW_SHIFT) + block
                            column = j * key_blocks + t
                            count += inside * mask_ref[(slot * n_pb * key_blocks + column) * rows + r]
                live[2 * base + count] = -1
                return base + ((count + 1) >> 1)

            total = lax.fori_loop(0, rows, row_step, total)
        for u in range(GROUP):
            live[2 * (total + u)] = 0
            live[2 * (total + u) + 1] = -1
        count_ref[step] = total


def plan(pb, masks, steps, n_pb, n_slots, key_blocks, rows, relay):
    sizes = [len(masks) * rows * ((len(step) * n_slots * key_blocks + 2) // 2) + GROUP for step in steps]
    out_shape = [jax.ShapeDtypeStruct((len(steps),), jnp.int32)]
    out_shape += [jax.ShapeDtypeStruct((2 * size,), jnp.int32) for size in sizes]
    counts, *lives = pl.pallas_call(
        functools.partial(plan_kernel, steps, n_pb, n_slots, key_blocks, rows, relay),
        out_shape=out_shape,
        in_specs=[SMEM] * (1 + len(masks)),
        out_specs=[SMEM] * len(out_shape),
        compiler_params=params(),
        name="plan",
    )(pb, *masks)
    return [(counts, i, live) for i, live in enumerate(lives)]


def in_parts(x):
    found = []
    for _ in range(3):
        found.append(x.astype(jnp.bfloat16).astype(jnp.float32))
        x = x - found[-1]
    return found


def attend_kernel(n_src, entry, first, mode, guests, count_ref, live_ref, q_own, *refs):
    n_kv = n_src
    guest_ref, refs = (refs[0], refs[1:]) if guests else (None, refs)
    kv_refs, refs = refs[:n_kv], refs[n_kv:]
    state_in, refs = ((), refs) if first else (refs[:3], refs[3:])
    if mode == "last":
        (out_ref, kv, q_ref, *state, sems) = refs
    elif mode == "send":
        (*state, part_ref, kv, q_ref, sems) = refs
    else:
        (*state, kv, q_ref, sems) = refs
    m_ref, l_ref, acc_ref = state
    blocks = kv.shape[0] // n_src
    rows = q_own.shape[0]
    copies = [
        pltpu.make_async_copy(kv_refs[s], kv.at[pl.ds(s * blocks, blocks)], sems.at[s]) for s in range(n_src)
    ]
    copies += [pltpu.make_async_copy(a, b, sems.at[n_src + i]) for i, (a, b) in enumerate(zip(state_in, state))]
    copies.append(pltpu.make_async_copy(q_own, q_ref.at[pl.ds(0, rows)], sems.at[n_src + 3]))
    if guests:
        copies.append(pltpu.make_async_copy(guest_ref, q_ref.at[pl.ds(rows, rows)], sems.at[n_src + 4]))
    for copy in copies:
        copy.start()
    if first:
        m_ref[...] = jnp.full(m_ref.shape, NEG, jnp.float32)
        l_ref[...] = jnp.zeros(l_ref.shape, jnp.float32)
        acc_ref[...] = jnp.zeros(acc_ref.shape, jnp.float32)
    for copy in copies:
        copy.wait()
    total = count_ref[entry]
    nn = (((1,), (0,)), ((), ()))
    f32, bf16 = jnp.float32, jnp.bfloat16

    def group_step(g, _):
        found = []
        for u in range(GROUP):
            index = g * GROUP + u
            code0, code1 = live_ref[2 * index], live_ref[2 * index + 1]
            r = code0 >> ROW_SHIFT
            b0 = code0 & ((1 << ROW_SHIFT) - 1)
            b1 = jnp.maximum(code1, 0) & ((1 << ROW_SHIFT) - 1)
            x = lax.dot_general(jnp.concatenate([kv[b0, 0], kv[b1, 0]]), q_ref[r], nn, preferred_element_type=f32)
            x0 = jnp.where(index < total, x[:BLOCK], NEG)
            x1 = jnp.where(code1 >= 0, x[BLOCK:], NEG)
            top = jnp.max(jnp.maximum(x0, x1), axis=0, keepdims=True)
            w0 = jnp.exp2((x0 - top) * EXP2_SCALE)
            w1 = jnp.exp2((x1 - top) * EXP2_SCALE)
            total_w = jnp.sum(w0 + w1, axis=0, keepdims=True)
            w = jnp.concatenate([w0.astype(bf16), w1.astype(bf16)])
            v = jnp.concatenate([kv[b0, 1], kv[b1, 1]], axis=1)
            found.append((r, top, total_w, lax.dot_general(v, w, nn, preferred_element_type=f32)))
        for r, top, total_w, part in found:
            m = m_ref[r]
            m_new = jnp.maximum(m, top)
            alpha = jnp.exp2((m - m_new) * EXP2_SCALE)
            beta = jnp.exp2((top - m_new) * EXP2_SCALE)
            m_ref[r] = m_new
            l_ref[r] = l_ref[r] * alpha + total_w * beta
            acc_ref[r] = acc_ref[r] * alpha + part * beta
        return 0

    lax.fori_loop(0, (total + GROUP - 1) // GROUP, group_step, 0)
    if mode == "last":
        for r in range(rows):
            out_ref[r * BLOCK : (r + 1) * BLOCK, :] = (acc_ref[r] / l_ref[r]).T.astype(out_ref.dtype)
    if mode == "send":
        for r in range(rows):
            l = l_ref[rows + r]
            part_ref[r, :HEAD_DIM] = (acc_ref[rows + r] / jnp.where(l > 0, l, 1.0)).astype(part_ref.dtype)
            words = in_parts(m_ref[rows + r]) + in_parts(l)
            words.append(jnp.zeros((STAT_ROWS - len(words), BLOCK), f32))
            part_ref[r, HEAD_DIM:] = jnp.concatenate(words).astype(part_ref.dtype)


def attend(listed, q, guest, sources, state, mode, sets, name):
    counts, entry, live = listed
    rows, dtype = q.shape[0], q.dtype
    first = state is None
    state = () if first else tuple(state)
    stat = (sets * rows, 1, BLOCK)
    shapes = [stat, stat, (sets * rows, HEAD_DIM, BLOCK)]
    if mode == "last":
        out_shape = [jax.ShapeDtypeStruct((rows * BLOCK, HEAD_DIM), dtype)]
    else:
        out_shape = [jax.ShapeDtypeStruct(shape, jnp.float32) for shape in shapes]
    if mode == "send":
        out_shape.append(jax.ShapeDtypeStruct((rows, HEAD_DIM + STAT_ROWS, BLOCK), dtype))
    n_src = len(sources)
    blocks = sources[0].shape[0]
    guests = () if guest is None else (guest,)
    scratch = [pltpu.VMEM((n_src * blocks,) + sources[0].shape[1:], dtype)]
    scratch += [pltpu.VMEM(((1 + len(guests)) * rows, HEAD_DIM, BLOCK), dtype)]
    if mode == "last":
        scratch += [pltpu.VMEM(shape, jnp.float32) for shape in shapes]
    scratch.append(pltpu.SemaphoreType.DMA((n_src + 5,)))
    return pl.pallas_call(
        functools.partial(attend_kernel, n_src, entry, first, mode, bool(guests)),
        out_shape=out_shape,
        in_specs=[SMEM, SMEM, ANY] + [ANY] * (len(guests) + n_src + len(state)),
        out_specs=[VMEM] * len(out_shape),
        scratch_shapes=scratch,
        compiler_params=params(),
        cost_estimate=pl.CostEstimate(flops=0, bytes_accessed=HEAD_DIM * BLOCK, transcendentals=0),
        name=name,
    )(counts, live, q, *guests, *sources, *state)


def merge_kernel(outer_ref, m_ref, l_ref, acc_ref, part_ref, out_ref):
    outer = outer_ref[0] > 0
    for r in range(part_ref.shape[0]):
        m, l = m_ref[r], l_ref[r]
        words = part_ref[r, HEAD_DIM:].astype(jnp.float32)
        top = jnp.where(outer, words[0:1] + words[1:2] + words[2:3], NEG)
        extra = jnp.where(outer, words[3:4] + words[4:5] + words[5:6], 0.0)
        m_new = jnp.maximum(m, top)
        alpha = jnp.exp2((m - m_new) * EXP2_SCALE)
        beta = jnp.exp2((top - m_new) * EXP2_SCALE) * extra
        done = (acc_ref[r] * alpha + part_ref[r, :HEAD_DIM].astype(jnp.float32) * beta) / (l * alpha + beta)
        out_ref[r * BLOCK : (r + 1) * BLOCK, :] = done.T.astype(out_ref.dtype)


def merge(outer, state, part, name):
    rows = part.shape[0]
    half = lambda x: pl.BlockSpec((rows,) + x.shape[1:], lambda i: (0, 0, 0))
    return pl.pallas_call(
        merge_kernel,
        out_shape=jax.ShapeDtypeStruct((rows * BLOCK, HEAD_DIM), part.dtype),
        grid=(1,),
        in_specs=[SMEM] + [half(x) for x in state] + [VMEM],
        out_specs=VMEM,
        compiler_params=params(),
        name=name,
    )(outer, *state, part)


def place_kernel(n_ka, heads, me_ref, *refs):
    pieces, out_ref, sems = refs[: n_ka * heads], refs[-2], refs[-1]
    copies = []
    for k in range(n_ka):
        for c in range(heads):
            col = pl.multiple_of(((me_ref[0] ^ k) * heads + c) * HEAD_DIM, HEAD_DIM)
            copies.append(
                pltpu.make_async_copy(pieces[c * n_ka + k], out_ref.at[:, pl.ds(col, HEAD_DIM)], sems.at[c, k])
            )
    for copy in copies:
        copy.start()
    for copy in copies:
        copy.wait()


def place(me, pieces, n_ka, heads):
    rows = pieces[0].shape[0]
    return pl.pallas_call(
        functools.partial(place_kernel, n_ka, heads),
        out_shape=jax.ShapeDtypeStruct((rows, HEADS * HEAD_DIM), pieces[0].dtype),
        in_specs=[SMEM] + [ANY] * (n_ka * heads),
        out_specs=ANY,
        scratch_shapes=[pltpu.SemaphoreType.DMA((heads, n_ka))],
        compiler_params=params(),
        name="place",
    )(me, *pieces)


def local(n_pb, n_ka, queries, keys, values, block_mask):
    heads = HEADS // n_ka
    shard = keys.shape[0]
    key_blocks = shard // BLOCK
    rows = queries.shape[0] // BLOCK
    me = lax.axis_index("ka").astype(jnp.int32)
    pb = lax.axis_index("pb").astype(jnp.int32)
    me1, pb1 = me[None], pb[None]
    relay = n_pb >= 4 and n_pb % 2 == 0
    def swap(x, k):
        return lax.ppermute(x, "ka", [(i, i ^ k) for i in range(n_ka)])

    def hops(odd, step):
        found = []
        for low in range(odd, n_pb - 1, 2):
            found += [(low, low + 1)] if low - (step - 1) >= 0 else []
            found += [(low + 1, low)] if low + 1 + (step - 1) < n_pb else []
        if relay and step > 1:
            found = [(i, j) for i, j in found if 0 < j < n_pb - 1]
        return found

    def exchange(x, odd, step):
        found = hops(odd, step)
        return lax.ppermute(x, "pb", found) if found else None

    def inward(x):
        return lax.ppermute(x, "pb", [(0, 1), (n_pb - 1, n_pb - 2)])

    def outward(x):
        return lax.ppermute(x, "pb", [(1, 0), (n_pb - 2, n_pb - 1)])

    def sort(x, before=None):
        mixed = [y if i == 0 else swap(y, 2 * i) for i, y in enumerate(x)]
        mixed = after(mixed, before)
        theirs = swap(jnp.stack([y[1] for y in mixed]), 1)
        return jnp.concatenate([jnp.stack([y[0] for y in mixed]), theirs]), mixed

    def blocks(x):
        return x[:, : 2 * shard].reshape(n_ka * key_blocks, 2, BLOCK, HEAD_DIM)

    def after(arrays, done):
        return arrays if done is None else lax.optimization_barrier((arrays, done))[0]

    def flags(x):
        return x[:, : block_mask.shape[1], :rows].astype(jnp.int32).reshape(-1)

    parts = (block_mask.T,) + ((inward(block_mask.T),) if relay else ())
    owns, over, guest = [], [], [None] * heads
    for c in range(heads):
        place_of = after(me1, (q, mixed)) if c else me1
        packed = pack(place_of, keys, values, parts if c == heads - 1 else (), n_ka, heads, c)
        if c == 0:
            q = turn(after(me1, packed), queries, heads)
            own, mixed = sort(packed, (q, parts))
        else:
            own, mixed = sort(after(packed, owns[0]), over[0])
        owns.append(blocks(own))
        before = ((over[0], guest[0]), over[0]) if c else (None, None)
        over.append([exchange(after(owns[c], before[odd]), odd, 1) for odd in (0, 1)])
        if relay:
            guest[c] = inward(after(q[c], over[0]))
    size = mask_rows(block_mask.shape[1])
    masks = [flags(own[:, 2 * shard + i * size :]) for i in range(len(parts))]

    steps = [((0, False),)]
    for step in range(1, n_pb):
        found = (((step, False),) if hops(0, step) else ()) + (((-step, True),) if hops(1, step) else ())
        if step == 1:
            steps[0] += found
        elif found:
            steps.append(found)
    last = len(steps) - 1
    lists = plan(pb1, masks, steps, n_pb, n_ka, key_blocks, rows, relay)
    state = [None] * heads

    def run(c, step, sources):
        kind = "keep" if step < last else "send" if relay else "last"
        sources = [x for x in sources if x is not None]
        name = f"attend_{c}_{step}"
        return attend(lists[step], q[c], guest[c], sources, state[c], kind, 2 if relay else 1, name)

    for step in range(last):
        for c in range(heads):
            sources = ([owns[c]] if step == 0 else []) + over[c]
            even, odd = over[c]
            if even is not None and odd is not None:
                even, odd = after((even, odd), (even, odd))
            over[c] = [exchange(odd, 0, step + 2), exchange(even, 1, step + 2)]
            state[c] = run(c, step, sources)

    pieces = []
    sent = None
    for c in range(heads):
        found = run(c, last, ([] if last else [owns[c]]) + over[c])
        if relay:
            outer = ((pb == 0) | (pb == n_pb - 1)).astype(jnp.int32)[None]
            out = merge(outer, found[:3], outward(after(found[3], sent)), f"merge_{c}")
        else:
            out = found[0]
        mine = [out] + [swap(out, k) for k in range(2, n_ka, 2)]
        sent = mine[: n_ka // 4 + 1]
        others = [swap(x, 1) for x in mine]
        pieces += [x for two in zip(mine, others) for x in two]
    return place(me1, pieces, n_ka, heads)


def solution(mesh):
    n_pb, n_ka = mesh.shape["pb"], mesh.shape["ka"]
    return jax.shard_map(
        functools.partial(local, n_pb, n_ka),
        mesh=mesh,
        in_specs=(P("pb", None), P(("ka", "pb"), None), P(("ka", "pb"), None), P("pb", "ka")),
        out_specs=P("pb", None),
        check_vma=False,
    )
```

```python
import functools
import math

import jax
import jax.numpy as jnp
from jax import lax
from jax.experimental import pallas as pl
from jax.experimental.pallas import tpu as pltpu
from jax.sharding import PartitionSpec as P

HEADS = 16
HEAD_DIM = 128
BLOCK = 128
NEG = -1e30
EXP2_SCALE = math.log2(math.e) / math.sqrt(HEAD_DIM)
GROUP = 8
STAT_ROWS = 16
ROW_SHIFT = 16
VMEM_BYTES = 40 * 1024 * 1024
MOST_VMEM_BYTES = 60 * 1024 * 1024

VMEM = pl.BlockSpec(memory_space=pltpu.VMEM)
SMEM = pl.BlockSpec(memory_space=pltpu.SMEM)
ANY = pl.BlockSpec(memory_space=pl.ANY)


def params(size=VMEM_BYTES):
    return pltpu.CompilerParams(vmem_limit_bytes=size)


def mask_rows(rows):
    return -(-rows // 16) * 16


def pack_kernel(n_ka, heads, c, n_masks, me_ref, *refs):
    mask_refs, refs = refs[:n_masks], refs[n_masks:]
    k_all, v_all, *out_refs, v_ref, sems = refs
    key_blocks = k_all.shape[0] // BLOCK
    copies = []
    for k in range(n_ka):
        out_ref = out_refs[k // 2]
        col = pl.multiple_of(((me_ref[0] ^ k) * heads + c) * HEAD_DIM, HEAD_DIM)
        for t in range(key_blocks):
            rows, at = pl.ds(t * BLOCK, BLOCK), pl.ds(2 * t * BLOCK, BLOCK)
            sem = sems.at[k * key_blocks + t]
            copies.append(
                (
                    pltpu.make_async_copy(k_all.at[rows, pl.ds(col, HEAD_DIM)], out_ref.at[k % 2, at], sem.at[0]),
                    pltpu.make_async_copy(v_all.at[rows, pl.ds(col, HEAD_DIM)], v_ref.at[k, t], sem.at[1]),
                )
            )
    for pair in copies:
        for copy in pair:
            copy.start()
    for i, mask_ref in enumerate(mask_refs):
        size = mask_rows(mask_ref.shape[0])
        row, column = (lax.broadcasted_iota(jnp.int32, (size, HEAD_DIM), axis) for axis in (0, 1))
        mask = jnp.zeros((size, HEAD_DIM), jnp.int32)
        for a in range(mask_ref.shape[0]):
            for b in range(mask_ref.shape[1]):
                mask = jnp.where((row == a) & (column == b), mask_ref[a, b], mask)
        mask = mask.astype(jnp.float32).astype(k_all.dtype)
        at = 2 * key_blocks * BLOCK + i * size
        for k in range(n_ka):
            out_refs[k // 2][k % 2, at : at + size] = mask
    for k in range(n_ka):
        for t in range(key_blocks):
            copies[k * key_blocks + t][1].wait()
            out_refs[k // 2][k % 2, (2 * t + 1) * BLOCK : (2 * t + 2) * BLOCK] = v_ref[k, t].T
    for pair in copies:
        pair[0].wait()


def pack(me, keys, values, masks, n_ka, heads, c):
    key_blocks = keys.shape[0] // BLOCK
    size = 2 * keys.shape[0] + sum(mask_rows(mask.shape[0]) for mask in masks)
    return pl.pallas_call(
        functools.partial(pack_kernel, n_ka, heads, c, len(masks)),
        out_shape=[jax.ShapeDtypeStruct((2, size, HEAD_DIM), keys.dtype)] * (n_ka // 2),
        in_specs=[SMEM] + [SMEM] * len(masks) + [ANY, ANY],
        out_specs=[VMEM] * (n_ka // 2),
        scratch_shapes=[
            pltpu.VMEM((n_ka, key_blocks, BLOCK, HEAD_DIM), values.dtype),
            pltpu.SemaphoreType.DMA((n_ka * key_blocks, 2)),
        ],
        compiler_params=params(MOST_VMEM_BYTES),
        cost_estimate=pl.CostEstimate(flops=0, bytes_accessed=keys.size, transcendentals=0),
        name=f"pack_{c}",
    )(me, *masks, keys, values)


def turn_kernel(heads, me_ref, q_all, *refs):
    out_refs, (q_ref, sem) = refs[:heads], refs[heads:]
    column = pl.multiple_of(me_ref[0] * heads * HEAD_DIM, HEAD_DIM)
    copy = pltpu.make_async_copy(q_all.at[:, pl.ds(column, heads * HEAD_DIM)], q_ref, sem)
    copy.start()
    copy.wait()
    for c in range(heads):
        for r in range(out_refs[c].shape[0]):
            out_refs[c][r] = q_ref[r * BLOCK : (r + 1) * BLOCK, c * HEAD_DIM : (c + 1) * HEAD_DIM].T


def turn(me, queries, heads):
    tokens = queries.shape[0]
    return pl.pallas_call(
        functools.partial(turn_kernel, heads),
        out_shape=[jax.ShapeDtypeStruct((tokens // BLOCK, HEAD_DIM, BLOCK), queries.dtype)] * heads,
        in_specs=[SMEM, ANY],
        out_specs=[VMEM] * heads,
        scratch_shapes=[pltpu.VMEM((tokens, heads * HEAD_DIM), queries.dtype), pltpu.SemaphoreType.DMA],
        compiler_params=params(MOST_VMEM_BYTES),
        cost_estimate=pl.CostEstimate(flops=0, bytes_accessed=queries.size // HEADS, transcendentals=0),
        name="turn",
    )(me, queries)


def plan_kernel(steps, n_pb, n_slots, key_blocks, rows, relay, pb_ref, *refs):
    mask_refs, count_ref, live_refs = refs[: -len(steps) - 1], refs[-len(steps) - 1], refs[-len(steps) :]
    pb = pb_ref[0]
    sign = 1 - 2 * (pb & 1)
    inner = ((pb > 0) & (pb < n_pb - 1)).astype(jnp.int32)
    helper = ((pb == 1) | (pb == n_pb - 2)).astype(jnp.int32)
    for step, (sources, live) in enumerate(zip(steps, live_refs)):
        total = jnp.int32(0)
        for guest, mask_ref in enumerate(mask_refs):

            def row_step(r, base, guest=guest, mask_ref=mask_ref):
                count = jnp.int32(0)
                for s, (delta, open_to_guests) in enumerate(sources):
                    if guest and not open_to_guests:
                        continue
                    j = pb + delta * sign
                    inside = ((j >= 0) & (j < n_pb)).astype(jnp.int32)
                    if relay and abs(delta) > 1:
                        inside = inside * inner
                    if guest:
                        inside = inside * helper
                    j = jnp.clip(j, 0, n_pb - 1)
                    for slot in range(n_slots):
                        for t in range(key_blocks):
                            block = (s * n_slots + slot) * key_blocks + t
                            live[2 * base + count] = ((r + guest * rows) << ROW_SHIFT) + block
                            column = j * key_blocks + t
                            count += inside * mask_ref[(slot * n_pb * key_blocks + column) * rows + r]
                live[2 * base + count] = -1
                return base + ((count + 1) >> 1)

            total = lax.fori_loop(0, rows, row_step, total)
        for u in range(GROUP):
            live[2 * (total + u)] = 0
            live[2 * (total + u) + 1] = -1
        count_ref[step] = total


def plan(pb, masks, steps, n_pb, n_slots, key_blocks, rows, relay):
    sizes = [len(masks) * rows * ((len(step) * n_slots * key_blocks + 2) // 2) + GROUP for step in steps]
    out_shape = [jax.ShapeDtypeStruct((len(steps),), jnp.int32)]
    out_shape += [jax.ShapeDtypeStruct((2 * size,), jnp.int32) for size in sizes]
    counts, *lives = pl.pallas_call(
        functools.partial(plan_kernel, steps, n_pb, n_slots, key_blocks, rows, relay),
        out_shape=out_shape,
        in_specs=[SMEM] * (1 + len(masks)),
        out_specs=[SMEM] * len(out_shape),
        compiler_params=params(),
        name="plan",
    )(pb, *masks)
    return [(counts, i, live) for i, live in enumerate(lives)]


def in_parts(x):
    found = []
    for _ in range(3):
        found.append(x.astype(jnp.bfloat16).astype(jnp.float32))
        x = x - found[-1]
    return found


def attend_kernel(n_src, entry, first, mode, guests, count_ref, live_ref, q_own, *refs):
    n_kv = n_src
    guest_ref, refs = (refs[0], refs[1:]) if guests else (None, refs)
    kv_refs, refs = refs[:n_kv], refs[n_kv:]
    state_in, refs = ((), refs) if first else (refs[:3], refs[3:])
    if mode == "last":
        (out_ref, kv, q_ref, *state, sems) = refs
    elif mode == "send":
        (*state, part_ref, kv, q_ref, sems) = refs
    else:
        (*state, kv, q_ref, sems) = refs
    m_ref, l_ref, acc_ref = state
    blocks = kv.shape[0] // n_src
    rows = q_own.shape[0]
    copies = [
        pltpu.make_async_copy(kv_refs[s], kv.at[pl.ds(s * blocks, blocks)], sems.at[s]) for s in range(n_src)
    ]
    copies += [pltpu.make_async_copy(a, b, sems.at[n_src + i]) for i, (a, b) in enumerate(zip(state_in, state))]
    copies.append(pltpu.make_async_copy(q_own, q_ref.at[pl.ds(0, rows)], sems.at[n_src + 3]))
    if guests:
        copies.append(pltpu.make_async_copy(guest_ref, q_ref.at[pl.ds(rows, rows)], sems.at[n_src + 4]))
    for copy in copies:
        copy.start()
    if first:
        m_ref[...] = jnp.full(m_ref.shape, NEG, jnp.float32)
        l_ref[...] = jnp.zeros(l_ref.shape, jnp.float32)
        acc_ref[...] = jnp.zeros(acc_ref.shape, jnp.float32)
    for copy in copies:
        copy.wait()
    total = count_ref[entry]
    nn = (((1,), (0,)), ((), ()))
    f32, bf16 = jnp.float32, jnp.bfloat16

    def group_step(g, _):
        found = []
        for u in range(GROUP):
            index = g * GROUP + u
            code0, code1 = live_ref[2 * index], live_ref[2 * index + 1]
            r = code0 >> ROW_SHIFT
            b0 = code0 & ((1 << ROW_SHIFT) - 1)
            b1 = jnp.maximum(code1, 0) & ((1 << ROW_SHIFT) - 1)
            x = lax.dot_general(jnp.concatenate([kv[b0, 0], kv[b1, 0]]), q_ref[r], nn, preferred_element_type=f32)
            x0 = jnp.where(index < total, x[:BLOCK], NEG)
            x1 = jnp.where(code1 >= 0, x[BLOCK:], NEG)
            top = jnp.max(jnp.maximum(x0, x1), axis=0, keepdims=True)
            w0 = jnp.exp2((x0 - top) * EXP2_SCALE)
            w1 = jnp.exp2((x1 - top) * EXP2_SCALE)
            total_w = jnp.sum(w0 + w1, axis=0, keepdims=True)
            w = jnp.concatenate([w0.astype(bf16), w1.astype(bf16)])
            v = jnp.concatenate([kv[b0, 1], kv[b1, 1]], axis=1)
            found.append((r, top, total_w, lax.dot_general(v, w, nn, preferred_element_type=f32)))
        for r, top, total_w, part in found:
            m = m_ref[r]
            m_new = jnp.maximum(m, top)
            alpha = jnp.exp2((m - m_new) * EXP2_SCALE)
            beta = jnp.exp2((top - m_new) * EXP2_SCALE)
            m_ref[r] = m_new
            l_ref[r] = l_ref[r] * alpha + total_w * beta
            acc_ref[r] = acc_ref[r] * alpha + part * beta
        return 0

    lax.fori_loop(0, (total + GROUP - 1) // GROUP, group_step, 0)
    if mode == "last":
        for r in range(rows):
            out_ref[r * BLOCK : (r + 1) * BLOCK, :] = (acc_ref[r] / l_ref[r]).T.astype(out_ref.dtype)
    if mode == "send":
        for r in range(rows):
            l = l_ref[rows + r]
            part_ref[r, :HEAD_DIM] = (acc_ref[rows + r] / jnp.where(l > 0, l, 1.0)).astype(part_ref.dtype)
            words = in_parts(m_ref[rows + r]) + in_parts(l)
            words.append(jnp.zeros((STAT_ROWS - len(words), BLOCK), f32))
            part_ref[r, HEAD_DIM:] = jnp.concatenate(words).astype(part_ref.dtype)


def attend(listed, q, guest, sources, state, mode, sets, name):
    counts, entry, live = listed
    rows, dtype = q.shape[0], q.dtype
    first = state is None
    state = () if first else tuple(state)
    stat = (sets * rows, 1, BLOCK)
    shapes = [stat, stat, (sets * rows, HEAD_DIM, BLOCK)]
    if mode == "last":
        out_shape = [jax.ShapeDtypeStruct((rows * BLOCK, HEAD_DIM), dtype)]
    else:
        out_shape = [jax.ShapeDtypeStruct(shape, jnp.float32) for shape in shapes]
    if mode == "send":
        out_shape.append(jax.ShapeDtypeStruct((rows, HEAD_DIM + STAT_ROWS, BLOCK), dtype))
    n_src = len(sources)
    blocks = sources[0].shape[0]
    guests = () if guest is None else (guest,)
    scratch = [pltpu.VMEM((n_src * blocks,) + sources[0].shape[1:], dtype)]
    scratch += [pltpu.VMEM(((1 + len(guests)) * rows, HEAD_DIM, BLOCK), dtype)]
    if mode == "last":
        scratch += [pltpu.VMEM(shape, jnp.float32) for shape in shapes]
    scratch.append(pltpu.SemaphoreType.DMA((n_src + 5,)))
    return pl.pallas_call(
        functools.partial(attend_kernel, n_src, entry, first, mode, bool(guests)),
        out_shape=out_shape,
        in_specs=[SMEM, SMEM, ANY] + [ANY] * (len(guests) + n_src + len(state)),
        out_specs=[VMEM] * len(out_shape),
        scratch_shapes=scratch,
        compiler_params=params(),
        cost_estimate=pl.CostEstimate(flops=0, bytes_accessed=HEAD_DIM * BLOCK, transcendentals=0),
        name=name,
    )(counts, live, q, *guests, *sources, *state)


def merge_kernel(outer_ref, m_ref, l_ref, acc_ref, part_ref, out_ref):
    outer = outer_ref[0] > 0
    for r in range(part_ref.shape[0]):
        m, l = m_ref[r], l_ref[r]
        words = part_ref[r, HEAD_DIM:].astype(jnp.float32)
        top = jnp.where(outer, words[0:1] + words[1:2] + words[2:3], NEG)
        extra = jnp.where(outer, words[3:4] + words[4:5] + words[5:6], 0.0)
        m_new = jnp.maximum(m, top)
        alpha = jnp.exp2((m - m_new) * EXP2_SCALE)
        beta = jnp.exp2((top - m_new) * EXP2_SCALE) * extra
        done = (acc_ref[r] * alpha + part_ref[r, :HEAD_DIM].astype(jnp.float32) * beta) / (l * alpha + beta)
        out_ref[r * BLOCK : (r + 1) * BLOCK, :] = done.T.astype(out_ref.dtype)


def merge(outer, state, part, name):
    rows = part.shape[0]
    half = lambda x: pl.BlockSpec((rows,) + x.shape[1:], lambda i: (0, 0, 0))
    return pl.pallas_call(
        merge_kernel,
        out_shape=jax.ShapeDtypeStruct((rows * BLOCK, HEAD_DIM), part.dtype),
        grid=(1,),
        in_specs=[SMEM] + [half(x) for x in state] + [VMEM],
        out_specs=VMEM,
        compiler_params=params(),
        name=name,
    )(outer, *state, part)


def place_kernel(n_ka, heads, me_ref, *refs):
    pieces, out_ref, sems = refs[: n_ka * heads], refs[-2], refs[-1]
    copies = []
    for k in range(n_ka):
        for c in range(heads):
            col = pl.multiple_of(((me_ref[0] ^ k) * heads + c) * HEAD_DIM, HEAD_DIM)
            copies.append(
                pltpu.make_async_copy(pieces[c * n_ka + k], out_ref.at[:, pl.ds(col, HEAD_DIM)], sems.at[c, k])
            )
    for copy in copies:
        copy.start()
    for copy in copies:
        copy.wait()


def place(me, pieces, n_ka, heads):
    rows = pieces[0].shape[0]
    return pl.pallas_call(
        functools.partial(place_kernel, n_ka, heads),
        out_shape=jax.ShapeDtypeStruct((rows, HEADS * HEAD_DIM), pieces[0].dtype),
        in_specs=[SMEM] + [ANY] * (n_ka * heads),
        out_specs=ANY,
        scratch_shapes=[pltpu.SemaphoreType.DMA((heads, n_ka))],
        compiler_params=params(),
        name="place",
    )(me, *pieces)


def local(n_pb, n_ka, queries, keys, values, block_mask):
    heads = HEADS // n_ka
    shard = keys.shape[0]
    key_blocks = shard // BLOCK
    rows = queries.shape[0] // BLOCK
    me = lax.axis_index("ka").astype(jnp.int32)
    pb = lax.axis_index("pb").astype(jnp.int32)
    me1, pb1 = me[None], pb[None]
    relay = n_pb >= 4 and n_pb % 2 == 0
    def swap(x, k):
        return lax.ppermute(x, "ka", [(i, i ^ k) for i in range(n_ka)])

    def hops(odd, step):
        found = []
        for low in range(odd, n_pb - 1, 2):
            found += [(low, low + 1)] if low - (step - 1) >= 0 else []
            found += [(low + 1, low)] if low + 1 + (step - 1) < n_pb else []
        if relay and step > 1:
            found = [(i, j) for i, j in found if 0 < j < n_pb - 1]
        return found

    def exchange(x, odd, step):
        found = hops(odd, step)
        return lax.ppermute(x, "pb", found) if found else None

    def inward(x):
        return lax.ppermute(x, "pb", [(0, 1), (n_pb - 1, n_pb - 2)])

    def outward(x):
        return lax.ppermute(x, "pb", [(1, 0), (n_pb - 2, n_pb - 1)])

    def sort(x, before=None):
        mixed = [y if i == 0 else swap(y, 2 * i) for i, y in enumerate(x)]
        mixed = after(mixed, before)
        theirs = swap(jnp.stack([y[1] for y in mixed]), 1)
        return jnp.concatenate([jnp.stack([y[0] for y in mixed]), theirs]), mixed

    def blocks(x):
        return x[:, : 2 * shard].reshape(n_ka * key_blocks, 2, BLOCK, HEAD_DIM)

    def after(arrays, done):
        return arrays if done is None else lax.optimization_barrier((arrays, done))[0]

    def flags(x):
        return x[:, : block_mask.shape[1], :rows].astype(jnp.int32).reshape(-1)

    parts = (block_mask.T,) + ((inward(block_mask.T),) if relay else ())
    owns, over, guest = [], [], [None] * heads
    for c in range(heads):
        place_of = after(me1, (q, mixed)) if c else me1
        packed = pack(place_of, keys, values, parts if c == heads - 1 else (), n_ka, heads, c)
        if c == 0:
            q = turn(after(me1, packed), queries, heads)
            own, mixed = sort(packed, (q, parts))
        else:
            own, mixed = sort(after(packed, owns[0]), over[0])
        owns.append(blocks(own))
        before = ((over[0], guest[0]), over[0]) if c else (None, None)
        over.append([exchange(after(owns[c], before[odd]), odd, 1) for odd in (0, 1)])
        if relay:
            guest[c] = inward(after(q[c], over[0]))
    size = mask_rows(block_mask.shape[1])
    masks = [flags(own[:, 2 * shard + i * size :]) for i in range(len(parts))]

    steps = [((0, False),)]
    for step in range(1, n_pb):
        found = (((step, False),) if hops(0, step) else ()) + (((-step, True),) if hops(1, step) else ())
        if step == 1:
            steps[0] += found
        elif found:
            steps.append(found)
    last = len(steps) - 1
    late = relay and last == 1
    if late:
        (own_source, even_source, odd_source), far_sources = steps
        steps += [(own_source, even_source), (odd_source,) + far_sources]
    lists = plan(pb1, masks, steps, n_pb, n_ka, key_blocks, rows, relay)
    state = [None] * heads

    def run(c, step, sources):
        kind = "keep" if step < last else "send" if relay else "last"
        sources = [x for x in sources if x is not None]
        name = f"attend_{c}_{step}"
        listed = lists[step + (2 if late and c else 0)]
        seen = None if late and c and step == 0 else guest[c]
        return attend(listed, q[c], seen, sources, state[c], kind, 2 if relay else 1, name)

    for step in range(last):
        for c in range(heads):
            sources = ([owns[c]] if step == 0 else []) + over[c]
            even, odd = over[c]
            near = odd
            if even is not None and odd is not None:
                even, odd = after((even, odd), (even, odd))
            over[c] = [exchange(odd, 0, step + 2), exchange(even, 1, step + 2)]
            if late and c:
                sources, over[c] = sources[:2], [near, over[c][1]]
            state[c] = run(c, step, sources)

    pieces = []
    sent = None
    for c in range(heads):
        found = run(c, last, ([] if last else [owns[c]]) + over[c])
        if relay:
            outer = ((pb == 0) | (pb == n_pb - 1)).astype(jnp.int32)[None]
            out = merge(outer, found[:3], outward(after(found[3], sent)), f"merge_{c}")
        else:
            out = found[0]
        mine = [out] + [swap(out, k) for k in range(2, n_ka, 2)]
        sent = mine
        others = [swap(x, 1) for x in mine]
        pieces += [x for two in zip(mine, others) for x in two]
    return place(me1, pieces, n_ka, heads)


def solution(mesh):
    n_pb, n_ka = mesh.shape["pb"], mesh.shape["ka"]
    return jax.shard_map(
        functools.partial(local, n_pb, n_ka),
        mesh=mesh,
        in_specs=(P("pb", None), P(("ka", "pb"), None), P(("ka", "pb"), None), P("pb", "ka")),
        out_specs=P("pb", None),
        check_vma=False,
    )
```

```python
import functools
import math

import jax
import jax.numpy as jnp
from jax import lax
from jax.experimental import pallas as pl
from jax.experimental.pallas import tpu as pltpu
from jax.sharding import PartitionSpec as P

HEADS = 16
HEAD_DIM = 128
BLOCK = 128
NEG = -1e30
EXP2_SCALE = math.log2(math.e) / math.sqrt(HEAD_DIM)
GROUP = 8
STAT_ROWS = 16
ROW_SHIFT = 16
VMEM_BYTES = 40 * 1024 * 1024
MOST_VMEM_BYTES = 60 * 1024 * 1024

VMEM = pl.BlockSpec(memory_space=pltpu.VMEM)
SMEM = pl.BlockSpec(memory_space=pltpu.SMEM)
ANY = pl.BlockSpec(memory_space=pl.ANY)


def params(size=VMEM_BYTES):
    return pltpu.CompilerParams(vmem_limit_bytes=size)


def mask_rows(rows):
    return -(-rows // 16) * 16


def pack_kernel(n_ka, heads, c, n_masks, me_ref, *refs):
    mask_refs, refs = refs[:n_masks], refs[n_masks:]
    k_all, v_all, *out_refs, v_ref, sems = refs
    key_blocks = k_all.shape[0] // BLOCK
    copies = []
    for k in range(n_ka):
        out_ref = out_refs[k // 2]
        col = pl.multiple_of(((me_ref[0] ^ k) * heads + c) * HEAD_DIM, HEAD_DIM)
        for t in range(key_blocks):
            rows, at = pl.ds(t * BLOCK, BLOCK), pl.ds(2 * t * BLOCK, BLOCK)
            sem = sems.at[k * key_blocks + t]
            copies.append(
                (
                    pltpu.make_async_copy(k_all.at[rows, pl.ds(col, HEAD_DIM)], out_ref.at[k % 2, at], sem.at[0]),
                    pltpu.make_async_copy(v_all.at[rows, pl.ds(col, HEAD_DIM)], v_ref.at[k, t], sem.at[1]),
                )
            )
    for pair in copies:
        for copy in pair:
            copy.start()
    for i, mask_ref in enumerate(mask_refs):
        size = mask_rows(mask_ref.shape[0])
        row, column = (lax.broadcasted_iota(jnp.int32, (size, HEAD_DIM), axis) for axis in (0, 1))
        mask = jnp.zeros((size, HEAD_DIM), jnp.int32)
        for a in range(mask_ref.shape[0]):
            for b in range(mask_ref.shape[1]):
                mask = jnp.where((row == a) & (column == b), mask_ref[a, b], mask)
        mask = mask.astype(jnp.float32).astype(k_all.dtype)
        at = 2 * key_blocks * BLOCK + i * size
        for k in range(n_ka):
            out_refs[k // 2][k % 2, at : at + size] = mask
    for k in range(n_ka):
        for t in range(key_blocks):
            copies[k * key_blocks + t][1].wait()
            out_refs[k // 2][k % 2, (2 * t + 1) * BLOCK : (2 * t + 2) * BLOCK] = v_ref[k, t].T
    for pair in copies:
        pair[0].wait()


def pack(me, keys, values, masks, n_ka, heads, c):
    key_blocks = keys.shape[0] // BLOCK
    size = 2 * keys.shape[0] + sum(mask_rows(mask.shape[0]) for mask in masks)
    return pl.pallas_call(
        functools.partial(pack_kernel, n_ka, heads, c, len(masks)),
        out_shape=[jax.ShapeDtypeStruct((2, size, HEAD_DIM), keys.dtype)] * (n_ka // 2),
        in_specs=[SMEM] + [SMEM] * len(masks) + [ANY, ANY],
        out_specs=[VMEM] * (n_ka // 2),
        scratch_shapes=[
            pltpu.VMEM((n_ka, key_blocks, BLOCK, HEAD_DIM), values.dtype),
            pltpu.SemaphoreType.DMA((n_ka * key_blocks, 2)),
        ],
        compiler_params=params(MOST_VMEM_BYTES),
        cost_estimate=pl.CostEstimate(flops=0, bytes_accessed=keys.size, transcendentals=0),
        name=f"pack_{c}",
    )(me, *masks, keys, values)


def turn_kernel(heads, me_ref, q_all, *refs):
    out_refs, (q_ref, sem) = refs[:heads], refs[heads:]
    column = pl.multiple_of(me_ref[0] * heads * HEAD_DIM, HEAD_DIM)
    copy = pltpu.make_async_copy(q_all.at[:, pl.ds(column, heads * HEAD_DIM)], q_ref, sem)
    copy.start()
    copy.wait()
    for c in range(heads):
        for r in range(out_refs[c].shape[0]):
            out_refs[c][r] = q_ref[r * BLOCK : (r + 1) * BLOCK, c * HEAD_DIM : (c + 1) * HEAD_DIM].T


def turn(me, queries, heads):
    tokens = queries.shape[0]
    return pl.pallas_call(
        functools.partial(turn_kernel, heads),
        out_shape=[jax.ShapeDtypeStruct((tokens // BLOCK, HEAD_DIM, BLOCK), queries.dtype)] * heads,
        in_specs=[SMEM, ANY],
        out_specs=[VMEM] * heads,
        scratch_shapes=[pltpu.VMEM((tokens, heads * HEAD_DIM), queries.dtype), pltpu.SemaphoreType.DMA],
        compiler_params=params(MOST_VMEM_BYTES),
        cost_estimate=pl.CostEstimate(flops=0, bytes_accessed=queries.size // HEADS, transcendentals=0),
        name="turn",
    )(me, queries)


def plan_kernel(steps, n_pb, n_slots, key_blocks, rows, relay, pb_ref, *refs):
    mask_refs, count_ref, live_refs = refs[: -len(steps) - 1], refs[-len(steps) - 1], refs[-len(steps) :]
    pb = pb_ref[0]
    sign = 1 - 2 * (pb & 1)
    inner = ((pb > 0) & (pb < n_pb - 1)).astype(jnp.int32)
    helper = ((pb == 1) | (pb == n_pb - 2)).astype(jnp.int32)
    for step, (sources, live) in enumerate(zip(steps, live_refs)):
        total = jnp.int32(0)
        for guest, mask_ref in enumerate(mask_refs):

            def row_step(r, base, guest=guest, mask_ref=mask_ref):
                count = jnp.int32(0)
                for s, (delta, open_to_guests) in enumerate(sources):
                    if guest and not open_to_guests:
                        continue
                    j = pb + delta * sign
                    inside = ((j >= 0) & (j < n_pb)).astype(jnp.int32)
                    if relay and abs(delta) > 1:
                        inside = inside * inner
                    if guest:
                        inside = inside * helper
                    j = jnp.clip(j, 0, n_pb - 1)
                    for slot in range(n_slots):
                        for t in range(key_blocks):
                            block = (s * n_slots + slot) * key_blocks + t
                            live[2 * base + count] = ((r + guest * rows) << ROW_SHIFT) + block
                            column = j * key_blocks + t
                            count += inside * mask_ref[(slot * n_pb * key_blocks + column) * rows + r]
                live[2 * base + count] = -1
                return base + ((count + 1) >> 1)

            total = lax.fori_loop(0, rows, row_step, total)
        for u in range(GROUP):
            live[2 * (total + u)] = 0
            live[2 * (total + u) + 1] = -1
        count_ref[step] = total


def plan(pb, masks, steps, n_pb, n_slots, key_blocks, rows, relay):
    sizes = [len(masks) * rows * ((len(step) * n_slots * key_blocks + 2) // 2) + GROUP for step in steps]
    out_shape = [jax.ShapeDtypeStruct((len(steps),), jnp.int32)]
    out_shape += [jax.ShapeDtypeStruct((2 * size,), jnp.int32) for size in sizes]
    counts, *lives = pl.pallas_call(
        functools.partial(plan_kernel, steps, n_pb, n_slots, key_blocks, rows, relay),
        out_shape=out_shape,
        in_specs=[SMEM] * (1 + len(masks)),
        out_specs=[SMEM] * len(out_shape),
        compiler_params=params(),
        name="plan",
    )(pb, *masks)
    return [(counts, i, live) for i, live in enumerate(lives)]


def in_parts(x):
    found = []
    for _ in range(3):
        found.append(x.astype(jnp.bfloat16).astype(jnp.float32))
        x = x - found[-1]
    return found


def attend_kernel(n_src, entry, first, mode, guests, count_ref, live_ref, q_own, *refs):
    n_kv = n_src
    guest_ref, refs = (refs[0], refs[1:]) if guests else (None, refs)
    kv_refs, refs = refs[:n_kv], refs[n_kv:]
    state_in, refs = ((), refs) if first else (refs[:3], refs[3:])
    if mode == "last":
        (out_ref, kv, q_ref, *state, sems) = refs
    elif mode == "send":
        (*state, part_ref, kv, q_ref, sems) = refs
    else:
        (*state, kv, q_ref, sems) = refs
    m_ref, l_ref, acc_ref = state
    blocks = kv.shape[0] // n_src
    rows = q_own.shape[0]
    copies = [
        pltpu.make_async_copy(kv_refs[s], kv.at[pl.ds(s * blocks, blocks)], sems.at[s]) for s in range(n_src)
    ]
    copies += [pltpu.make_async_copy(a, b, sems.at[n_src + i]) for i, (a, b) in enumerate(zip(state_in, state))]
    copies.append(pltpu.make_async_copy(q_own, q_ref.at[pl.ds(0, rows)], sems.at[n_src + 3]))
    if guests:
        copies.append(pltpu.make_async_copy(guest_ref, q_ref.at[pl.ds(rows, rows)], sems.at[n_src + 4]))
    for copy in copies:
        copy.start()
    if first:
        m_ref[...] = jnp.full(m_ref.shape, NEG, jnp.float32)
        l_ref[...] = jnp.zeros(l_ref.shape, jnp.float32)
        acc_ref[...] = jnp.zeros(acc_ref.shape, jnp.float32)
    for copy in copies:
        copy.wait()
    total = count_ref[entry]
    nn = (((1,), (0,)), ((), ()))
    f32, bf16 = jnp.float32, jnp.bfloat16

    def group_step(g, _):
        found = []
        for u in range(GROUP):
            index = g * GROUP + u
            code0, code1 = live_ref[2 * index], live_ref[2 * index + 1]
            r = code0 >> ROW_SHIFT
            b0 = code0 & ((1 << ROW_SHIFT) - 1)
            b1 = jnp.maximum(code1, 0) & ((1 << ROW_SHIFT) - 1)
            x = lax.dot_general(jnp.concatenate([kv[b0, 0], kv[b1, 0]]), q_ref[r], nn, preferred_element_type=f32)
            x0 = jnp.where(index < total, x[:BLOCK], NEG)
            x1 = jnp.where(code1 >= 0, x[BLOCK:], NEG)
            top = jnp.max(jnp.maximum(x0, x1), axis=0, keepdims=True)
            w0 = jnp.exp2((x0 - top) * EXP2_SCALE)
            w1 = jnp.exp2((x1 - top) * EXP2_SCALE)
            total_w = jnp.sum(w0 + w1, axis=0, keepdims=True)
            w = jnp.concatenate([w0.astype(bf16), w1.astype(bf16)])
            v = jnp.concatenate([kv[b0, 1], kv[b1, 1]], axis=1)
            found.append((r, top, total_w, lax.dot_general(v, w, nn, preferred_element_type=f32)))
        for r, top, total_w, part in found:
            m = m_ref[r]
            m_new = jnp.maximum(m, top)
            alpha = jnp.exp2((m - m_new) * EXP2_SCALE)
            beta = jnp.exp2((top - m_new) * EXP2_SCALE)
            m_ref[r] = m_new
            l_ref[r] = l_ref[r] * alpha + total_w * beta
            acc_ref[r] = acc_ref[r] * alpha + part * beta
        return 0

    lax.fori_loop(0, (total + GROUP - 1) // GROUP, group_step, 0)
    if mode == "last":
        for r in range(rows):
            out_ref[r * BLOCK : (r + 1) * BLOCK, :] = (acc_ref[r] / l_ref[r]).T.astype(out_ref.dtype)
    if mode == "send":
        for r in range(rows):
            l = l_ref[rows + r]
            part_ref[r, :HEAD_DIM] = (acc_ref[rows + r] / jnp.where(l > 0, l, 1.0)).astype(part_ref.dtype)
            words = in_parts(m_ref[rows + r]) + in_parts(l)
            words.append(jnp.zeros((STAT_ROWS - len(words), BLOCK), f32))
            part_ref[r, HEAD_DIM:] = jnp.concatenate(words).astype(part_ref.dtype)


def attend(listed, q, guest, sources, state, mode, sets, name):
    counts, entry, live = listed
    rows, dtype = q.shape[0], q.dtype
    first = state is None
    state = () if first else tuple(state)
    stat = (sets * rows, 1, BLOCK)
    shapes = [stat, stat, (sets * rows, HEAD_DIM, BLOCK)]
    if mode == "last":
        out_shape = [jax.ShapeDtypeStruct((rows * BLOCK, HEAD_DIM), dtype)]
    else:
        out_shape = [jax.ShapeDtypeStruct(shape, jnp.float32) for shape in shapes]
    if mode == "send":
        out_shape.append(jax.ShapeDtypeStruct((rows, HEAD_DIM + STAT_ROWS, BLOCK), dtype))
    n_src = len(sources)
    blocks = sources[0].shape[0]
    guests = () if guest is None else (guest,)
    scratch = [pltpu.VMEM((n_src * blocks,) + sources[0].shape[1:], dtype)]
    scratch += [pltpu.VMEM(((1 + len(guests)) * rows, HEAD_DIM, BLOCK), dtype)]
    if mode == "last":
        scratch += [pltpu.VMEM(shape, jnp.float32) for shape in shapes]
    scratch.append(pltpu.SemaphoreType.DMA((n_src + 5,)))
    return pl.pallas_call(
        functools.partial(attend_kernel, n_src, entry, first, mode, bool(guests)),
        out_shape=out_shape,
        in_specs=[SMEM, SMEM, ANY] + [ANY] * (len(guests) + n_src + len(state)),
        out_specs=[VMEM] * len(out_shape),
        scratch_shapes=scratch,
        compiler_params=params(),
        cost_estimate=pl.CostEstimate(flops=0, bytes_accessed=HEAD_DIM * BLOCK, transcendentals=0),
        name=name,
    )(counts, live, q, *guests, *sources, *state)


def merge_kernel(outer_ref, m_ref, l_ref, acc_ref, part_ref, out_ref):
    outer = outer_ref[0] > 0
    for r in range(part_ref.shape[0]):
        m, l = m_ref[r], l_ref[r]
        words = part_ref[r, HEAD_DIM:].astype(jnp.float32)
        top = jnp.where(outer, words[0:1] + words[1:2] + words[2:3], NEG)
        extra = jnp.where(outer, words[3:4] + words[4:5] + words[5:6], 0.0)
        m_new = jnp.maximum(m, top)
        alpha = jnp.exp2((m - m_new) * EXP2_SCALE)
        beta = jnp.exp2((top - m_new) * EXP2_SCALE) * extra
        done = (acc_ref[r] * alpha + part_ref[r, :HEAD_DIM].astype(jnp.float32) * beta) / (l * alpha + beta)
        out_ref[r * BLOCK : (r + 1) * BLOCK, :] = done.T.astype(out_ref.dtype)


def merge(outer, state, part, name):
    rows = part.shape[0]
    half = lambda x: pl.BlockSpec((rows,) + x.shape[1:], lambda i: (0, 0, 0))
    return pl.pallas_call(
        merge_kernel,
        out_shape=jax.ShapeDtypeStruct((rows * BLOCK, HEAD_DIM), part.dtype),
        grid=(1,),
        in_specs=[SMEM] + [half(x) for x in state] + [VMEM],
        out_specs=VMEM,
        compiler_params=params(),
        name=name,
    )(outer, *state, part)


def place_kernel(n_ka, heads, me_ref, *refs):
    pieces, out_ref, sems = refs[: n_ka * heads], refs[-2], refs[-1]
    copies = []
    for k in range(n_ka):
        for c in range(heads):
            col = pl.multiple_of(((me_ref[0] ^ k) * heads + c) * HEAD_DIM, HEAD_DIM)
            copies.append(
                pltpu.make_async_copy(pieces[c * n_ka + k], out_ref.at[:, pl.ds(col, HEAD_DIM)], sems.at[c, k])
            )
    for copy in copies:
        copy.start()
    for copy in copies:
        copy.wait()


def place(me, pieces, n_ka, heads):
    rows = pieces[0].shape[0]
    return pl.pallas_call(
        functools.partial(place_kernel, n_ka, heads),
        out_shape=jax.ShapeDtypeStruct((rows, HEADS * HEAD_DIM), pieces[0].dtype),
        in_specs=[SMEM] + [ANY] * (n_ka * heads),
        out_specs=ANY,
        scratch_shapes=[pltpu.SemaphoreType.DMA((heads, n_ka))],
        compiler_params=params(),
        name="place",
    )(me, *pieces)


def local(n_pb, n_ka, queries, keys, values, block_mask):
    heads = HEADS // n_ka
    shard = keys.shape[0]
    key_blocks = shard // BLOCK
    rows = queries.shape[0] // BLOCK
    me = lax.axis_index("ka").astype(jnp.int32)
    pb = lax.axis_index("pb").astype(jnp.int32)
    me1, pb1 = me[None], pb[None]
    relay = n_pb >= 4 and n_pb % 2 == 0
    def swap(x, k):
        return lax.ppermute(x, "ka", [(i, i ^ k) for i in range(n_ka)])

    def hops(odd, step):
        found = []
        for low in range(odd, n_pb - 1, 2):
            found += [(low, low + 1)] if low - (step - 1) >= 0 else []
            found += [(low + 1, low)] if low + 1 + (step - 1) < n_pb else []
        if relay and step > 1:
            found = [(i, j) for i, j in found if 0 < j < n_pb - 1]
        return found

    def exchange(x, odd, step):
        found = hops(odd, step)
        return lax.ppermute(x, "pb", found) if found else None

    def inward(x):
        return lax.ppermute(x, "pb", [(0, 1), (n_pb - 1, n_pb - 2)])

    def outward(x):
        return lax.ppermute(x, "pb", [(1, 0), (n_pb - 2, n_pb - 1)])

    def sort(x, before=None):
        mixed = [y if i == 0 else swap(y, 2 * i) for i, y in enumerate(x)]
        mixed = after(mixed, before)
        theirs = swap(jnp.stack([y[1] for y in mixed]), 1)
        return jnp.concatenate([jnp.stack([y[0] for y in mixed]), theirs]), mixed

    def blocks(x):
        return x[:, : 2 * shard].reshape(n_ka * key_blocks, 2, BLOCK, HEAD_DIM)

    def after(arrays, done):
        return arrays if done is None else lax.optimization_barrier((arrays, done))[0]

    def flags(x):
        return x[:, : block_mask.shape[1], :rows].astype(jnp.int32).reshape(-1)

    steps = [((0, False),)]
    for step in range(1, n_pb):
        found = (((step, False),) if hops(0, step) else ()) + (((-step, True),) if hops(1, step) else ())
        if step == 1:
            steps[0] += found
        elif found:
            steps.append(found)
    last = len(steps) - 1
    parts = (block_mask.T,) + ((inward(block_mask.T),) if relay else ())
    owns, over, guest = [], [], [None] * heads
    for c in range(heads):
        place_of = after(me1, (q, mixed)) if c else me1
        packed = pack(place_of, keys, values, parts if c == heads - 1 else (), n_ka, heads, c)
        if c == 0:
            q = turn(after(me1, packed), queries, heads)
            own, mixed = sort(packed, (q, parts))
        else:
            own, mixed = sort(after(packed, owns[0]), over[0])
        owns.append(blocks(own))
        if c == heads - 1:
            size = mask_rows(block_mask.shape[1])
            masks = [flags(own[:, 2 * shard + i * size :]) for i in range(len(parts))]
            lists = plan(pb1, masks, steps, n_pb, n_ka, key_blocks, rows, relay)
        before = ((over[0], guest[0], lists[0][0] if c == heads - 1 else None), over[0]) if c else (None, None)
        over.append([exchange(after(owns[c], before[odd]), odd, 1) for odd in (0, 1)])
        if relay:
            guest[c] = inward(after(q[c], over[0]))
    state = [None] * heads

    def run(c, step, sources):
        kind = "keep" if step < last else "send" if relay else "last"
        sources = [x for x in sources if x is not None]
        name = f"attend_{c}_{step}"
        return attend(lists[step], q[c], guest[c], sources, state[c], kind, 2 if relay else 1, name)

    for step in range(last):
        for c in range(heads):
            sources = ([owns[c]] if step == 0 else []) + over[c]
            even, odd = over[c]
            if even is not None and odd is not None:
                even, odd = after((even, odd), guest[c] if c else (even, odd))
            over[c] = [exchange(odd, 0, step + 2), exchange(even, 1, step + 2)]
            state[c] = run(c, step, sources)

    pieces = []
    sent = far = None
    for c in range(heads):
        found = run(c, last, ([] if last else [owns[c]]) + after(over[c], sent))
        if relay:
            outer = ((pb == 0) | (pb == n_pb - 1)).astype(jnp.int32)[None]
            out = merge(outer, found[:3], outward(after(found[3], far)), f"merge_{c}")
        else:
            out = found[0]
        mine = [out] + [swap(out, k) for k in range(2, n_ka, 2)]
        sent, far = mine[: n_ka // 4 + 1], mine[n_ka // 4 + 1 :]
        others = [swap(x, 1) for x in mine]
        pieces += [x for two in zip(mine, others) for x in two]
    return place(me1, pieces, n_ka, heads)


def solution(mesh):
    n_pb, n_ka = mesh.shape["pb"], mesh.shape["ka"]
    return jax.shard_map(
        functools.partial(local, n_pb, n_ka),
        mesh=mesh,
        in_specs=(P("pb", None), P(("ka", "pb"), None), P(("ka", "pb"), None), P("pb", "ka")),
        out_specs=P("pb", None),
        check_vma=False,
    )
```

```python
import functools
import math

import jax
import jax.numpy as jnp
from jax import lax
from jax.experimental import pallas as pl
from jax.experimental.pallas import tpu as pltpu
from jax.sharding import PartitionSpec as P

HEADS = 16
HEAD_DIM = 128
BLOCK = 128
NEG = -1e30
EXP2_SCALE = math.log2(math.e) / math.sqrt(HEAD_DIM)
GROUP = 8
STAT_ROWS = 16
ROW_SHIFT = 16
VMEM_BYTES = 40 * 1024 * 1024
MOST_VMEM_BYTES = 60 * 1024 * 1024

VMEM = pl.BlockSpec(memory_space=pltpu.VMEM)
SMEM = pl.BlockSpec(memory_space=pltpu.SMEM)
ANY = pl.BlockSpec(memory_space=pl.ANY)


def params(size=VMEM_BYTES):
    return pltpu.CompilerParams(vmem_limit_bytes=size)


def mask_rows(rows):
    return -(-rows // 16) * 16


def pack_kernel(n_ka, heads, c, n_masks, me_ref, *refs):
    mask_refs, refs = refs[:n_masks], refs[n_masks:]
    k_all, v_all, *out_refs, v_ref, sems = refs
    key_blocks = k_all.shape[0] // BLOCK
    copies = []
    for k in range(n_ka):
        out_ref = out_refs[k // 2]
        col = pl.multiple_of(((me_ref[0] ^ k) * heads + c) * HEAD_DIM, HEAD_DIM)
        for t in range(key_blocks):
            rows, at = pl.ds(t * BLOCK, BLOCK), pl.ds(2 * t * BLOCK, BLOCK)
            sem = sems.at[k * key_blocks + t]
            copies.append(
                (
                    pltpu.make_async_copy(k_all.at[rows, pl.ds(col, HEAD_DIM)], out_ref.at[k % 2, at], sem.at[0]),
                    pltpu.make_async_copy(v_all.at[rows, pl.ds(col, HEAD_DIM)], v_ref.at[k, t], sem.at[1]),
                )
            )
    for pair in copies:
        for copy in pair:
            copy.start()
    for i, mask_ref in enumerate(mask_refs):
        size = mask_rows(mask_ref.shape[0])
        row, column = (lax.broadcasted_iota(jnp.int32, (size, HEAD_DIM), axis) for axis in (0, 1))
        mask = jnp.zeros((size, HEAD_DIM), jnp.int32)
        for a in range(mask_ref.shape[0]):
            for b in range(mask_ref.shape[1]):
                mask = jnp.where((row == a) & (column == b), mask_ref[a, b], mask)
        mask = mask.astype(jnp.float32).astype(k_all.dtype)
        at = 2 * key_blocks * BLOCK + i * size
        for k in range(n_ka):
            out_refs[k // 2][k % 2, at : at + size] = mask
    for k in range(n_ka):
        for t in range(key_blocks):
            copies[k * key_blocks + t][1].wait()
            out_refs[k // 2][k % 2, (2 * t + 1) * BLOCK : (2 * t + 2) * BLOCK] = v_ref[k, t].T
    for pair in copies:
        pair[0].wait()


def pack(me, keys, values, masks, n_ka, heads, c):
    key_blocks = keys.shape[0] // BLOCK
    size = 2 * keys.shape[0] + sum(mask_rows(mask.shape[0]) for mask in masks)
    return pl.pallas_call(
        functools.partial(pack_kernel, n_ka, heads, c, len(masks)),
        out_shape=[jax.ShapeDtypeStruct((2, size, HEAD_DIM), keys.dtype)] * (n_ka // 2),
        in_specs=[SMEM] + [SMEM] * len(masks) + [ANY, ANY],
        out_specs=[VMEM] * (n_ka // 2),
        scratch_shapes=[
            pltpu.VMEM((n_ka, key_blocks, BLOCK, HEAD_DIM), values.dtype),
            pltpu.SemaphoreType.DMA((n_ka * key_blocks, 2)),
        ],
        compiler_params=params(MOST_VMEM_BYTES),
        cost_estimate=pl.CostEstimate(flops=0, bytes_accessed=keys.size, transcendentals=0),
        name=f"pack_{c}",
    )(me, *masks, keys, values)


def turn_kernel(heads, me_ref, q_all, *refs):
    out_refs, (q_ref, sem) = refs[:heads], refs[heads:]
    column = pl.multiple_of(me_ref[0] * heads * HEAD_DIM, HEAD_DIM)
    copy = pltpu.make_async_copy(q_all.at[:, pl.ds(column, heads * HEAD_DIM)], q_ref, sem)
    copy.start()
    copy.wait()
    for c in range(heads):
        for r in range(out_refs[c].shape[0]):
            out_refs[c][r] = q_ref[r * BLOCK : (r + 1) * BLOCK, c * HEAD_DIM : (c + 1) * HEAD_DIM].T


def turn(me, queries, heads):
    tokens = queries.shape[0]
    return pl.pallas_call(
        functools.partial(turn_kernel, heads),
        out_shape=[jax.ShapeDtypeStruct((tokens // BLOCK, HEAD_DIM, BLOCK), queries.dtype)] * heads,
        in_specs=[SMEM, ANY],
        out_specs=[VMEM] * heads,
        scratch_shapes=[pltpu.VMEM((tokens, heads * HEAD_DIM), queries.dtype), pltpu.SemaphoreType.DMA],
        compiler_params=params(MOST_VMEM_BYTES),
        cost_estimate=pl.CostEstimate(flops=0, bytes_accessed=queries.size // HEADS, transcendentals=0),
        name="turn",
    )(me, queries)


def plan_kernel(steps, n_pb, n_slots, key_blocks, rows, relay, pb_ref, *refs):
    mask_refs, count_ref, live_refs = refs[: -len(steps) - 1], refs[-len(steps) - 1], refs[-len(steps) :]
    pb = pb_ref[0]
    sign = 1 - 2 * (pb & 1)
    inner = ((pb > 0) & (pb < n_pb - 1)).astype(jnp.int32)
    helper = ((pb == 1) | (pb == n_pb - 2)).astype(jnp.int32)
    for step, (sources, live) in enumerate(zip(steps, live_refs)):
        total = jnp.int32(0)
        for guest, mask_ref in enumerate(mask_refs):

            def row_step(r, base, guest=guest, mask_ref=mask_ref):
                count = jnp.int32(0)
                for s, (delta, open_to_guests) in enumerate(sources):
                    if guest and not open_to_guests:
                        continue
                    j = pb + delta * sign
                    inside = ((j >= 0) & (j < n_pb)).astype(jnp.int32)
                    if relay and abs(delta) > 1:
                        inside = inside * inner
                    if guest:
                        inside = inside * helper
                    j = jnp.clip(j, 0, n_pb - 1)
                    for slot in range(n_slots):
                        for t in range(key_blocks):
                            block = (s * n_slots + slot) * key_blocks + t
                            live[2 * base + count] = ((r + guest * rows) << ROW_SHIFT) + block
                            column = j * key_blocks + t
                            count += inside * mask_ref[(slot * n_pb * key_blocks + column) * rows + r]
                live[2 * base + count] = -1
                return base + ((count + 1) >> 1)

            total = lax.fori_loop(0, rows, row_step, total)
        for u in range(GROUP):
            live[2 * (total + u)] = 0
            live[2 * (total + u) + 1] = -1
        count_ref[step] = total


def plan(pb, masks, steps, n_pb, n_slots, key_blocks, rows, relay):
    sizes = [len(masks) * rows * ((len(step) * n_slots * key_blocks + 2) // 2) + GROUP for step in steps]
    out_shape = [jax.ShapeDtypeStruct((len(steps),), jnp.int32)]
    out_shape += [jax.ShapeDtypeStruct((2 * size,), jnp.int32) for size in sizes]
    counts, *lives = pl.pallas_call(
        functools.partial(plan_kernel, steps, n_pb, n_slots, key_blocks, rows, relay),
        out_shape=out_shape,
        in_specs=[SMEM] * (1 + len(masks)),
        out_specs=[SMEM] * len(out_shape),
        compiler_params=params(),
        name="plan",
    )(pb, *masks)
    return [(counts, i, live) for i, live in enumerate(lives)]


def in_parts(x):
    found = []
    for _ in range(3):
        found.append(x.astype(jnp.bfloat16).astype(jnp.float32))
        x = x - found[-1]
    return found


def attend_kernel(n_src, entry, first, mode, guests, count_ref, live_ref, q_own, *refs):
    n_kv = n_src
    guest_ref, refs = (refs[0], refs[1:]) if guests else (None, refs)
    kv_refs, refs = refs[:n_kv], refs[n_kv:]
    state_in, refs = ((), refs) if first else (refs[:3], refs[3:])
    if mode == "last":
        (out_ref, kv, q_ref, *state, sems) = refs
    elif mode == "send":
        (*state, part_ref, kv, q_ref, sems) = refs
    else:
        (*state, kv, q_ref, sems) = refs
    m_ref, l_ref, acc_ref = state
    blocks = kv.shape[0] // n_src
    rows = q_own.shape[0]
    copies = [
        pltpu.make_async_copy(kv_refs[s], kv.at[pl.ds(s * blocks, blocks)], sems.at[s]) for s in range(n_src)
    ]
    copies += [pltpu.make_async_copy(a, b, sems.at[n_src + i]) for i, (a, b) in enumerate(zip(state_in, state))]
    copies.append(pltpu.make_async_copy(q_own, q_ref.at[pl.ds(0, rows)], sems.at[n_src + 3]))
    if guests:
        copies.append(pltpu.make_async_copy(guest_ref, q_ref.at[pl.ds(rows, rows)], sems.at[n_src + 4]))
    for copy in copies:
        copy.start()
    if first:
        m_ref[...] = jnp.full(m_ref.shape, NEG, jnp.float32)
        l_ref[...] = jnp.zeros(l_ref.shape, jnp.float32)
        acc_ref[...] = jnp.zeros(acc_ref.shape, jnp.float32)
    for copy in copies:
        copy.wait()
    total = count_ref[entry]
    nn = (((1,), (0,)), ((), ()))
    f32, bf16 = jnp.float32, jnp.bfloat16

    def group_step(g, _):
        found = []
        for u in range(GROUP):
            index = g * GROUP + u
            code0, code1 = live_ref[2 * index], live_ref[2 * index + 1]
            r = code0 >> ROW_SHIFT
            b0 = code0 & ((1 << ROW_SHIFT) - 1)
            b1 = jnp.maximum(code1, 0) & ((1 << ROW_SHIFT) - 1)
            x = lax.dot_general(jnp.concatenate([kv[b0, 0], kv[b1, 0]]), q_ref[r], nn, preferred_element_type=f32)
            x0 = jnp.where(index < total, x[:BLOCK], NEG)
            x1 = jnp.where(code1 >= 0, x[BLOCK:], NEG)
            top = jnp.max(jnp.maximum(x0, x1), axis=0, keepdims=True)
            w0 = jnp.exp2((x0 - top) * EXP2_SCALE)
            w1 = jnp.exp2((x1 - top) * EXP2_SCALE)
            total_w = jnp.sum(w0 + w1, axis=0, keepdims=True)
            w = jnp.concatenate([w0.astype(bf16), w1.astype(bf16)])
            v = jnp.concatenate([kv[b0, 1], kv[b1, 1]], axis=1)
            found.append((r, top, total_w, lax.dot_general(v, w, nn, preferred_element_type=f32)))
        for r, top, total_w, part in found:
            m = m_ref[r]
            m_new = jnp.maximum(m, top)
            alpha = jnp.exp2((m - m_new) * EXP2_SCALE)
            beta = jnp.exp2((top - m_new) * EXP2_SCALE)
            m_ref[r] = m_new
            l_ref[r] = l_ref[r] * alpha + total_w * beta
            acc_ref[r] = acc_ref[r] * alpha + part * beta
        return 0

    lax.fori_loop(0, (total + GROUP - 1) // GROUP, group_step, 0)
    if mode == "last":
        for r in range(rows):
            out_ref[r * BLOCK : (r + 1) * BLOCK, :] = (acc_ref[r] / l_ref[r]).T.astype(out_ref.dtype)
    if mode == "send":
        for r in range(rows):
            l = l_ref[rows + r]
            part_ref[r, :HEAD_DIM] = (acc_ref[rows + r] / jnp.where(l > 0, l, 1.0)).astype(part_ref.dtype)
            words = in_parts(m_ref[rows + r]) + in_parts(l)
            words.append(jnp.zeros((STAT_ROWS - len(words), BLOCK), f32))
            part_ref[r, HEAD_DIM:] = jnp.concatenate(words).astype(part_ref.dtype)


def attend(listed, q, guest, sources, state, mode, sets, name):
    counts, entry, live = listed
    rows, dtype = q.shape[0], q.dtype
    first = state is None
    state = () if first else tuple(state)
    stat = (sets * rows, 1, BLOCK)
    shapes = [stat, stat, (sets * rows, HEAD_DIM, BLOCK)]
    if mode == "last":
        out_shape = [jax.ShapeDtypeStruct((rows * BLOCK, HEAD_DIM), dtype)]
    else:
        out_shape = [jax.ShapeDtypeStruct(shape, jnp.float32) for shape in shapes]
    if mode == "send":
        out_shape.append(jax.ShapeDtypeStruct((rows, HEAD_DIM + STAT_ROWS, BLOCK), dtype))
    n_src = len(sources)
    blocks = sources[0].shape[0]
    guests = () if guest is None else (guest,)
    scratch = [pltpu.VMEM((n_src * blocks,) + sources[0].shape[1:], dtype)]
    scratch += [pltpu.VMEM(((1 + len(guests)) * rows, HEAD_DIM, BLOCK), dtype)]
    if mode == "last":
        scratch += [pltpu.VMEM(shape, jnp.float32) for shape in shapes]
    scratch.append(pltpu.SemaphoreType.DMA((n_src + 5,)))
    return pl.pallas_call(
        functools.partial(attend_kernel, n_src, entry, first, mode, bool(guests)),
        out_shape=out_shape,
        in_specs=[SMEM, SMEM, ANY] + [ANY] * (len(guests) + n_src + len(state)),
        out_specs=[VMEM] * len(out_shape),
        scratch_shapes=scratch,
        compiler_params=params(),
        cost_estimate=pl.CostEstimate(flops=0, bytes_accessed=HEAD_DIM * BLOCK, transcendentals=0),
        name=name,
    )(counts, live, q, *guests, *sources, *state)


def merge_kernel(outer_ref, m_ref, l_ref, acc_ref, part_ref, out_ref):
    outer = outer_ref[0] > 0
    for r in range(part_ref.shape[0]):
        m, l = m_ref[r], l_ref[r]
        words = part_ref[r, HEAD_DIM:].astype(jnp.float32)
        top = jnp.where(outer, words[0:1] + words[1:2] + words[2:3], NEG)
        extra = jnp.where(outer, words[3:4] + words[4:5] + words[5:6], 0.0)
        m_new = jnp.maximum(m, top)
        alpha = jnp.exp2((m - m_new) * EXP2_SCALE)
        beta = jnp.exp2((top - m_new) * EXP2_SCALE) * extra
        done = (acc_ref[r] * alpha + part_ref[r, :HEAD_DIM].astype(jnp.float32) * beta) / (l * alpha + beta)
        out_ref[r * BLOCK : (r + 1) * BLOCK, :] = done.T.astype(out_ref.dtype)


def merge(outer, state, part, name):
    rows = part.shape[0]
    half = lambda x: pl.BlockSpec((rows,) + x.shape[1:], lambda i: (0, 0, 0))
    return pl.pallas_call(
        merge_kernel,
        out_shape=jax.ShapeDtypeStruct((rows * BLOCK, HEAD_DIM), part.dtype),
        grid=(1,),
        in_specs=[SMEM] + [half(x) for x in state] + [VMEM],
        out_specs=VMEM,
        compiler_params=params(),
        name=name,
    )(outer, *state, part)


def place_kernel(n_ka, heads, me_ref, *refs):
    pieces, out_ref, sems = refs[: n_ka * heads], refs[-2], refs[-1]
    copies = []
    for k in range(n_ka):
        for c in range(heads):
            col = pl.multiple_of(((me_ref[0] ^ k) * heads + c) * HEAD_DIM, HEAD_DIM)
            copies.append(
                pltpu.make_async_copy(pieces[c * n_ka + k], out_ref.at[:, pl.ds(col, HEAD_DIM)], sems.at[c, k])
            )
    for copy in copies:
        copy.start()
    for copy in copies:
        copy.wait()


def place(me, pieces, n_ka, heads):
    rows = pieces[0].shape[0]
    return pl.pallas_call(
        functools.partial(place_kernel, n_ka, heads),
        out_shape=jax.ShapeDtypeStruct((rows, HEADS * HEAD_DIM), pieces[0].dtype),
        in_specs=[SMEM] + [ANY] * (n_ka * heads),
        out_specs=ANY,
        scratch_shapes=[pltpu.SemaphoreType.DMA((heads, n_ka))],
        compiler_params=params(),
        name="place",
    )(me, *pieces)


def local(n_pb, n_ka, queries, keys, values, block_mask):
    heads = HEADS // n_ka
    shard = keys.shape[0]
    key_blocks = shard // BLOCK
    rows = queries.shape[0] // BLOCK
    me = lax.axis_index("ka").astype(jnp.int32)
    pb = lax.axis_index("pb").astype(jnp.int32)
    me1, pb1 = me[None], pb[None]
    relay = n_pb >= 4 and n_pb % 2 == 0
    def swap(x, k):
        return lax.ppermute(x, "ka", [(i, i ^ k) for i in range(n_ka)])

    def hops(odd, step):
        found = []
        for low in range(odd, n_pb - 1, 2):
            found += [(low, low + 1)] if low - (step - 1) >= 0 else []
            found += [(low + 1, low)] if low + 1 + (step - 1) < n_pb else []
        if relay and step > 1:
            found = [(i, j) for i, j in found if 0 < j < n_pb - 1]
        return found

    def exchange(x, odd, step):
        found = hops(odd, step)
        return lax.ppermute(x, "pb", found) if found else None

    def inward(x):
        return lax.ppermute(x, "pb", [(0, 1), (n_pb - 1, n_pb - 2)])

    def outward(x):
        return lax.ppermute(x, "pb", [(1, 0), (n_pb - 2, n_pb - 1)])

    def sort(x, before=None):
        mixed = [y if i == 0 else swap(y, 2 * i) for i, y in enumerate(x)]
        theirs = swap(after(jnp.stack([y[1] for y in mixed]), before), 1)
        rows_of = lambda at: jnp.concatenate([jnp.stack([y[0, at] for y in mixed]), theirs[:, at]])
        own = rows_of(slice(0, 2 * shard)).reshape(n_ka * key_blocks, 2, BLOCK, HEAD_DIM)
        return own, rows_of(slice(2 * shard, None)), mixed

    def after(arrays, done):
        return arrays if done is None else lax.optimization_barrier((arrays, done))[0]

    def flags(x):
        return x[:, : block_mask.shape[1], :rows].astype(jnp.int32).reshape(-1)

    steps = [((0, False),)]
    for step in range(1, n_pb):
        found = (((step, False),) if hops(0, step) else ()) + (((-step, True),) if hops(1, step) else ())
        if step == 1:
            steps[0] += found
        elif found:
            steps.append(found)
    last = len(steps) - 1
    parts = (block_mask.T,) + ((inward(block_mask.T),) if relay and heads == 1 else ())
    owns, over, guest = [], [], [None] * heads
    for c in range(heads):
        place_of = after(me1, (q, owns[0])) if c else me1
        packed = pack(place_of, keys, values, parts if c == heads - 1 else (), n_ka, heads, c)
        if c == 0:
            if relay and heads > 1:
                parts += (inward(after(block_mask.T, packed)),)
            q = turn(after(me1, packed), queries, heads)
            own, marks, mixed = sort(packed, (q, parts))
        else:
            own, marks, mixed = sort(after(packed, owns[0]), over[0])
        owns.append(own)
        if c == heads - 1:
            size = mask_rows(block_mask.shape[1])
            masks = [flags(marks[:, i * size :]) for i in range(len(parts))]
            lists = plan(pb1, masks, steps, n_pb, n_ka, key_blocks, rows, relay)
        before = ((over[0], guest[0], lists[0][0] if c == heads - 1 else None), over[0]) if c else (None, None)
        over.append([exchange(after(owns[c], before[odd]), odd, 1) for odd in (0, 1)])
        if relay:
            guest[c] = inward(after(q[c], over[0]))
    state = [None] * heads

    def run(c, step, sources):
        kind = "keep" if step < last else "send" if relay else "last"
        sources = [x for x in sources if x is not None]
        name = f"attend_{c}_{step}"
        return attend(lists[step], q[c], guest[c], sources, state[c], kind, 2 if relay else 1, name)

    for step in range(last):
        for c in range(heads):
            sources = ([owns[c]] if step == 0 else []) + over[c]
            even, odd = over[c]
            if even is not None and odd is not None:
                even, odd = after((even, odd), guest[c] if c else (even, odd))
            over[c] = [exchange(odd, 0, step + 2), exchange(even, 1, step + 2)]
            state[c] = run(c, step, sources)

    pieces = []
    sent = far = None
    for c in range(heads):
        found = run(c, last, ([] if last else [owns[c]]) + after(over[c], sent))
        if relay:
            outer = ((pb == 0) | (pb == n_pb - 1)).astype(jnp.int32)[None]
            out = merge(outer, found[:3], outward(after(found[3], far)), f"merge_{c}")
        else:
            out = found[0]
        mine = [out] + [swap(out, k) for k in range(2, n_ka, 2)]
        sent, far = mine[: n_ka // 4 + 1], mine[n_ka // 4 + 1 :]
        others = [swap(x, 1) for x in mine]
        pieces += [x for two in zip(mine, others) for x in two]
    return place(me1, pieces, n_ka, heads)


def solution(mesh):
    n_pb, n_ka = mesh.shape["pb"], mesh.shape["ka"]
    return jax.shard_map(
        functools.partial(local, n_pb, n_ka),
        mesh=mesh,
        in_specs=(P("pb", None), P(("ka", "pb"), None), P(("ka", "pb"), None), P("pb", "ka")),
        out_specs=P("pb", None),
        check_vma=False,
    )
```

```python
import functools
import math

import jax
import jax.numpy as jnp
from jax import lax
from jax.experimental import pallas as pl
from jax.experimental.pallas import tpu as pltpu
from jax.sharding import PartitionSpec as P

HEADS = 16
HEAD_DIM = 128
BLOCK = 128
NEG = -1e30
EXP2_SCALE = math.log2(math.e) / math.sqrt(HEAD_DIM)
GROUP = 8
STAT_ROWS = 16
ROW_SHIFT = 16
VMEM_BYTES = 40 * 1024 * 1024
MOST_VMEM_BYTES = 60 * 1024 * 1024

VMEM = pl.BlockSpec(memory_space=pltpu.VMEM)
SMEM = pl.BlockSpec(memory_space=pltpu.SMEM)
ANY = pl.BlockSpec(memory_space=pl.ANY)


def params(size=VMEM_BYTES):
    return pltpu.CompilerParams(vmem_limit_bytes=size)


def mask_rows(rows):
    return -(-rows // 16) * 16


def pack_kernel(n_ka, heads, c, n_masks, me_ref, *refs):
    mask_refs, refs = refs[:n_masks], refs[n_masks:]
    k_all, v_all, *out_refs, v_ref, sems = refs
    key_blocks = k_all.shape[0] // BLOCK
    copies = []
    for k in range(n_ka):
        out_ref = out_refs[k // 2]
        col = pl.multiple_of(((me_ref[0] ^ k) * heads + c) * HEAD_DIM, HEAD_DIM)
        for t in range(key_blocks):
            rows, at = pl.ds(t * BLOCK, BLOCK), pl.ds(2 * t * BLOCK, BLOCK)
            sem = sems.at[k * key_blocks + t]
            copies.append(
                (
                    pltpu.make_async_copy(k_all.at[rows, pl.ds(col, HEAD_DIM)], out_ref.at[k % 2, at], sem.at[0]),
                    pltpu.make_async_copy(v_all.at[rows, pl.ds(col, HEAD_DIM)], v_ref.at[k, t], sem.at[1]),
                )
            )
    for pair in copies:
        for copy in pair:
            copy.start()
    for i, mask_ref in enumerate(mask_refs):
        size = mask_rows(mask_ref.shape[0])
        row, column = (lax.broadcasted_iota(jnp.int32, (size, HEAD_DIM), axis) for axis in (0, 1))
        mask = jnp.zeros((size, HEAD_DIM), jnp.int32)
        for a in range(mask_ref.shape[0]):
            for b in range(mask_ref.shape[1]):
                mask = jnp.where((row == a) & (column == b), mask_ref[a, b], mask)
        mask = mask.astype(jnp.float32).astype(k_all.dtype)
        at = 2 * key_blocks * BLOCK + i * size
        for k in range(n_ka):
            out_refs[k // 2][k % 2, at : at + size] = mask
    for k in range(n_ka):
        for t in range(key_blocks):
            copies[k * key_blocks + t][1].wait()
            out_refs[k // 2][k % 2, (2 * t + 1) * BLOCK : (2 * t + 2) * BLOCK] = v_ref[k, t].T
    for pair in copies:
        pair[0].wait()


def pack(me, keys, values, masks, n_ka, heads, c):
    key_blocks = keys.shape[0] // BLOCK
    size = 2 * keys.shape[0] + sum(mask_rows(mask.shape[0]) for mask in masks)
    return pl.pallas_call(
        functools.partial(pack_kernel, n_ka, heads, c, len(masks)),
        out_shape=[jax.ShapeDtypeStruct((2, size, HEAD_DIM), keys.dtype)] * (n_ka // 2),
        in_specs=[SMEM] + [SMEM] * len(masks) + [ANY, ANY],
        out_specs=[VMEM] * (n_ka // 2),
        scratch_shapes=[
            pltpu.VMEM((n_ka, key_blocks, BLOCK, HEAD_DIM), values.dtype),
            pltpu.SemaphoreType.DMA((n_ka * key_blocks, 2)),
        ],
        compiler_params=params(MOST_VMEM_BYTES),
        cost_estimate=pl.CostEstimate(flops=0, bytes_accessed=keys.size, transcendentals=0),
        name=f"pack_{c}",
    )(me, *masks, keys, values)


def turn_kernel(heads, me_ref, q_all, *refs):
    out_refs, (q_ref, sem) = refs[:heads], refs[heads:]
    column = pl.multiple_of(me_ref[0] * heads * HEAD_DIM, HEAD_DIM)
    copy = pltpu.make_async_copy(q_all.at[:, pl.ds(column, heads * HEAD_DIM)], q_ref, sem)
    copy.start()
    copy.wait()
    for c in range(heads):
        for r in range(out_refs[c].shape[0]):
            out_refs[c][r] = q_ref[r * BLOCK : (r + 1) * BLOCK, c * HEAD_DIM : (c + 1) * HEAD_DIM].T


def turn(me, queries, heads):
    tokens = queries.shape[0]
    return pl.pallas_call(
        functools.partial(turn_kernel, heads),
        out_shape=[jax.ShapeDtypeStruct((tokens // BLOCK, HEAD_DIM, BLOCK), queries.dtype)] * heads,
        in_specs=[SMEM, ANY],
        out_specs=[VMEM] * heads,
        scratch_shapes=[pltpu.VMEM((tokens, heads * HEAD_DIM), queries.dtype), pltpu.SemaphoreType.DMA],
        compiler_params=params(MOST_VMEM_BYTES),
        cost_estimate=pl.CostEstimate(flops=0, bytes_accessed=queries.size // HEADS, transcendentals=0),
        name="turn",
    )(me, queries)


def plan_kernel(steps, n_pb, n_slots, key_blocks, rows, relay, pb_ref, *refs):
    mask_refs, count_ref, live_refs = refs[: -len(steps) - 1], refs[-len(steps) - 1], refs[-len(steps) :]
    pb = pb_ref[0]
    sign = 1 - 2 * (pb & 1)
    inner = ((pb > 0) & (pb < n_pb - 1)).astype(jnp.int32)
    helper = ((pb == 1) | (pb == n_pb - 2)).astype(jnp.int32)
    for step, (sources, live) in enumerate(zip(steps, live_refs)):
        total = jnp.int32(0)
        for guest, mask_ref in enumerate(mask_refs):

            def row_step(r, base, guest=guest, mask_ref=mask_ref):
                count = jnp.int32(0)
                for s, (delta, open_to_guests) in enumerate(sources):
                    if guest and not open_to_guests:
                        continue
                    j = pb + delta * sign
                    inside = ((j >= 0) & (j < n_pb)).astype(jnp.int32)
                    if relay and abs(delta) > 1:
                        inside = inside * inner
                    if guest:
                        inside = inside * helper
                    j = jnp.clip(j, 0, n_pb - 1)
                    for slot in range(n_slots):
                        for t in range(key_blocks):
                            block = (s * n_slots + slot) * key_blocks + t
                            live[2 * base + count] = ((r + guest * rows) << ROW_SHIFT) + block
                            column = j * key_blocks + t
                            count += inside * mask_ref[(slot * n_pb * key_blocks + column) * rows + r]
                live[2 * base + count] = -1
                return base + ((count + 1) >> 1)

            total = lax.fori_loop(0, rows, row_step, total)
        for u in range(GROUP):
            live[2 * (total + u)] = 0
            live[2 * (total + u) + 1] = -1
        count_ref[step] = total


def plan(pb, masks, steps, n_pb, n_slots, key_blocks, rows, relay):
    sizes = [len(masks) * rows * ((len(step) * n_slots * key_blocks + 2) // 2) + GROUP for step in steps]
    out_shape = [jax.ShapeDtypeStruct((len(steps),), jnp.int32)]
    out_shape += [jax.ShapeDtypeStruct((2 * size,), jnp.int32) for size in sizes]
    counts, *lives = pl.pallas_call(
        functools.partial(plan_kernel, steps, n_pb, n_slots, key_blocks, rows, relay),
        out_shape=out_shape,
        in_specs=[SMEM] * (1 + len(masks)),
        out_specs=[SMEM] * len(out_shape),
        compiler_params=params(),
        name="plan",
    )(pb, *masks)
    return [(counts, i, live) for i, live in enumerate(lives)]


def in_parts(x):
    found = []
    for _ in range(3):
        found.append(x.astype(jnp.bfloat16).astype(jnp.float32))
        x = x - found[-1]
    return found


def attend_kernel(n_src, entry, first, mode, guests, count_ref, live_ref, q_own, *refs):
    n_kv = n_src
    guest_ref, refs = (refs[0], refs[1:]) if guests else (None, refs)
    kv_refs, refs = refs[:n_kv], refs[n_kv:]
    state_in, refs = ((), refs) if first else (refs[:3], refs[3:])
    if mode == "last":
        (out_ref, kv, q_ref, *state, sems) = refs
    elif mode == "send":
        (*state, part_ref, kv, q_ref, sems) = refs
    else:
        (*state, kv, q_ref, sems) = refs
    m_ref, l_ref, acc_ref = state
    blocks = kv.shape[0] // n_src
    rows = q_own.shape[0]
    copies = [
        pltpu.make_async_copy(kv_refs[s], kv.at[pl.ds(s * blocks, blocks)], sems.at[s]) for s in range(n_src)
    ]
    copies += [pltpu.make_async_copy(a, b, sems.at[n_src + i]) for i, (a, b) in enumerate(zip(state_in, state))]
    copies.append(pltpu.make_async_copy(q_own, q_ref.at[pl.ds(0, rows)], sems.at[n_src + 3]))
    if guests:
        copies.append(pltpu.make_async_copy(guest_ref, q_ref.at[pl.ds(rows, rows)], sems.at[n_src + 4]))
    for copy in copies:
        copy.start()
    if first:
        m_ref[...] = jnp.full(m_ref.shape, NEG, jnp.float32)
        l_ref[...] = jnp.zeros(l_ref.shape, jnp.float32)
        acc_ref[...] = jnp.zeros(acc_ref.shape, jnp.float32)
    for copy in copies:
        copy.wait()
    total = count_ref[entry]
    nn = (((1,), (0,)), ((), ()))
    f32, bf16 = jnp.float32, jnp.bfloat16

    def group_step(g, _):
        found = []
        for u in range(GROUP):
            index = g * GROUP + u
            code0, code1 = live_ref[2 * index], live_ref[2 * index + 1]
            r = code0 >> ROW_SHIFT
            b0 = code0 & ((1 << ROW_SHIFT) - 1)
            b1 = jnp.maximum(code1, 0) & ((1 << ROW_SHIFT) - 1)
            x = lax.dot_general(jnp.concatenate([kv[b0, 0], kv[b1, 0]]), q_ref[r], nn, preferred_element_type=f32)
            x0 = jnp.where(index < total, x[:BLOCK], NEG)
            x1 = jnp.where(code1 >= 0, x[BLOCK:], NEG)
            top = jnp.max(jnp.maximum(x0, x1), axis=0, keepdims=True)
            w0 = jnp.exp2((x0 - top) * EXP2_SCALE)
            w1 = jnp.exp2((x1 - top) * EXP2_SCALE)
            total_w = jnp.sum(w0 + w1, axis=0, keepdims=True)
            w = jnp.concatenate([w0.astype(bf16), w1.astype(bf16)])
            v = jnp.concatenate([kv[b0, 1], kv[b1, 1]], axis=1)
            found.append((r, top, total_w, lax.dot_general(v, w, nn, preferred_element_type=f32)))
        for r, top, total_w, part in found:
            m = m_ref[r]
            m_new = jnp.maximum(m, top)
            alpha = jnp.exp2((m - m_new) * EXP2_SCALE)
            beta = jnp.exp2((top - m_new) * EXP2_SCALE)
            m_ref[r] = m_new
            l_ref[r] = l_ref[r] * alpha + total_w * beta
            acc_ref[r] = acc_ref[r] * alpha + part * beta
        return 0

    lax.fori_loop(0, (total + GROUP - 1) // GROUP, group_step, 0)
    if mode == "last":
        for r in range(rows):
            out_ref[r * BLOCK : (r + 1) * BLOCK, :] = (acc_ref[r] / l_ref[r]).T.astype(out_ref.dtype)
    if mode == "send":
        for r in range(rows):
            l = l_ref[rows + r]
            part_ref[r, :HEAD_DIM] = (acc_ref[rows + r] / jnp.where(l > 0, l, 1.0)).astype(part_ref.dtype)
            words = in_parts(m_ref[rows + r]) + in_parts(l)
            words.append(jnp.zeros((STAT_ROWS - len(words), BLOCK), f32))
            part_ref[r, HEAD_DIM:] = jnp.concatenate(words).astype(part_ref.dtype)


def attend(listed, q, guest, sources, state, mode, sets, name):
    counts, entry, live = listed
    rows, dtype = q.shape[0], q.dtype
    first = state is None
    state = () if first else tuple(state)
    stat = (sets * rows, 1, BLOCK)
    shapes = [stat, stat, (sets * rows, HEAD_DIM, BLOCK)]
    if mode == "last":
        out_shape = [jax.ShapeDtypeStruct((rows * BLOCK, HEAD_DIM), dtype)]
    else:
        out_shape = [jax.ShapeDtypeStruct(shape, jnp.float32) for shape in shapes]
    if mode == "send":
        out_shape.append(jax.ShapeDtypeStruct((rows, HEAD_DIM + STAT_ROWS, BLOCK), dtype))
    n_src = len(sources)
    blocks = sources[0].shape[0]
    guests = () if guest is None else (guest,)
    scratch = [pltpu.VMEM((n_src * blocks,) + sources[0].shape[1:], dtype)]
    scratch += [pltpu.VMEM(((1 + len(guests)) * rows, HEAD_DIM, BLOCK), dtype)]
    if mode == "last":
        scratch += [pltpu.VMEM(shape, jnp.float32) for shape in shapes]
    scratch.append(pltpu.SemaphoreType.DMA((n_src + 5,)))
    return pl.pallas_call(
        functools.partial(attend_kernel, n_src, entry, first, mode, bool(guests)),
        out_shape=out_shape,
        in_specs=[SMEM, SMEM, ANY] + [ANY] * (len(guests) + n_src + len(state)),
        out_specs=[VMEM] * len(out_shape),
        scratch_shapes=scratch,
        compiler_params=params(),
        cost_estimate=pl.CostEstimate(flops=0, bytes_accessed=HEAD_DIM * BLOCK, transcendentals=0),
        name=name,
    )(counts, live, q, *guests, *sources, *state)


def merge_kernel(outer_ref, m_ref, l_ref, acc_ref, part_ref, out_ref):
    outer = outer_ref[0] > 0
    for r in range(part_ref.shape[0]):
        m, l = m_ref[r], l_ref[r]
        words = part_ref[r, HEAD_DIM:].astype(jnp.float32)
        top = jnp.where(outer, words[0:1] + words[1:2] + words[2:3], NEG)
        extra = jnp.where(outer, words[3:4] + words[4:5] + words[5:6], 0.0)
        m_new = jnp.maximum(m, top)
        alpha = jnp.exp2((m - m_new) * EXP2_SCALE)
        beta = jnp.exp2((top - m_new) * EXP2_SCALE) * extra
        done = (acc_ref[r] * alpha + part_ref[r, :HEAD_DIM].astype(jnp.float32) * beta) / (l * alpha + beta)
        out_ref[r * BLOCK : (r + 1) * BLOCK, :] = done.T.astype(out_ref.dtype)


def merge(outer, state, part, name):
    rows = part.shape[0]
    half = lambda x: pl.BlockSpec((rows,) + x.shape[1:], lambda i: (0, 0, 0))
    return pl.pallas_call(
        merge_kernel,
        out_shape=jax.ShapeDtypeStruct((rows * BLOCK, HEAD_DIM), part.dtype),
        grid=(1,),
        in_specs=[SMEM] + [half(x) for x in state] + [VMEM],
        out_specs=VMEM,
        compiler_params=params(),
        name=name,
    )(outer, *state, part)


def place_kernel(n_ka, heads, me_ref, *refs):
    pieces, out_ref, sems = refs[: n_ka * heads], refs[-2], refs[-1]
    copies = []
    for k in range(n_ka):
        for c in range(heads):
            col = pl.multiple_of(((me_ref[0] ^ k) * heads + c) * HEAD_DIM, HEAD_DIM)
            copies.append(
                pltpu.make_async_copy(pieces[c * n_ka + k], out_ref.at[:, pl.ds(col, HEAD_DIM)], sems.at[c, k])
            )
    for copy in copies:
        copy.start()
    for copy in copies:
        copy.wait()


def place(me, pieces, n_ka, heads):
    rows = pieces[0].shape[0]
    return pl.pallas_call(
        functools.partial(place_kernel, n_ka, heads),
        out_shape=jax.ShapeDtypeStruct((rows, HEADS * HEAD_DIM), pieces[0].dtype),
        in_specs=[SMEM] + [ANY] * (n_ka * heads),
        out_specs=ANY,
        scratch_shapes=[pltpu.SemaphoreType.DMA((heads, n_ka))],
        compiler_params=params(),
        name="place",
    )(me, *pieces)


def local(n_pb, n_ka, queries, keys, values, block_mask):
    heads = HEADS // n_ka
    shard = keys.shape[0]
    key_blocks = shard // BLOCK
    rows = queries.shape[0] // BLOCK
    me = lax.axis_index("ka").astype(jnp.int32)
    pb = lax.axis_index("pb").astype(jnp.int32)
    me1, pb1 = me[None], pb[None]
    relay = n_pb >= 4 and n_pb % 2 == 0
    def swap(x, k):
        return lax.ppermute(x, "ka", [(i, i ^ k) for i in range(n_ka)])

    def hops(odd, step):
        found = []
        for low in range(odd, n_pb - 1, 2):
            found += [(low, low + 1)] if low - (step - 1) >= 0 else []
            found += [(low + 1, low)] if low + 1 + (step - 1) < n_pb else []
        if relay and step > 1:
            found = [(i, j) for i, j in found if 0 < j < n_pb - 1]
        return found

    def exchange(x, odd, step):
        found = hops(odd, step)
        return lax.ppermute(x, "pb", found) if found else None

    def inward(x):
        return lax.ppermute(x, "pb", [(0, 1), (n_pb - 1, n_pb - 2)])

    def outward(x):
        return lax.ppermute(x, "pb", [(1, 0), (n_pb - 2, n_pb - 1)])

    def sort(x, before=None):
        mixed = [y if i == 0 else swap(y, 2 * i) for i, y in enumerate(x)]
        theirs = swap(after(jnp.stack([y[1] for y in mixed]), before), 1)
        rows_of = lambda at: jnp.concatenate([jnp.stack([y[0, at] for y in mixed]), theirs[:, at]])
        own = rows_of(slice(0, 2 * shard)).reshape(n_ka * key_blocks, 2, BLOCK, HEAD_DIM)
        return own, rows_of(slice(2 * shard, None)), mixed

    def after(arrays, done):
        return arrays if done is None else lax.optimization_barrier((arrays, done))[0]

    def flags(x):
        return x[:, : block_mask.shape[1], :rows].astype(jnp.int32).reshape(-1)

    steps = [((0, False),)]
    for step in range(1, n_pb):
        found = (((step, False),) if hops(0, step) else ()) + (((-step, True),) if hops(1, step) else ())
        if step == 1:
            steps[0] += found
        elif found:
            steps.append(found)
    last = len(steps) - 1
    parts = (block_mask.T,) + ((inward(block_mask.T),) if relay and heads == 1 else ())
    owns, over, guest = [], [], [None] * heads
    for c in range(heads):
        place_of = after(me1, (q, owns[0])) if c else me1
        packed = pack(place_of, keys, values, parts if c == heads - 1 else (), n_ka, heads, c)
        if c == 0:
            if relay and heads > 1:
                parts += (inward(after(block_mask.T, packed)),)
            q = turn(after(me1, packed), queries, heads)
            own, marks, mixed = sort(packed, (q, parts))
        else:
            own, marks, mixed = sort(after(packed, owns[0]), over[0])
        owns.append(own)
        if c == heads - 1:
            size = mask_rows(block_mask.shape[1])
            masks = [flags(marks[:, i * size :]) for i in range(len(parts))]
            lists = plan(pb1, masks, steps, n_pb, n_ka, key_blocks, rows, relay)
        before = ((over[0], guest[0], lists[0][0] if c == heads - 1 else None), over[0]) if c else (None, None)
        over.append([exchange(after(owns[c], before[odd]), odd, 1) for odd in (0, 1)])
        if relay:
            guest[c] = inward(after(q[c], over[0]))
    state = [None] * heads

    def run(c, step, sources):
        kind = "keep" if step < last else "send" if relay else "last"
        sources = [x for x in sources if x is not None]
        name = f"attend_{c}_{step}"
        return attend(lists[step], q[c], guest[c], sources, state[c], kind, 2 if relay else 1, name)

    for step in range(last):
        for c in range(heads):
            sources = ([owns[c]] if step == 0 else []) + over[c]
            even, odd = over[c]
            if even is not None and odd is not None:
                even, odd = after((even, odd), (even, odd))
            over[c] = [exchange(odd, 0, step + 2), exchange(even, 1, step + 2)]
            state[c] = run(c, step, sources)

    pieces = []
    sent = far = None
    for c in range(heads):
        found = run(c, last, ([] if last else [owns[c]]) + after(over[c], sent))
        if relay:
            outer = ((pb == 0) | (pb == n_pb - 1)).astype(jnp.int32)[None]
            out = merge(outer, found[:3], after(outward(after(found[3], far)), guest[c + 1 :]), f"merge_{c}")
        else:
            out = found[0]
        mine = [out] + [swap(out, k) for k in range(2, n_ka, 2)]
        sent, far = mine[: n_ka // 4 + 1], mine[n_ka // 4 + 1 :]
        others = [swap(x, 1) for x in mine]
        pieces += [x for two in zip(mine, others) for x in two]
    return place(me1, pieces, n_ka, heads)


def solution(mesh):
    n_pb, n_ka = mesh.shape["pb"], mesh.shape["ka"]
    return jax.shard_map(
        functools.partial(local, n_pb, n_ka),
        mesh=mesh,
        in_specs=(P("pb", None), P(("ka", "pb"), None), P(("ka", "pb"), None), P("pb", "ka")),
        out_specs=P("pb", None),
        check_vma=False,
    )
```
